256 devices in a mesh: dom: 64 (over z, y, core), ray: 4 (over x).
Axes of the slice: x: 4, y: 4, z: 8, core: 2. Of those that a mesh axis runs over, the one named last changes fastest.
Arguments:
- projections: bfloat16 [64, 64, 8192], P('dom', None, 'ray'), may hold values from -6 to 6
- phase_kernel: bfloat16 [129], replicated, may hold values from -0.5 to 0.5
- image: bfloat16 [131072, 64], P('dom'), may hold values from -6 to 6
- tile_library: bfloat16 [64, 4, 16, 128, 128], P('dom', 'ray'), may hold values from -0.25 to 0.25
- tile_entry: int32 [64, 4, 256], P('dom', 'ray'), may hold values from 0 to 15
- tile_image: int32 [64, 4, 256], P('dom', 'ray'), may hold values from 0 to 15
- tile_slot: int32 [64, 4, 256], P('dom', 'ray'), may hold values from 0 to 63
- tile_count: int32 [64, 4], P('dom', 'ray'), may hold values from 64 to 256, as said below
- slot_block: int32 [64, 4, 64], P('dom', 'ray'), may hold values from 0 to 15
Outputs:
- residual: bfloat16 [64, 64, 8192], P('dom', None, 'ray')
- image_next: float32 [131072, 64], P(('dom', 'ray'))
The draws below stay inside these ranges and needn't reach their ends.
Inputs may be any that keep to these rules, and one draw needn't show every extreme that they name: `tile_count`: each device has at most 256 live tiles; some device holds exactly 256. Entries beyond a device's count are not used.
All inputs are finite; a program needn't handle non-finite values.
Results may differ from the reference program's by a relative error of at most 0.0075.
Values may be sent and summed in bfloat16 or wider, within the bound.
No kernel may reach another device: no remote copies, remote signals or barrier semaphores. Data moves between devices by JAX's collectives and lax.ppermute only.
A program may use at most 64 MiB of HBM per device.

```python
import jax
import jax.numpy as jnp
from jax import lax

DET = 8192
TILE = 128
HALF = 64
SMOOTH = 8
ANG_DEV = 1
SLICES = 64
IB_DEV = 16
TILE_CAP = 256
LIB = 16
NA = 64
RAY_BLOCKS = 16
PIX = 131072
N_DOM = 64
N_RAY = 4


def draw_projections(key, part):
    background_key, stripe_key = jax.random.split(jax.random.fold_in(key, 11), 2)
    background = jnp.clip(jax.random.normal(background_key, (NA, SLICES, DET), jnp.float32), -4.0, 4.0)
    stripes = jnp.clip(jax.random.normal(stripe_key, (1, SLICES, DET), jnp.float32), -2.0, 2.0)
    return (background + stripes).astype(jnp.bfloat16)


def draw_tile_count(key, part):
    divisor_key, busiest_key = jax.random.split(jax.random.fold_in(key, 7))
    divisor = jax.random.randint(divisor_key, (N_DOM * N_RAY,), 1, 5)
    counts = TILE_CAP // divisor
    busiest = jax.random.randint(busiest_key, (), 0, N_DOM * N_RAY)
    counts = counts.at[busiest].set(TILE_CAP)
    return counts.reshape(N_DOM, N_RAY).astype(jnp.int32)


def with_ends(values, rng, least, top_value):
    extent = values.shape
    spot = [jax.random.randint(jax.random.fold_in(rng, axis), (), 0, extent[axis]) for axis in range(len(extent))]
    values = values.at[tuple(spot)].set(least)
    longest = extent.index(max(extent))
    spot[longest] = (spot[longest] + 1) % extent[longest]
    return values.at[tuple(spot)].set(top_value)


def shard_levels(stream_key, extent, cuts, smallest, top_value):
    loudness, own = 1.0, jax.random.fold_in(stream_key, 6)
    for axis_at, shards_of in cuts:
        draws = jnp.exp(jax.random.uniform(jax.random.fold_in(own, axis_at), (shards_of,), jnp.float32, smallest / len(cuts), top_value / len(cuts)))
        loudness = loudness * jnp.repeat(draws, extent[axis_at] // shards_of).reshape([-1 if axis == axis_at else 1 for axis in range(len(extent))])
    return loudness


def bell_draw(rng, extent, spread, reach, pieces=(), kind=jnp.bfloat16):
    drawn = spread * jax.random.normal(rng, extent, jnp.float32)
    if pieces:
        drawn = drawn * shard_levels(rng, extent, pieces, -0.22, 0.18)
    return jnp.clip(drawn, -reach, reach).astype(kind)


def setup_inputs(seed: int = 0) -> dict:
    key_list = jax.random.split(jax.random.key(seed), 10)
    projections = draw_projections(jax.random.fold_in(key_list[9], 71), 0)
    phase_kernel = bell_draw(key_list[1], (2 * HALF + 1,), (2 * HALF + 1) ** -0.5, 0.5)
    image = bell_draw(key_list[2], (PIX, SLICES), 1.0, 6.0, ((0, 64),))
    tile_library = bell_draw(key_list[3], (N_DOM, N_RAY, LIB, TILE, TILE), (TILE * TILE_CAP // N_DOM) ** -0.5, 0.25, ((0, 64), (1, 4)))
    tile_entry = with_ends(jax.random.randint(key_list[4], (N_DOM, N_RAY, TILE_CAP), 0, LIB), jax.random.fold_in(key_list[4], 1), 0, LIB - 1).astype(jnp.int32)
    tile_image = with_ends(jax.random.randint(key_list[5], (N_DOM, N_RAY, TILE_CAP), 0, IB_DEV), jax.random.fold_in(key_list[5], 1), 0, IB_DEV - 1).astype(jnp.int32)
    tile_slot = with_ends(jax.random.randint(key_list[6], (N_DOM, N_RAY, TILE_CAP), 0, N_DOM), jax.random.fold_in(key_list[6], 1), 0, N_DOM - 1).astype(jnp.int32)
    tile_count = draw_tile_count(jax.random.fold_in(key_list[9], 71), 0)
    slot_block = with_ends(jax.random.randint(key_list[8], (N_DOM, N_RAY, N_DOM), 0, RAY_BLOCKS), jax.random.fold_in(key_list[8], 1), 0, RAY_BLOCKS - 1).astype(jnp.int32)
    return dict(projections=projections, phase_kernel=phase_kernel, image=image, tile_library=tile_library, tile_entry=tile_entry, tile_image=tile_image, tile_slot=tile_slot, tile_count=tile_count, slot_block=slot_block)


relax_factor = 0.25


def toeplitz(kernel, tile_size):
    taps = kernel.shape[0]
    padded = jnp.concatenate([kernel, jnp.zeros((2 * tile_size + 1 - taps,), kernel.dtype)])
    tiled = jnp.tile(padded, tile_size)[: 2 * tile_size * tile_size]
    return tiled.reshape(tile_size, 2 * tile_size).T


def phase_angle(row_block, kernel):
    half_width = (kernel.shape[0] - 1) // 2
    block_count = DET // TILE
    padded = jnp.pad(row_block, ((0, 0), (half_width, 2 * TILE - half_width)))
    blocks = padded.reshape(SLICES, block_count + 2, TILE)
    windows = jnp.concatenate([blocks[:, :block_count], blocks[:, 1:block_count + 1]], axis=-1)
    weights = toeplitz(kernel, TILE).astype(jnp.float32)
    filtered = jnp.einsum("sbi,ij->sbj", windows.astype(jnp.float32), weights)
    return filtered.reshape(SLICES, DET).astype(jnp.bfloat16)


def reference(projections, phase_kernel, image, tile_library, tile_entry, tile_image, tile_slot, tile_count, slot_block):
    phase = lax.map(lambda row_block: phase_angle(row_block, phase_kernel), projections)
    by_slice = jnp.swapaxes(phase, 0, 1)
    profile = lax.map(lambda plane: jnp.median(plane.astype(jnp.float32), axis=0), by_slice)
    padded = jnp.pad(profile, ((0, 0), (SMOOTH, SMOOTH)))
    window_sum = jnp.zeros_like(profile)
    for offset in range(2 * SMOOTH + 1):
        window_sum = window_sum + padded[:, offset:offset + DET]
    position = jnp.arange(DET)
    in_range = (jnp.minimum(position + SMOOTH, DET - 1) - jnp.maximum(position - SMOOTH, 0) + 1).astype(jnp.float32)
    stripe = (profile - window_sum / in_range).astype(jnp.bfloat16)
    corrected = (phase.astype(jnp.float32) - stripe.astype(jnp.float32)[None]).astype(jnp.bfloat16)

    block_count = DET // TILE
    per_owner = DET // (N_RAY * TILE)
    image_blocks = image.reshape(N_DOM, IB_DEV, TILE, SLICES)

    def device_tiles(device_index):
        subdomain = device_index // N_RAY
        quarter = device_index % N_RAY
        library = tile_library[subdomain, quarter]
        entries = tile_entry[subdomain, quarter]
        images = tile_image[subdomain, quarter]
        slots = tile_slot[subdomain, quarter]
        live_mask = jnp.arange(TILE_CAP) < tile_count[subdomain, quarter]
        matrices = library[entries].astype(jnp.float32)
        return subdomain, quarter, matrices, images, slots, live_mask

    def ray_targets(subdomain, quarter):
        carried = slot_block[:, quarter, subdomain]
        angle_index = jnp.arange(N_DOM) * ANG_DEV + carried // per_owner
        column_block = quarter * per_owner + carried % per_owner
        return angle_index, column_block

    def forward_step(device_index, forward):
        subdomain, quarter, matrices, images, slots, live_mask = device_tiles(device_index)
        target = jnp.where(live_mask, slots, N_DOM)
        sources = image_blocks[subdomain][images].astype(jnp.float32)
        product = jnp.einsum("krp,kps->ksr", matrices, sources)
        partial_value = jnp.zeros((N_DOM, SLICES, TILE), jnp.float32).at[target].add(product, mode="drop")
        rounded = lax.optimization_barrier(partial_value.astype(jnp.bfloat16))
        angle_index, column_block = ray_targets(subdomain, quarter)
        return forward.at[angle_index, :, column_block, :].add(rounded.astype(jnp.float32))

    forward = lax.fori_loop(0, N_DOM * N_RAY, forward_step, jnp.zeros((NA, SLICES, block_count, TILE), jnp.float32))
    residual = (corrected.astype(jnp.float32) - forward.reshape(NA, SLICES, DET)).astype(jnp.bfloat16)
    residual_blocks = residual.reshape(NA, SLICES, block_count, TILE)

    def adjoint_step(device_index, gradient):
        subdomain, quarter, matrices, images, slots, live_mask = device_tiles(device_index)
        angle_index, column_block = ray_targets(subdomain, quarter)
        returned = residual_blocks[angle_index, :, column_block, :].astype(jnp.float32)
        image_target = jnp.where(live_mask, images, IB_DEV)
        product = jnp.einsum("krp,ksr->kps", matrices, returned[slots])
        local_sum = jnp.zeros((IB_DEV, TILE, SLICES), jnp.float32).at[image_target].add(product, mode="drop")
        return gradient.at[subdomain].add(local_sum)

    gradient = lax.fori_loop(0, N_DOM * N_RAY, adjoint_step, jnp.zeros((N_DOM, IB_DEV, TILE, SLICES), jnp.float32))
    image_next = image.astype(jnp.float32) + relax_factor * gradient.reshape(PIX, SLICES)
    return residual, image_next
```

```python
import jax
import jax.numpy as jnp
from jax import lax
from jax.experimental import pallas as pl
from jax.experimental.pallas import tpu as pltpu
from jax.sharding import PartitionSpec as P

T = 128
SMOOTH = 8
RELAX = 0.25
CHUNKS = 1
SECTION = 32
LIMIT = 48 * 2**20
F32, BF16 = jnp.float32, jnp.bfloat16
NT = (((1,), (1,)), ((), ()))
VMEM = pl.BlockSpec(memory_space=pltpu.VMEM)
SMEM = pl.BlockSpec(memory_space=pltpu.SMEM)
ANY = pl.BlockSpec(memory_space=pl.ANY)


def params(**more):
    return pltpu.CompilerParams(vmem_limit_bytes=LIMIT, **more)


def middle_network(n):
    pairs = []
    p = 1
    while p < n:
        k = p
        while k >= 1:
            for j in range(k % p, n - k, 2 * k):
                for i in range(min(k, n - j - k)):
                    if (i + j) // (2 * p) == (i + j + k) // (2 * p):
                        pairs.append((i + j, i + j + k))
            k //= 2
        p *= 2
    needed = {n // 2 - 1, n // 2}
    kept = []
    for a, b in reversed(pairs):
        if a in needed or b in needed:
            kept.append((a, b, a in needed, b in needed))
            needed |= {a, b}
    return kept[::-1]


def band(kernel):
    taps = kernel.shape[0]
    padded = jnp.concatenate([kernel, jnp.zeros((2 * T + 1 - taps,), kernel.dtype)])
    tiled = jnp.tile(padded, T)[: 2 * T * T].reshape(T, 2 * T)
    return jnp.pad(tiled, ((0, 0), (T // 2, T // 2)))


def lanes(block):
    return pl.ds(pl.multiple_of(block * T, T), T)


def forward_call(lists, image, library, first, size, rows, blocks, owners):
    entries = library.shape[0]
    capacity = lists.shape[1]

    def kernel(lists_ref, image_ref, library_ref, send_ref, turned, product, total, packed, sem):
        for i in range(blocks):
            block = image_ref[i * T : (i + 1) * T, :].astype(F32)
            turned[i * size : (i + 1) * size, :] = block.T[first : first + size, :].astype(BF16)
        for e in range(entries):
            product[:, e * T : (e + 1) * T] = lax.dot_general(
                turned[...], library_ref[e], NT, preferred_element_type=F32
            )
        total[...] = jnp.zeros_like(total)

        def add(k):
            e, i, s = lists_ref[0, k], lists_ref[1, k], lists_ref[2, k]
            total[s] += product[pl.ds(pl.multiple_of(i * size, size), size), lanes(e)]

        def group(g, carry):
            for u in range(8):
                add(g * 8 + u)
            return carry

        lax.fori_loop(0, lists_ref[3, 0], group, 0)
        packed[...] = total[:owners].astype(BF16)
        copy = pltpu.make_async_copy(packed, send_ref.at[:, pl.ds(0, size), :], sem)
        copy.start()
        copy.wait()

    return pl.pallas_call(
        kernel,
        out_shape=jax.ShapeDtypeStruct((owners, rows, T), BF16),
        in_specs=[SMEM, VMEM, VMEM],
        out_specs=ANY,
        scratch_shapes=[
            pltpu.VMEM((blocks * size, T), BF16),
            pltpu.VMEM((blocks * size, entries * T), F32),
            pltpu.VMEM((owners + 1, size, T), F32),
            pltpu.VMEM((owners, size, T), BF16),
            pltpu.SemaphoreType.DMA,
        ],
        compiler_params=params(),
        cost_estimate=pl.CostEstimate(
            flops=2 * capacity * size * T * T, bytes_accessed=8 * 2**20, transcendentals=0
        ),
        name="forward_tiles",
    )(lists, image, library)


def phase_call(projections, left, right, taps, numbers, send, offset):
    slices, columns = projections.shape
    per = columns // T

    def kernel(x_ref, l_ref, r_ref, taps_ref, n_ref, _, phase_ref, send_ref, wide, spread, packed, sem):
        wide[:, :T] = l_ref[...]
        wide[:, T : T + columns] = x_ref[...]
        wide[:, T + columns :] = r_ref[...]
        spread[...] = jnp.zeros_like(spread)

        def put(row, value):
            spread[pl.ds(row, slices, stride=SECTION), :] = value

        def product(start, stop, low):
            return lax.dot_general(
                wide[:, start * T : stop * T],
                taps_ref[:, low * T : (low + stop - start) * T],
                NT,
                preferred_element_type=F32,
            ).astype(BF16)

        for b in range(per):
            value = product(b, b + 3, 0)
            phase_ref[:, b * T : (b + 1) * T] = value
            put(b, value.astype(F32))
        put(per, product(0, 2, 1).astype(F32))
        put(per + 1, product(per, per + 2, 0).astype(F32))
        put(per + 2, n_ref[...])
        packed[...] = spread[...].astype(BF16).reshape(slices, SECTION, T)
        copy = pltpu.make_async_copy(packed, send_ref.at[:, pl.ds(offset, SECTION), :], sem)
        copy.start()
        copy.wait()

    return pl.pallas_call(
        kernel,
        out_shape=[
            jax.ShapeDtypeStruct((slices, columns), BF16),
            jax.ShapeDtypeStruct(send.shape, BF16),
        ],
        in_specs=[VMEM, VMEM, VMEM, VMEM, VMEM, ANY],
        out_specs=[VMEM, ANY],
        scratch_shapes=[
            pltpu.VMEM((slices, columns + 2 * T), BF16),
            pltpu.VMEM((slices * SECTION, T), F32),
            pltpu.VMEM((slices, SECTION, T), BF16),
            pltpu.SemaphoreType.DMA,
        ],
        input_output_aliases={5: 1},
        compiler_params=params(),
        cost_estimate=pl.CostEstimate(flops=2**26, bytes_accessed=2**20, transcendentals=0),
        name="phase_filter",
    )(projections, left, right, taps, numbers, send)


def stripe_of(quarter, quarters, arrived_ref, offset, values, rimmed):
    angles = arrived_ref.shape[0]
    for a in range(angles):
        values[a] = arrived_ref[a, offset : offset + SECTION, :].astype(F32)[:24]
    network = middle_network(angles)

    def middle(g, carry):
        rows = pl.ds(pl.multiple_of(g * 8, 8), 8)
        v = [values[a, rows, :] for a in range(angles)]
        for a, b, low, high in network:
            x, y = v[a], v[b]
            if low:
                v[a] = jnp.minimum(x, y)
            if high:
                v[b] = jnp.maximum(x, y)
        rimmed[pl.ds(g * 8 + 1, 8), :] = (v[angles // 2 - 1] + v[angles // 2]) * 0.5
        return carry

    lax.fori_loop(0, 3, middle, 0)
    before, after = rimmed[17:18, :], rimmed[18:19, :]
    rimmed[0:1, :] = jnp.where(quarter == 0, jnp.zeros_like(before), before)
    rimmed[17:18, :] = jnp.where(quarter == quarters - 1, jnp.zeros_like(after), after)
    prev, cur, nxt = rimmed[0:16, :], rimmed[1:17, :], rimmed[2:18, :]
    lane = lax.broadcasted_iota(jnp.int32, (16, T), 1)
    total = cur
    for o in range(1, SMOOTH + 1):
        total += pltpu.roll(jnp.where(lane < o, nxt, cur), T - o, 1)
        total += pltpu.roll(jnp.where(lane >= T - o, prev, cur), o, 1)
    place = quarter * (16 * T) + lax.broadcasted_iota(jnp.int32, (16, T), 0) * T + lane
    last = quarters * 16 * T - 1
    count = jnp.minimum(place + SMOOTH, last) - jnp.maximum(place - SMOOTH, 0) + 1
    return cur - total / count.astype(F32)


def residual_call(carried, quarter, arrived, phase, first, size, rows, section, quarters):
    owners = arrived.shape[0]
    columns = phase.shape[1]

    def kernel(c_ref, q_ref, arrived_ref, phase_ref, forward_ref, back_ref, values, rimmed, less):
        forward_ref[...] = jnp.zeros_like(forward_ref)
        for d in range(owners):
            forward_ref[:, lanes(c_ref[0, d])] += arrived_ref[d, :size, :].astype(F32)
        less[...] = (phase_ref[first : first + size, :].astype(F32) - forward_ref[...]).astype(BF16)
        for d in range(owners):
            back_ref[d, :size, :] = less[:, lanes(c_ref[0, d])]
        if section:
            stripe = stripe_of(q_ref[0], quarters, arrived_ref, size, values, rimmed).astype(BF16)
            for d in range(owners):
                back_ref[d, size:, :] = stripe

    return pl.pallas_call(
        kernel,
        out_shape=[
            jax.ShapeDtypeStruct((size, columns), F32),
            jax.ShapeDtypeStruct((owners, rows, T), BF16),
        ],
        in_specs=[SMEM, SMEM, VMEM, VMEM],
        out_specs=[VMEM, VMEM],
        scratch_shapes=[
            pltpu.VMEM((owners, 24, T), F32),
            pltpu.VMEM((32, T), F32),
            pltpu.VMEM((size, columns), BF16),
        ],
        compiler_params=params(),
        cost_estimate=pl.CostEstimate(flops=2**24, bytes_accessed=8 * 2**20, transcendentals=0),
        name="slot_residual",
    )(carried, quarter, arrived, phase)


def adjoint_call(lists, carried, returned, striped, offset, library, first, size, blocks, own):
    entries = library.shape[0]
    owners = returned.shape[0]
    per = 16
    same = striped is returned

    def kernel(*refs):
        refs = list(refs)
        lists_ref, c_ref, returned_ref = refs[:3]
        refs = refs[3:]
        striped_ref = returned_ref if same else refs.pop(0)
        library_ref = refs.pop(0)
        if own:
            phase_ref = refs.pop(0)
            forward_refs = [refs.pop(0) for _ in own[1]]
        update_ref = refs.pop(0)
        if own:
            residual_ref = refs.pop(0)
        stripes, terms, bins = refs
        stripes[...] = striped_ref[:, offset : offset + per, :].astype(F32).reshape(owners * per, T)
        for e in range(owners):
            stripe = stripes[pl.ds(first * per + c_ref[e], size, stride=per), :]
            terms[e] = returned_ref[e, :size, :].astype(F32) - stripe
        bins[...] = jnp.zeros_like(bins)

        def add(k):
            e, i, s = lists_ref[0, k], lists_ref[1, k], lists_ref[2, k]
            bins[pl.ds(pl.multiple_of(i * size, size), size), lanes(e)] += terms[s]

        def group(g, carry):
            for u in range(8):
                add(g * 8 + u)
            return carry

        terms[owners] = jnp.zeros((size, T), F32)
        lax.fori_loop(0, lists_ref[3, 0], group, 0)
        update_ref[...] = (
            jnp.dot(
                bins[...].astype(BF16),
                library_ref[...].reshape(entries * T, T),
                preferred_element_type=F32,
            )
            .astype(BF16)
            .reshape(blocks, size, T)
        )
        if own:
            for n, forward_ref in enumerate(forward_refs):
                depth = forward_ref.shape[0]
                for b in range(per):
                    where = slice(b * T, (b + 1) * T)
                    stripe = stripes[pl.ds(n * depth * per + b, depth, stride=per), :]
                    value = phase_ref[n * depth : (n + 1) * depth, where].astype(F32) - stripe
                    value = value.astype(BF16).astype(F32) - forward_ref[:, where]
                    residual_ref[n * depth : (n + 1) * depth, where] = value.astype(BF16)

    args = [lists, carried, returned] + ([] if same else [striped]) + [library]
    out_shape = [jax.ShapeDtypeStruct((blocks, size, T), BF16)]
    if own:
        args += [own[0], *own[1]]
        out_shape.append(jax.ShapeDtypeStruct(own[0].shape, BF16))
    return pl.pallas_call(
        kernel,
        out_shape=out_shape,
        in_specs=[SMEM, SMEM] + [VMEM] * (len(args) - 2),
        out_specs=[VMEM] * len(out_shape),
        scratch_shapes=[
            pltpu.VMEM((owners * per, T), F32),
            pltpu.VMEM((owners + 1, size, T), F32),
            pltpu.VMEM((blocks * size, entries * T), F32),
        ],
        compiler_params=params(),
        cost_estimate=pl.CostEstimate(
            flops=2 * 256 * size * T * T, bytes_accessed=8 * 2**20, transcendentals=0
        ),
        name="adjoint_tiles",
    )(*args)


def image_call(quarter, image, parts, quarters):
    pixels, slices = image.shape
    held = pixels // quarters
    mine = held // T

    def kernel(q_ref, image_ref, *refs):
        parts_refs, out_ref = refs[:-1], refs[-1]
        start = q_ref[0] * held
        for i in range(mine):
            pieces = []
            for ref in parts_refs:
                total = ref[i].astype(F32)
                for q in range(1, quarters):
                    total += ref[q * mine + i].astype(F32)
                pieces.append(total)
            update = jnp.concatenate(pieces, axis=0) if len(pieces) > 1 else pieces[0]
            rows = pl.ds(pl.multiple_of(start + i * T, T), T)
            out_ref[i * T : (i + 1) * T, :] = image_ref[rows, :].astype(F32) + RELAX * update.T

    return pl.pallas_call(
        kernel,
        out_shape=jax.ShapeDtypeStruct((held, slices), F32),
        in_specs=[SMEM, VMEM] + [VMEM] * len(parts),
        out_specs=VMEM,
        compiler_params=params(),
        cost_estimate=pl.CostEstimate(flops=2**18, bytes_accessed=2**20, transcendentals=0),
        name="image_step",
    )(quarter, image, *parts)


def exchanged(array, axis):
    return lax.all_to_all(array, axis, split_axis=0, concat_axis=0, tiled=True)


def shards(projections, phase_kernel, image, tile_library, tile_entry, tile_image, tile_slot, tile_count, slot_block):
    projections = projections[0]
    library = tile_library[0, 0]
    slices = projections.shape[0]
    owners, quarters = lax.axis_size("dom"), lax.axis_size("ray")
    blocks = image.shape[0] // T
    quarter = lax.axis_index("ray").astype(jnp.int32).reshape(1)
    capacity = tile_entry.shape[-1]
    count = tile_count[0, 0]
    live = jnp.arange(capacity) < count
    lists = jnp.stack(
        [
            jnp.where(live, tile_entry[0, 0], 0),
            jnp.where(live, tile_image[0, 0], 0),
            jnp.where(live, tile_slot[0, 0], owners),
            jnp.full((capacity,), (count + 7) // 8, jnp.int32),
        ]
    )
    carried = slot_block[0]
    size = slices // CHUNKS

    left = lax.ppermute(projections[:, -T:], "ray", [(i, i + 1) for i in range(quarters - 1)])
    right = lax.ppermute(projections[:, :T], "ray", [(i + 1, i) for i in range(quarters - 1)])
    taps = band(phase_kernel)
    numbers = jnp.broadcast_to(carried[0].astype(F32)[:, None], (owners, T))

    arrived, forwards, returned, updates = [], [], [], []
    for n in range(CHUNKS):
        rows = size + (SECTION if n == 0 else 0)
        send = forward_call(lists, image, library, n * size, size, rows, blocks, owners)
        if n == 0:
            phase, send = phase_call(projections, left, right, taps, numbers, send, size)
        arrived.append(exchanged(send, "dom"))
    theirs = arrived[0][:, size + 18, 0].astype(jnp.int32)
    for n in range(CHUNKS):
        rows = size + (16 if n == 0 else 0)
        forward, back = residual_call(
            carried, quarter, arrived[n], phase, n * size, size, rows, n == 0, quarters
        )
        forwards.append(forward)
        returned.append(exchanged(back, "dom"))
    for n in range(CHUNKS):
        own = (phase, forwards) if n == 0 else None
        made = adjoint_call(
            lists, theirs, returned[n], returned[0], size, library, n * size, size, blocks, own
        )
        if own:
            residual = made[1]
        updates.append(exchanged(made[0], "ray"))
    image_next = image_call(quarter, image, updates, quarters)
    return residual[None], image_next


def solution(mesh):
    return jax.shard_map(
        shards,
        mesh=mesh,
        in_specs=(
            P("dom", None, "ray"),
            P(),
            P("dom", None),
            P("dom", "ray", None, None, None),
            P("dom", "ray", None),
            P("dom", "ray", None),
            P("dom", "ray", None),
            P("dom", "ray"),
            P("dom", "ray", None),
        ),
        out_specs=(P("dom", None, "ray"), P(("dom", "ray"), None)),
        check_vma=False,
    )
```

```python
import jax
import jax.numpy as jnp
from jax import lax
from jax.experimental import pallas as pl
from jax.experimental.pallas import tpu as pltpu
from jax.sharding import PartitionSpec as P

T = 128
SMOOTH = 8
RELAX = 0.25
SECTION = 32
MIB = 2**20
F32, BF16 = jnp.float32, jnp.bfloat16
NT = (((1,), (1,)), ((), ()))
VMEM = pl.BlockSpec(memory_space=pltpu.VMEM)
SMEM = pl.BlockSpec(memory_space=pltpu.SMEM)
HBM = pl.BlockSpec(memory_space=pltpu.HBM)


def params(limit=63):
    return pltpu.CompilerParams(vmem_limit_bytes=limit * MIB)


def middle_network(n):
    pairs = []
    p = 1
    while p < n:
        k = p
        while k >= 1:
            for j in range(k % p, n - k, 2 * k):
                for i in range(min(k, n - j - k)):
                    if (i + j) // (2 * p) == (i + j + k) // (2 * p):
                        pairs.append((i + j, i + j + k))
            k //= 2
        p *= 2
    needed = {n // 2 - 1, n // 2}
    kept = []
    for a, b in reversed(pairs):
        if a in needed or b in needed:
            kept.append((a, b, a in needed, b in needed))
            needed |= {a, b}
    return kept[::-1]


def band(kernel):
    taps = kernel.shape[0]
    padded = jnp.concatenate([kernel, jnp.zeros((2 * T + 1 - taps,), kernel.dtype)])
    tiled = jnp.tile(padded, T)[: 2 * T * T].reshape(T, 2 * T)
    return jnp.pad(tiled, ((0, 0), (T // 2, T // 2)))


def lanes(block):
    return pl.ds(pl.multiple_of(block * T, T), T)


def first_call(entry, place, slot, count, numbers, projections, left, right, taps, image, library):
    slices, columns = projections.shape
    entries, capacity = library.shape[0], entry.shape[1]
    blocks = image.shape[1] // T
    owners = slices
    per = columns // T
    rows = slices + SECTION
    parts = 4

    def kernel(
        entry_hbm, place_hbm, slot_hbm, count_ref, n_hbm, x_hbm, l_ref, r_ref, taps_ref, image_hbm, library_hbm,
        phase_ref, send_ref, entry_ref, place_ref, slot_ref, n_ref, library_ref, wide, spread, row, stacked,
        product, total, packed, sems, loads,
    ):
        pairs = [(x_hbm, wide.at[:, pl.ds(T, columns)]), (n_hbm, n_ref), (library_hbm, library_ref)]
        pairs += [
            (image_hbm.at[:, pl.ds(i * T, T)], stacked.at[pl.ds(i * slices, slices)]) for i in range(blocks)
        ]
        pairs += [(entry_hbm, entry_ref), (place_hbm, place_ref), (slot_hbm, slot_ref)]
        fetches = [pltpu.make_async_copy(a, b, loads.at[n]) for n, (a, b) in enumerate(pairs)]
        for fetch in fetches:
            fetch.start()
        wide[:, :T] = l_ref[...]
        wide[:, T + columns :] = r_ref[...]
        spread[...] = jnp.zeros_like(spread)

        def put(at, value):
            spread[pl.ds(at, slices, stride=SECTION), :] = value

        def filtered(start, stop, low):
            return lax.dot_general(
                wide[:, start * T : stop * T],
                taps_ref[:, low * T : (low + stop - start) * T],
                NT,
                preferred_element_type=F32,
            ).astype(BF16)

        fetches[0].wait()
        for b in range(per):
            value = filtered(b, b + 3, 0)
            phase_ref[:, b * T : (b + 1) * T] = value
            put(b, value.astype(F32))
        put(per, filtered(0, 2, 1).astype(F32))
        put(per + 1, filtered(per, per + 2, 0).astype(F32))
        row[...] = jnp.zeros_like(row)
        fetches[1].wait()
        row[0:1, :owners] = n_ref[...].astype(F32)
        put(per + 2, jnp.broadcast_to(row[0:1, :], (slices, T)))
        packed[:, slices:, :] = spread[...].astype(BF16).reshape(slices, SECTION, T)

        total[...] = jnp.zeros_like(total)
        for fetch in fetches[2:]:
            fetch.wait()
        for e in range(0, entries, 2):
            product[:, e * T : (e + 2) * T] = lax.dot_general(
                stacked[...], library_ref[e : e + 2].reshape(2 * T, T), NT, preferred_element_type=F32
            )

        def add(k):
            live = k < count_ref[0, 0]
            e = jnp.where(live, entry_ref[0, k], 0)
            i = jnp.where(live, place_ref[0, k], 0)
            s = jnp.where(live, slot_ref[0, k], owners)
            total[s] += product[pl.ds(pl.multiple_of(i * slices, slices), slices), lanes(e)]

        def group(g, carry):
            for u in range(8):
                add(g * 8 + u)
            return carry

        lax.fori_loop(0, (count_ref[0, 0] + 7) // 8, group, 0)
        step = owners // parts
        copies = []
        for n in range(parts):
            packed[n * step : (n + 1) * step, :slices, :] = total[n * step : (n + 1) * step].astype(BF16)
            here = pl.ds(n * step, step)
            copies.append(pltpu.make_async_copy(packed.at[here], send_ref.at[here], sems.at[n]))
            copies[-1].start()
        for copy in copies:
            copy.wait()

    return pl.pallas_call(
        kernel,
        out_shape=[
            jax.ShapeDtypeStruct((slices, columns), BF16),
            jax.ShapeDtypeStruct((owners, rows, T), BF16),
        ],
        in_specs=[HBM] * 3 + [SMEM, HBM, HBM] + [VMEM] * 3 + [HBM, HBM],
        out_specs=[VMEM, HBM],
        scratch_shapes=[
            pltpu.SMEM(entry.shape, jnp.int32),
            pltpu.SMEM(place.shape, jnp.int32),
            pltpu.SMEM(slot.shape, jnp.int32),
            pltpu.VMEM(numbers.shape, jnp.int32),
            pltpu.VMEM(library.shape, BF16),
            pltpu.VMEM((slices, columns + 2 * T), BF16),
            pltpu.VMEM((slices * SECTION, T), F32),
            pltpu.VMEM((8, T), F32),
            pltpu.VMEM((blocks * slices, T), BF16),
            pltpu.VMEM((blocks * slices, entries * T), F32),
            pltpu.VMEM((owners + 1, slices, T), F32),
            pltpu.VMEM((owners, rows, T), BF16),
            pltpu.SemaphoreType.DMA((parts,)),
            pltpu.SemaphoreType.DMA((blocks + 6,)),
        ],
        compiler_params=params(),
        cost_estimate=pl.CostEstimate(
            flops=2 * capacity * slices * T * T, bytes_accessed=8 * 2**20, transcendentals=0
        ),
        name="filter_and_forward",
    )(entry, place, slot, count, numbers, projections, left, right, taps, image, library)


def stripe_of(quarter, quarters, arrived_ref, offset, values, rimmed):
    angles = arrived_ref.shape[0]
    for a in range(angles):
        values[a] = arrived_ref[a, offset : offset + SECTION, :].astype(F32)[:24]
    network = middle_network(angles)

    def middle(g, carry):
        rows = pl.ds(pl.multiple_of(g * 8, 8), 8)
        v = [values[a, rows, :] for a in range(angles)]
        for a, b, low, high in network:
            x, y = v[a], v[b]
            if low:
                v[a] = jnp.minimum(x, y)
            if high:
                v[b] = jnp.maximum(x, y)
        rimmed[pl.ds(g * 8 + 1, 8), :] = (v[angles // 2 - 1] + v[angles // 2]) * 0.5
        return carry

    lax.fori_loop(0, 3, middle, 0)
    before, after = rimmed[17:18, :], rimmed[18:19, :]
    rimmed[0:1, :] = jnp.where(quarter == 0, jnp.zeros_like(before), before)
    rimmed[17:18, :] = jnp.where(quarter == quarters - 1, jnp.zeros_like(after), after)
    prev, cur, nxt = rimmed[0:16, :], rimmed[1:17, :], rimmed[2:18, :]
    lane = lax.broadcasted_iota(jnp.int32, (16, T), 1)
    total = cur
    for o in range(1, SMOOTH + 1):
        total += pltpu.roll(jnp.where(lane < o, nxt, cur), T - o, 1)
        total += pltpu.roll(jnp.where(lane >= T - o, prev, cur), o, 1)
    place = quarter * (16 * T) + lax.broadcasted_iota(jnp.int32, (16, T), 0) * T + lane
    last = quarters * 16 * T - 1
    count = jnp.minimum(place + SMOOTH, last) - jnp.maximum(place - SMOOTH, 0) + 1
    return cur - total / count.astype(F32)


def back_call(carried, quarter, arrived, phase, quarters):
    owners = arrived.shape[0]
    size, columns = phase.shape
    rows = size + 16
    parts = 4

    def kernel(c_ref, q_ref, arrived_ref, phase_ref, forward_ref, send_ref, values, rimmed, less, packed, sems):
        stripe = stripe_of(q_ref[0], quarters, arrived_ref, size, values, rimmed).astype(BF16)
        forward_ref[...] = jnp.zeros_like(forward_ref)
        for d in range(owners):
            forward_ref[:, lanes(c_ref[0, d])] += arrived_ref[d, :size, :].astype(F32)
        less[...] = (phase_ref[...].astype(F32) - forward_ref[...]).astype(BF16)
        step = owners // parts
        copies = []
        for n in range(parts):
            for d in range(n * step, (n + 1) * step):
                packed[d, :size, :] = less[:, lanes(c_ref[0, d])]
                packed[d, size:, :] = stripe
            here = pl.ds(n * step, step)
            copies.append(pltpu.make_async_copy(packed.at[here], send_ref.at[here], sems.at[n]))
            copies[-1].start()
        for copy in copies:
            copy.wait()

    return pl.pallas_call(
        kernel,
        out_shape=[
            jax.ShapeDtypeStruct((size, columns), F32),
            jax.ShapeDtypeStruct((owners, rows, T), BF16),
        ],
        in_specs=[SMEM, SMEM, VMEM, VMEM],
        out_specs=[VMEM, HBM],
        scratch_shapes=[
            pltpu.VMEM((owners, 24, T), F32),
            pltpu.VMEM((32, T), F32),
            pltpu.VMEM((size, columns), BF16),
            pltpu.VMEM((owners, rows, T), BF16),
            pltpu.SemaphoreType.DMA((parts,)),
        ],
        compiler_params=params(),
        cost_estimate=pl.CostEstimate(flops=2**24, bytes_accessed=8 * 2**20, transcendentals=0),
        name="sum_and_stripe",
    )(carried, quarter, arrived, phase)


def adjoint_call(entry, place, slot, count, theirs, returned, library, blocks):
    entries = library.shape[0]
    owners = returned.shape[0]
    per = 16
    size = returned.shape[1] - per

    def kernel(
        entry_hbm, place_hbm, slot_hbm, count_ref, c_ref, returned_ref, library_hbm,
        update_ref, stripe_ref, entry_ref, place_ref, slot_ref, library_ref, stripes, terms, bins, loads,
    ):
        pairs = [(entry_hbm, entry_ref), (place_hbm, place_ref), (slot_hbm, slot_ref), (library_hbm, library_ref)]
        fetches = [pltpu.make_async_copy(a, b, loads.at[n]) for n, (a, b) in enumerate(pairs)]
        for fetch in fetches:
            fetch.start()
        stripes[...] = returned_ref[:, size:, :].astype(F32).reshape(owners * per, T)
        for b in range(per):
            stripe_ref[b] = stripes[pl.ds(b, size, stride=per), :]
        for e in range(owners):
            terms[e] = returned_ref[e, :size, :].astype(F32) - stripe_ref[c_ref[e]]
        terms[owners] = jnp.zeros((size, T), F32)
        bins[...] = jnp.zeros_like(bins)
        for fetch in fetches:
            fetch.wait()

        def add(k):
            live = k < count_ref[0, 0]
            e = jnp.where(live, entry_ref[0, k], 0)
            i = jnp.where(live, place_ref[0, k], 0)
            s = jnp.where(live, slot_ref[0, k], owners)
            bins[pl.ds(pl.multiple_of(i * size, size), size), lanes(e)] += terms[s]

        def group(g, carry):
            for u in range(8):
                add(g * 8 + u)
            return carry

        lax.fori_loop(0, (count_ref[0, 0] + 7) // 8, group, 0)
        half = blocks // 2
        for h in range(2):
            update_ref[h * half : (h + 1) * half] = (
                jnp.dot(
                    bins[h * half * size : (h + 1) * half * size, :].astype(BF16),
                    library_ref[...].reshape(entries * T, T),
                    preferred_element_type=F32,
                )
                .astype(BF16)
                .reshape(half, size, T)
            )

    return pl.pallas_call(
        kernel,
        out_shape=[
            jax.ShapeDtypeStruct((blocks, size, T), BF16),
            jax.ShapeDtypeStruct((per, size, T), F32),
        ],
        in_specs=[HBM] * 3 + [SMEM, SMEM, VMEM, HBM],
        out_specs=[VMEM, VMEM],
        scratch_shapes=[
            pltpu.SMEM(entry.shape, jnp.int32),
            pltpu.SMEM(place.shape, jnp.int32),
            pltpu.SMEM(slot.shape, jnp.int32),
            pltpu.VMEM(library.shape, BF16),
            pltpu.VMEM((owners * per, T), F32),
            pltpu.VMEM((owners + 1, size, T), F32),
            pltpu.VMEM((blocks * size, entries * T), F32),
            pltpu.SemaphoreType.DMA((4,)),
        ],
        compiler_params=params(),
        cost_estimate=pl.CostEstimate(
            flops=2 * 256 * size * T * T, bytes_accessed=8 * 2**20, transcendentals=0
        ),
        name="adjoint_tiles",
    )(entry, place, slot, count, theirs, returned, library)


def residual_call(phase, stripe, forward):
    per = stripe.shape[0]

    def kernel(phase_ref, stripe_ref, forward_ref, residual_ref):
        for b in range(per):
            where = slice(b * T, (b + 1) * T)
            corrected = (phase_ref[:, where].astype(F32) - stripe_ref[b]).astype(BF16)
            residual_ref[:, where] = (corrected.astype(F32) - forward_ref[:, where]).astype(BF16)

    return pl.pallas_call(
        kernel,
        out_shape=jax.ShapeDtypeStruct(phase.shape, BF16),
        in_specs=[VMEM] * 3,
        out_specs=VMEM,
        compiler_params=params(12),
        cost_estimate=pl.CostEstimate(flops=2**19, bytes_accessed=2**21, transcendentals=0),
        name="residual",
    )(phase, stripe, forward)


def image_call(quarter, image, parts, quarters):
    slices, pixels = image.shape
    held = pixels // quarters
    mine = held // T

    def kernel(q_ref, image_ref, parts_ref, out_ref):
        for i in range(mine):
            total = parts_ref[i].astype(F32)
            for q in range(1, quarters):
                total += parts_ref[q * mine + i].astype(F32)
            own = image_ref[:, lanes(q_ref[0] * mine + i)].astype(F32)
            out_ref[:, i * T : (i + 1) * T] = own + RELAX * total

    return pl.pallas_call(
        kernel,
        out_shape=jax.ShapeDtypeStruct((slices, held), F32),
        in_specs=[SMEM, VMEM, VMEM],
        out_specs=VMEM,
        compiler_params=params(12),
        cost_estimate=pl.CostEstimate(flops=2**18, bytes_accessed=2**20, transcendentals=0),
        name="image_step",
    )(quarter, image, parts)


def exchanged(array, axis):
    return lax.all_to_all(array, axis, split_axis=0, concat_axis=0, tiled=True)


def shards(projections, phase_kernel, image, tile_library, tile_entry, tile_image, tile_slot, tile_count, slot_block):
    projections = projections[0]
    library = tile_library[0, 0]
    image = image.T
    slices = projections.shape[0]
    quarters = lax.axis_size("ray")
    quarter = lax.axis_index("ray").astype(jnp.int32).reshape(1)
    tiles = (tile_entry[0], tile_image[0], tile_slot[0], tile_count)
    carried = slot_block[0]

    left = lax.ppermute(projections[:, -T:], "ray", [(i, i + 1) for i in range(quarters - 1)])
    right = lax.ppermute(projections[:, :T], "ray", [(i + 1, i) for i in range(quarters - 1)])
    phase, send = first_call(*tiles, carried, projections, left, right, band(phase_kernel), image, library)
    arrived = exchanged(send, "dom")
    numbers = lax.dynamic_slice_in_dim(arrived[:, slices + 18, :], lax.axis_index("dom"), 1, axis=1)
    theirs = numbers[:, 0].astype(jnp.int32)
    forward, back = back_call(carried, quarter, arrived, phase, quarters)
    returned = exchanged(back, "dom")
    update, stripe = adjoint_call(*tiles, theirs, returned, library, image.shape[1] // T)
    parts = exchanged(update, "ray")
    residual = residual_call(phase, stripe, forward)
    image_next = image_call(quarter, image, parts, quarters)
    return residual[None], image_next.T


def solution(mesh):
    return jax.shard_map(
        shards,
        mesh=mesh,
        in_specs=(
            P("dom", None, "ray"),
            P(),
            P("dom", None),
            P("dom", "ray", None, None, None),
            P("dom", "ray", None),
            P("dom", "ray", None),
            P("dom", "ray", None),
            P("dom", "ray"),
            P("dom", "ray", None),
        ),
        out_specs=(P("dom", None, "ray"), P(("dom", "ray"), None)),
        check_vma=False,
    )
```

```python
import jax
import jax.numpy as jnp
from jax import lax
from jax.experimental import pallas as pl
from jax.experimental.pallas import tpu as pltpu
from jax.sharding import PartitionSpec as P

T = 128
SMOOTH = 8
RELAX = 0.25
SECTION = 32
MIB = 2**20
F32, BF16 = jnp.float32, jnp.bfloat16
NT = (((1,), (1,)), ((), ()))
VMEM = pl.BlockSpec(memory_space=pltpu.VMEM)
SMEM = pl.BlockSpec(memory_space=pltpu.SMEM)
HBM = pl.BlockSpec(memory_space=pltpu.HBM)


def params(limit=63):
    return pltpu.CompilerParams(vmem_limit_bytes=limit * MIB)


def middle_network(n):
    pairs = []
    p = 1
    while p < n:
        k = p
        while k >= 1:
            for j in range(k % p, n - k, 2 * k):
                for i in range(min(k, n - j - k)):
                    if (i + j) // (2 * p) == (i + j + k) // (2 * p):
                        pairs.append((i + j, i + j + k))
            k //= 2
        p *= 2
    needed = {n // 2 - 1, n // 2}
    kept = []
    for a, b in reversed(pairs):
        if a in needed or b in needed:
            kept.append((a, b, a in needed, b in needed))
            needed |= {a, b}
    return kept[::-1]


def lanes(block):
    return pl.ds(pl.multiple_of(block * T, T), T)


def first_call(entry, place, slot, count, numbers, projections, left, right, taps, image, library):
    slices, columns = projections.shape
    entries, capacity = library.shape[0], entry.shape[1]
    blocks = image.shape[1] // T
    owners = slices
    per = columns // T
    rows = slices + SECTION
    parts = 4
    loads = per + blocks + 8

    def kernel(
        entry_hbm, place_hbm, slot_hbm, count_hbm, n_hbm, x_hbm, l_hbm, r_hbm, taps_ref, image_hbm, library_hbm,
        phase_ref, send_ref, entry_ref, place_ref, slot_ref, count_ref, n_ref, library_ref, wide, band, spread, row,
        stacked, product, total, packed, sems, load_sems,
    ):
        def block(n):
            return pl.ds(n * slices, slices)

        pairs = [(x_hbm.at[:, pl.ds(b * T, T)], wide.at[block(b + 2)]) for b in range(per)]
        pairs += [(l_hbm, wide.at[block(1)]), (r_hbm, wide.at[block(per + 2)]), (n_hbm, n_ref)]
        early = len(pairs)
        pairs += [(library_hbm, library_ref)]
        pairs += [(image_hbm.at[:, pl.ds(i * T, T)], stacked.at[block(i)]) for i in range(blocks)]
        late = len(pairs)
        pairs += [(entry_hbm, entry_ref), (place_hbm, place_ref), (slot_hbm, slot_ref), (count_hbm, count_ref)]
        fetches = [pltpu.make_async_copy(a, b, load_sems.at[n]) for n, (a, b) in enumerate(pairs)]
        for fetch in fetches:
            fetch.start()

        spread[...] = jnp.zeros_like(spread)
        row[...] = jnp.zeros_like(row)
        wide[block(0), :] = jnp.zeros((slices, T), BF16)
        wide[block(per + 3), :] = jnp.zeros((slices, T), BF16)
        spun = pltpu.roll(jnp.broadcast_to(taps_ref[0:1, :], (T, 3 * T)), T // 2, 1, stride=1, stride_axis=0)
        band[...] = spun.astype(BF16)
        for fetch in fetches[:early]:
            fetch.wait()
        filtered = sum(
            lax.dot_general(
                wide[n * slices : (n + per + 2) * slices, :],
                band[:, n * T : (n + 1) * T],
                NT,
                preferred_element_type=F32,
            )
            for n in range(3)
        ).astype(BF16)

        def put(at, value):
            spread[pl.ds(at, slices, stride=SECTION), :] = value.astype(F32)

        for b in range(per):
            value = filtered[(b + 1) * slices : (b + 2) * slices]
            phase_ref[:, b * T : (b + 1) * T] = value
            put(b, value)
        put(per, filtered[:slices])
        put(per + 1, filtered[(per + 1) * slices :])
        row[0:1, :owners] = n_ref[...].astype(F32)
        put(per + 2, jnp.broadcast_to(row[0:1, :], (slices, T)))
        packed[:, slices:, :] = spread[...].astype(BF16).reshape(slices, SECTION, T)

        total[...] = jnp.zeros_like(total)
        for fetch in fetches[early:late]:
            fetch.wait()
        for e in range(0, entries, 2):
            product[:, e * T : (e + 2) * T] = lax.dot_general(
                stacked[...], library_ref[e : e + 2].reshape(2 * T, T), NT, preferred_element_type=F32
            )
        for fetch in fetches[late:]:
            fetch.wait()

        def add(k):
            live = k < count_ref[0, 0]
            e = jnp.where(live, entry_ref[0, k], 0)
            i = jnp.where(live, place_ref[0, k], 0)
            s = jnp.where(live, slot_ref[0, k], owners)
            total[s] += product[pl.ds(pl.multiple_of(i * slices, slices), slices), lanes(e)]

        def group(g, carry):
            for u in range(8):
                add(g * 8 + u)
            return carry

        lax.fori_loop(0, (count_ref[0, 0] + 7) // 8, group, 0)
        step = owners // parts
        copies = []
        for n in range(parts):
            packed[n * step : (n + 1) * step, :slices, :] = total[n * step : (n + 1) * step].astype(BF16)
            here = pl.ds(n * step, step)
            copies.append(pltpu.make_async_copy(packed.at[here], send_ref.at[here], sems.at[n]))
            copies[-1].start()
        for copy in copies:
            copy.wait()

    return pl.pallas_call(
        kernel,
        out_shape=[
            jax.ShapeDtypeStruct((slices, columns), BF16),
            jax.ShapeDtypeStruct((owners, rows, T), BF16),
        ],
        in_specs=[HBM] * 8 + [VMEM] + [HBM] * 2,
        out_specs=[VMEM, HBM],
        scratch_shapes=[
            pltpu.SMEM(entry.shape, jnp.int32),
            pltpu.SMEM(place.shape, jnp.int32),
            pltpu.SMEM(slot.shape, jnp.int32),
            pltpu.SMEM(count.shape, jnp.int32),
            pltpu.VMEM(numbers.shape, jnp.int32),
            pltpu.VMEM(library.shape, BF16),
            pltpu.VMEM(((per + 4) * slices, T), BF16),
            pltpu.VMEM((T, 3 * T), BF16),
            pltpu.VMEM((slices * SECTION, T), F32),
            pltpu.VMEM((8, T), F32),
            pltpu.VMEM((blocks * slices, T), BF16),
            pltpu.VMEM((blocks * slices, entries * T), F32),
            pltpu.VMEM((owners + 1, slices, T), F32),
            pltpu.VMEM((owners, rows, T), BF16),
            pltpu.SemaphoreType.DMA((parts,)),
            pltpu.SemaphoreType.DMA((loads,)),
        ],
        compiler_params=params(),
        cost_estimate=pl.CostEstimate(
            flops=2 * capacity * slices * T * T, bytes_accessed=8 * 2**20, transcendentals=0
        ),
        name="filter_and_forward",
    )(entry, place, slot, count, numbers, projections, left, right, taps, image, library)


def stripe_of(quarter, quarters, section, values, rimmed):
    angles = section.shape[0]
    values[...] = section[...].astype(F32)
    network = middle_network(angles)

    def middle(g, carry):
        rows = pl.ds(pl.multiple_of(g * 8, 8), 8)
        v = [values[a, rows, :] for a in range(angles)]
        for a, b, low, high in network:
            x, y = v[a], v[b]
            if low:
                v[a] = jnp.minimum(x, y)
            if high:
                v[b] = jnp.maximum(x, y)
        rimmed[pl.ds(g * 8 + 1, 8), :] = (v[angles // 2 - 1] + v[angles // 2]) * 0.5
        return carry

    lax.fori_loop(0, 3, middle, 0)
    before, after = rimmed[17:18, :], rimmed[18:19, :]
    rimmed[0:1, :] = jnp.where(quarter == 0, jnp.zeros_like(before), before)
    rimmed[17:18, :] = jnp.where(quarter == quarters - 1, jnp.zeros_like(after), after)
    prev, cur, nxt = rimmed[0:16, :], rimmed[1:17, :], rimmed[2:18, :]
    lane = lax.broadcasted_iota(jnp.int32, (16, T), 1)
    total = cur
    for o in range(1, SMOOTH + 1):
        total += pltpu.roll(jnp.where(lane < o, nxt, cur), T - o, 1)
        total += pltpu.roll(jnp.where(lane >= T - o, prev, cur), o, 1)
    place = quarter * (16 * T) + lax.broadcasted_iota(jnp.int32, (16, T), 0) * T + lane
    last = quarters * 16 * T - 1
    count = jnp.minimum(place + SMOOTH, last) - jnp.maximum(place - SMOOTH, 0) + 1
    return cur - total / count.astype(F32)


def back_call(carried, quarter, arrived, phase, quarters):
    owners = arrived.shape[0]
    size, columns = phase.shape
    rows = size + 16
    parts = 4

    def kernel(
        c_ref, q_ref, arrived_hbm, phase_ref, forward_ref, send_ref, values, rimmed, less, packed, section, partial,
        sems, load_sems,
    ):
        step = owners // parts
        pairs = [(arrived_hbm.at[:, pl.ds(size, SECTION), :], section)]
        for n in range(parts):
            here = pl.ds(n * step, step)
            pairs.append((arrived_hbm.at[here, pl.ds(0, size), :], partial.at[here]))
        fetches = [pltpu.make_async_copy(a, b, load_sems.at[n]) for n, (a, b) in enumerate(pairs)]
        for fetch in fetches:
            fetch.start()
        forward_ref[...] = jnp.zeros_like(forward_ref)
        fetches[0].wait()
        stripe = stripe_of(q_ref[0], quarters, section, values, rimmed).astype(BF16)
        for n in range(parts):
            fetches[n + 1].wait()
            for d in range(n * step, (n + 1) * step):
                forward_ref[:, lanes(c_ref[0, d])] += partial[d].astype(F32)
        less[...] = (phase_ref[...].astype(F32) - forward_ref[...]).astype(BF16)
        copies = []
        for n in range(parts):
            for d in range(n * step, (n + 1) * step):
                packed[d, :size, :] = less[:, lanes(c_ref[0, d])]
                packed[d, size:, :] = stripe
            here = pl.ds(n * step, step)
            copies.append(pltpu.make_async_copy(packed.at[here], send_ref.at[here], sems.at[n]))
            copies[-1].start()
        for copy in copies:
            copy.wait()

    return pl.pallas_call(
        kernel,
        out_shape=[
            jax.ShapeDtypeStruct((size, columns), F32),
            jax.ShapeDtypeStruct((owners, rows, T), BF16),
        ],
        in_specs=[SMEM, SMEM, HBM, VMEM],
        out_specs=[VMEM, HBM],
        scratch_shapes=[
            pltpu.VMEM((owners, SECTION, T), F32),
            pltpu.VMEM((32, T), F32),
            pltpu.VMEM((size, columns), BF16),
            pltpu.VMEM((owners, rows, T), BF16),
            pltpu.VMEM((owners, SECTION, T), BF16),
            pltpu.VMEM((owners, size, T), BF16),
            pltpu.SemaphoreType.DMA((parts,)),
            pltpu.SemaphoreType.DMA((parts + 1,)),
        ],
        compiler_params=params(),
        cost_estimate=pl.CostEstimate(flops=2**24, bytes_accessed=8 * 2**20, transcendentals=0),
        name="sum_and_stripe",
    )(carried, quarter, arrived, phase)


def adjoint_call(entry, place, slot, count, theirs, returned, library, blocks):
    entries = library.shape[0]
    owners = returned.shape[0]
    per = 16
    size = returned.shape[1] - per

    def kernel(
        entry_hbm, place_hbm, slot_hbm, count_hbm, c_ref, returned_hbm, library_hbm,
        update_ref, stripe_ref, entry_ref, place_ref, slot_ref, count_ref, returned_ref, library_ref, stripes, terms,
        bins, loads,
    ):
        pairs = [(returned_hbm, returned_ref), (entry_hbm, entry_ref), (place_hbm, place_ref), (slot_hbm, slot_ref)]
        pairs += [(count_hbm, count_ref), (library_hbm, library_ref)]
        fetches = [pltpu.make_async_copy(a, b, loads.at[n]) for n, (a, b) in enumerate(pairs)]
        for fetch in fetches:
            fetch.start()
        bins[...] = jnp.zeros_like(bins)
        fetches[0].wait()
        stripes[...] = returned_ref[:, size:, :].astype(F32).reshape(owners * per, T)
        for b in range(per):
            stripe_ref[b] = stripes[pl.ds(b, size, stride=per), :]
        for e in range(owners):
            terms[e] = returned_ref[e, :size, :].astype(F32) - stripe_ref[c_ref[e]]
        terms[owners] = jnp.zeros((size, T), F32)
        for fetch in fetches[1:]:
            fetch.wait()

        def add(k):
            live = k < count_ref[0, 0]
            e = jnp.where(live, entry_ref[0, k], 0)
            i = jnp.where(live, place_ref[0, k], 0)
            s = jnp.where(live, slot_ref[0, k], owners)
            bins[pl.ds(pl.multiple_of(i * size, size), size), lanes(e)] += terms[s]

        def group(g, carry):
            for u in range(8):
                add(g * 8 + u)
            return carry

        lax.fori_loop(0, (count_ref[0, 0] + 7) // 8, group, 0)
        half = blocks // 2
        for h in range(2):
            update_ref[h * half : (h + 1) * half] = (
                jnp.dot(
                    bins[h * half * size : (h + 1) * half * size, :].astype(BF16),
                    library_ref[...].reshape(entries * T, T),
                    preferred_element_type=F32,
                )
                .astype(BF16)
                .reshape(half, size, T)
            )

    return pl.pallas_call(
        kernel,
        out_shape=[
            jax.ShapeDtypeStruct((blocks, size, T), BF16),
            jax.ShapeDtypeStruct((per, size, T), F32),
        ],
        in_specs=[HBM] * 4 + [SMEM, HBM, HBM],
        out_specs=[VMEM, VMEM],
        scratch_shapes=[
            pltpu.SMEM(entry.shape, jnp.int32),
            pltpu.SMEM(place.shape, jnp.int32),
            pltpu.SMEM(slot.shape, jnp.int32),
            pltpu.SMEM(count.shape, jnp.int32),
            pltpu.VMEM(returned.shape, BF16),
            pltpu.VMEM(library.shape, BF16),
            pltpu.VMEM((owners * per, T), F32),
            pltpu.VMEM((owners + 1, size, T), F32),
            pltpu.VMEM((blocks * size, entries * T), F32),
            pltpu.SemaphoreType.DMA((6,)),
        ],
        compiler_params=params(),
        cost_estimate=pl.CostEstimate(
            flops=2 * 256 * size * T * T, bytes_accessed=8 * 2**20, transcendentals=0
        ),
        name="adjoint_tiles",
    )(entry, place, slot, count, theirs, returned, library)


def residual_call(phase, stripe, forward):
    per = stripe.shape[0]

    def kernel(phase_ref, stripe_ref, forward_ref, residual_ref):
        for b in range(per):
            where = slice(b * T, (b + 1) * T)
            corrected = (phase_ref[:, where].astype(F32) - stripe_ref[b]).astype(BF16)
            residual_ref[:, where] = (corrected.astype(F32) - forward_ref[:, where]).astype(BF16)

    return pl.pallas_call(
        kernel,
        out_shape=jax.ShapeDtypeStruct(phase.shape, BF16),
        in_specs=[VMEM] * 3,
        out_specs=VMEM,
        compiler_params=params(12),
        cost_estimate=pl.CostEstimate(flops=2**19, bytes_accessed=2**21, transcendentals=0),
        name="residual",
    )(phase, stripe, forward)


def image_call(quarter, image, parts, quarters):
    slices, pixels = image.shape
    held = pixels // quarters
    mine = held // T

    def kernel(q_ref, image_ref, parts_ref, out_ref):
        for i in range(mine):
            total = parts_ref[i].astype(F32)
            for q in range(1, quarters):
                total += parts_ref[q * mine + i].astype(F32)
            own = image_ref[:, lanes(q_ref[0] * mine + i)].astype(F32)
            out_ref[:, i * T : (i + 1) * T] = own + RELAX * total

    return pl.pallas_call(
        kernel,
        out_shape=jax.ShapeDtypeStruct((slices, held), F32),
        in_specs=[SMEM, VMEM, VMEM],
        out_specs=VMEM,
        compiler_params=params(12),
        cost_estimate=pl.CostEstimate(flops=2**18, bytes_accessed=2**20, transcendentals=0),
        name="image_step",
    )(quarter, image, parts)


def exchanged(array, axis):
    return lax.all_to_all(array, axis, split_axis=0, concat_axis=0, tiled=True)


def shards(projections, phase_kernel, image, tile_library, tile_entry, tile_image, tile_slot, tile_count, slot_block):
    projections = projections[0]
    library = tile_library[0, 0]
    image = image.T
    slices = projections.shape[0]
    quarters = lax.axis_size("ray")
    quarter = lax.axis_index("ray").astype(jnp.int32).reshape(1)
    tiles = (tile_entry[0], tile_image[0], tile_slot[0], tile_count)
    carried = slot_block[0]

    left = lax.ppermute(projections[:, -T:], "ray", [(i, i + 1) for i in range(quarters - 1)])
    right = lax.ppermute(projections[:, :T], "ray", [(i + 1, i) for i in range(quarters - 1)])
    taps = jnp.pad(phase_kernel.astype(F32), (0, 3 * T - phase_kernel.shape[0])).reshape(1, 3 * T)
    phase, send = first_call(*tiles, carried, projections, left, right, taps, image, library)
    arrived = exchanged(send, "dom")
    numbers = lax.dynamic_slice_in_dim(arrived[:, slices + 18, :], lax.axis_index("dom"), 1, axis=1)
    theirs = numbers[:, 0].astype(jnp.int32)
    forward, back = back_call(carried, quarter, arrived, phase, quarters)
    returned = exchanged(back, "dom")
    update, stripe = adjoint_call(*tiles, theirs, returned, library, image.shape[1] // T)
    parts = exchanged(update, "ray")
    residual = residual_call(phase, stripe, forward)
    image_next = image_call(quarter, image, parts, quarters)
    return residual[None], image_next.T


def solution(mesh):
    return jax.shard_map(
        shards,
        mesh=mesh,
        in_specs=(
            P("dom", None, "ray"),
            P(),
            P("dom", None),
            P("dom", "ray", None, None, None),
            P("dom", "ray", None),
            P("dom", "ray", None),
            P("dom", "ray", None),
            P("dom", "ray"),
            P("dom", "ray", None),
        ),
        out_specs=(P("dom", None, "ray"), P(("dom", "ray"), None)),
        check_vma=False,
    )
```

```python
import jax
import jax.numpy as jnp
from jax import lax
from jax.experimental import pallas as pl
from jax.experimental.pallas import tpu as pltpu
from jax.sharding import PartitionSpec as P

T = 128
SMOOTH = 8
RELAX = 0.25
SECTION = 32
MIB = 2**20
F32, BF16 = jnp.float32, jnp.bfloat16
NT = (((1,), (1,)), ((), ()))
VMEM = pl.BlockSpec(memory_space=pltpu.VMEM)
SMEM = pl.BlockSpec(memory_space=pltpu.SMEM)
HBM = pl.BlockSpec(memory_space=pltpu.HBM)


def params(limit=32):
    return pltpu.CompilerParams(vmem_limit_bytes=limit * MIB)


def middle_network(n):
    pairs = []
    p = 1
    while p < n:
        k = p
        while k >= 1:
            for j in range(k % p, n - k, 2 * k):
                for i in range(min(k, n - j - k)):
                    if (i + j) // (2 * p) == (i + j + k) // (2 * p):
                        pairs.append((i + j, i + j + k))
            k //= 2
        p *= 2
    needed = {n // 2 - 1, n // 2}
    kept = []
    for a, b in reversed(pairs):
        if a in needed or b in needed:
            kept.append((a, b, a in needed, b in needed))
            needed |= {a, b}
    return kept[::-1]


def lanes(block):
    return pl.ds(pl.multiple_of(block * T, T), T)


def first_call(entry, place, slot, count, numbers, projections, left, right, taps, image, library):
    slices, columns = projections.shape
    entries, capacity = library.shape[0], entry.shape[1]
    blocks = image.shape[1] // T
    owners = slices
    per = columns // T
    rows = slices + SECTION
    parts = 4
    loads = per + blocks + 5

    def kernel(
        entry_hbm, place_hbm, slot_hbm, count_ref, n_hbm, x_hbm, l_ref, r_ref, taps_ref, image_hbm, library_hbm,
        phase_ref, send_ref, entry_ref, place_ref, slot_ref, n_ref, library_ref, wide, band, spread, row,
        stacked, product, total, packed, section, sems, load_sems,
    ):
        def block(n):
            return pl.ds(n * slices, slices)

        pairs = [(x_hbm.at[:, pl.ds(b * T, T)], wide.at[block(b + 2)]) for b in range(per)]
        pairs += [(n_hbm, n_ref)]
        early = len(pairs)
        pairs += [(library_hbm, library_ref)]
        pairs += [(image_hbm.at[:, pl.ds(i * T, T)], stacked.at[block(i)]) for i in range(blocks)]
        late = len(pairs)
        pairs += [(entry_hbm, entry_ref), (place_hbm, place_ref), (slot_hbm, slot_ref)]
        fetches = [pltpu.make_async_copy(a, b, load_sems.at[n]) for n, (a, b) in enumerate(pairs)]
        for fetch in fetches:
            fetch.start()

        spread[...] = jnp.zeros_like(spread)
        row[...] = jnp.zeros_like(row)
        wide[block(0), :] = jnp.zeros((slices, T), BF16)
        wide[block(1), :] = l_ref[...]
        wide[block(per + 2), :] = r_ref[...]
        wide[block(per + 3), :] = jnp.zeros((slices, T), BF16)
        spun = pltpu.roll(jnp.broadcast_to(taps_ref[0:1, :], (T, 3 * T)), T // 2, 1, stride=1, stride_axis=0)
        band[...] = spun.astype(BF16)
        for fetch in fetches[:early]:
            fetch.wait()
        filtered = sum(
            lax.dot_general(
                wide[n * slices : (n + per + 2) * slices, :],
                band[:, n * T : (n + 1) * T],
                NT,
                preferred_element_type=F32,
            )
            for n in range(3)
        ).astype(BF16)

        def put(at, value):
            spread[pl.ds(at, slices, stride=SECTION), :] = value.astype(F32)

        for b in range(per):
            value = filtered[(b + 1) * slices : (b + 2) * slices]
            phase_ref[:, b * T : (b + 1) * T] = value
            put(b, value)
        put(per, filtered[:slices])
        put(per + 1, filtered[(per + 1) * slices :])
        row[0:1, :owners] = n_ref[...].astype(F32)
        put(per + 2, jnp.broadcast_to(row[0:1, :], (slices, T)))
        section[...] = spread[...].astype(BF16).reshape(slices, SECTION, T)
        copies = [pltpu.make_async_copy(section, send_ref.at[:, pl.ds(slices, SECTION), :], sems.at[parts])]
        copies[0].start()

        total[...] = jnp.zeros_like(total)
        for fetch in fetches[early:late]:
            fetch.wait()
        for e in range(0, entries, 2):
            product[:, e * T : (e + 2) * T] = lax.dot_general(
                stacked[...], library_ref[e : e + 2].reshape(2 * T, T), NT, preferred_element_type=F32
            )
        for fetch in fetches[late:]:
            fetch.wait()

        def add(k):
            live = k < count_ref[0, 0]
            e = jnp.where(live, entry_ref[0, k], 0)
            i = jnp.where(live, place_ref[0, k], 0)
            s = jnp.where(live, slot_ref[0, k], owners)
            total[s] += product[pl.ds(pl.multiple_of(i * slices, slices), slices), lanes(e)]

        def group(g, carry):
            for u in range(8):
                add(g * 8 + u)
            return carry

        lax.fori_loop(0, (count_ref[0, 0] + 7) // 8, group, 0)
        step = owners // parts
        for n in range(parts):
            packed[n * step : (n + 1) * step] = total[n * step : (n + 1) * step].astype(BF16)
            here = pl.ds(n * step, step)
            copies.append(
                pltpu.make_async_copy(packed.at[here], send_ref.at[here, pl.ds(0, slices), :], sems.at[n])
            )
            copies[-1].start()
        for copy in copies:
            copy.wait()

    return pl.pallas_call(
        kernel,
        out_shape=[
            jax.ShapeDtypeStruct((slices, columns), BF16),
            pltpu.HBM((owners, rows, T), BF16),
        ],
        in_specs=[HBM] * 3 + [SMEM] + [HBM] * 2 + [VMEM] * 3 + [HBM] * 2,
        out_specs=[VMEM, HBM],
        scratch_shapes=[
            pltpu.SMEM(entry.shape, jnp.int32),
            pltpu.SMEM(place.shape, jnp.int32),
            pltpu.SMEM(slot.shape, jnp.int32),
            pltpu.VMEM(numbers.shape, jnp.int32),
            pltpu.VMEM(library.shape, BF16),
            pltpu.VMEM(((per + 4) * slices, T), BF16),
            pltpu.VMEM((T, 3 * T), BF16),
            pltpu.VMEM((slices * SECTION, T), F32),
            pltpu.VMEM((8, T), F32),
            pltpu.VMEM((blocks * slices, T), BF16),
            pltpu.VMEM((blocks * slices, entries * T), F32),
            pltpu.VMEM((owners + 1, slices, T), F32),
            pltpu.VMEM((owners, slices, T), BF16),
            pltpu.VMEM((slices, SECTION, T), BF16),
            pltpu.SemaphoreType.DMA((parts + 1,)),
            pltpu.SemaphoreType.DMA((loads,)),
        ],
        compiler_params=params(),
        cost_estimate=pl.CostEstimate(
            flops=2 * capacity * slices * T * T, bytes_accessed=8 * 2**20, transcendentals=0
        ),
        name="filter_and_forward",
    )(*map(in_hbm, (entry, place, slot)), count, *map(in_hbm, (numbers, projections)), left, right, taps,
      *map(in_hbm, (image, library)))


def stripe_of(quarter, quarters, arrived_ref, offset, values, rimmed):
    angles = arrived_ref.shape[0]
    values[...] = arrived_ref[:, offset:, :].astype(F32)
    network = middle_network(angles)

    def middle(g, carry):
        rows = pl.ds(pl.multiple_of(g * 8, 8), 8)
        v = [values[a, rows, :] for a in range(angles)]
        for a, b, low, high in network:
            x, y = v[a], v[b]
            if low:
                v[a] = jnp.minimum(x, y)
            if high:
                v[b] = jnp.maximum(x, y)
        rimmed[pl.ds(g * 8 + 1, 8), :] = (v[angles // 2 - 1] + v[angles // 2]) * 0.5
        return carry

    lax.fori_loop(0, 3, middle, 0)
    before, after = rimmed[17:18, :], rimmed[18:19, :]
    rimmed[0:1, :] = jnp.where(quarter == 0, jnp.zeros_like(before), before)
    rimmed[17:18, :] = jnp.where(quarter == quarters - 1, jnp.zeros_like(after), after)
    prev, cur, nxt = rimmed[0:16, :], rimmed[1:17, :], rimmed[2:18, :]
    lane = lax.broadcasted_iota(jnp.int32, (16, T), 1)
    total = cur
    for o in range(1, SMOOTH + 1):
        total += pltpu.roll(jnp.where(lane < o, nxt, cur), T - o, 1)
        total += pltpu.roll(jnp.where(lane >= T - o, prev, cur), o, 1)
    place = quarter * (16 * T) + lax.broadcasted_iota(jnp.int32, (16, T), 0) * T + lane
    last = quarters * 16 * T - 1
    count = jnp.minimum(place + SMOOTH, last) - jnp.maximum(place - SMOOTH, 0) + 1
    return cur - total / count.astype(F32)


def back_call(carried, quarter, arrived, phase, quarters):
    owners = arrived.shape[0]
    size, columns = phase.shape
    rows = size + 16
    parts = 4

    def kernel(
        c_ref, q_ref, arrived_ref, phase_ref, forward_hbm, send_ref, values, rimmed, forward, less, packed, sems
    ):
        forward[...] = jnp.zeros_like(forward)
        for d in range(owners):
            forward[:, lanes(c_ref[0, d])] += arrived_ref[d, :size, :].astype(F32)
        copies = [pltpu.make_async_copy(forward, forward_hbm, sems.at[parts])]
        copies[0].start()
        stripe = stripe_of(q_ref[0], quarters, arrived_ref, size, values, rimmed).astype(BF16)
        less[...] = (phase_ref[...].astype(F32) - forward[...]).astype(BF16)
        step = owners // parts
        for n in range(parts):
            for d in range(n * step, (n + 1) * step):
                packed[d, :size, :] = less[:, lanes(c_ref[0, d])]
                packed[d, size:, :] = stripe
            here = pl.ds(n * step, step)
            copies.append(pltpu.make_async_copy(packed.at[here], send_ref.at[here], sems.at[n]))
            copies[-1].start()
        for copy in copies:
            copy.wait()

    return pl.pallas_call(
        kernel,
        out_shape=[
            pltpu.HBM((size, columns), F32),
            pltpu.HBM((owners, rows, T), BF16),
        ],
        in_specs=[SMEM, SMEM, VMEM, VMEM],
        out_specs=[HBM, HBM],
        scratch_shapes=[
            pltpu.VMEM((owners, SECTION, T), F32),
            pltpu.VMEM((32, T), F32),
            pltpu.VMEM((size, columns), F32),
            pltpu.VMEM((size, columns), BF16),
            pltpu.VMEM((owners, rows, T), BF16),
            pltpu.SemaphoreType.DMA((parts + 1,)),
        ],
        compiler_params=params(),
        cost_estimate=pl.CostEstimate(flops=2**24, bytes_accessed=8 * 2**20, transcendentals=0),
        name="sum_and_stripe",
    )(carried, quarter, arrived, phase)


def adjoint_call(entry, place, slot, count, theirs, returned, library, blocks):
    entries = library.shape[0]
    owners = returned.shape[0]
    per = 16
    size = returned.shape[1] - per

    def kernel(
        entry_hbm, place_hbm, slot_hbm, count_ref, c_ref, returned_ref, library_hbm,
        update_hbm, stripe_ref, entry_ref, place_ref, slot_ref, library_ref, stripes, terms, bins, update, loads,
        sems,
    ):
        pairs = [(entry_hbm, entry_ref), (place_hbm, place_ref), (slot_hbm, slot_ref), (library_hbm, library_ref)]
        fetches = [pltpu.make_async_copy(a, b, loads.at[n]) for n, (a, b) in enumerate(pairs)]
        for fetch in fetches:
            fetch.start()
        bins[...] = jnp.zeros_like(bins)
        stripes[...] = returned_ref[:, size:, :].astype(F32).reshape(owners * per, T)
        for b in range(per):
            stripe_ref[b] = stripes[pl.ds(b, size, stride=per), :]
        for e in range(owners):
            terms[e] = returned_ref[e, :size, :].astype(F32) - stripe_ref[c_ref[e]]
        terms[owners] = jnp.zeros((size, T), F32)
        for fetch in fetches:
            fetch.wait()

        def add(k):
            live = k < count_ref[0, 0]
            e = jnp.where(live, entry_ref[0, k], 0)
            i = jnp.where(live, place_ref[0, k], 0)
            s = jnp.where(live, slot_ref[0, k], owners)
            bins[pl.ds(pl.multiple_of(i * size, size), size), lanes(e)] += terms[s]

        def group(g, carry):
            for u in range(8):
                add(g * 8 + u)
            return carry

        lax.fori_loop(0, (count_ref[0, 0] + 7) // 8, group, 0)
        half = blocks // 2
        copies = []
        for h in range(2):
            here = pl.ds(h * half, half)
            update[here] = (
                jnp.dot(
                    bins[h * half * size : (h + 1) * half * size, :].astype(BF16),
                    library_ref[...].reshape(entries * T, T),
                    preferred_element_type=F32,
                )
                .astype(BF16)
                .reshape(half, size, T)
            )
            copies.append(pltpu.make_async_copy(update.at[here], update_hbm.at[here], sems.at[h]))
            copies[-1].start()
        for copy in copies:
            copy.wait()

    return pl.pallas_call(
        kernel,
        out_shape=[
            pltpu.HBM((blocks, size, T), BF16),
            jax.ShapeDtypeStruct((per, size, T), F32),
        ],
        in_specs=[HBM] * 3 + [SMEM, SMEM, VMEM, HBM],
        out_specs=[HBM, VMEM],
        scratch_shapes=[
            pltpu.SMEM(entry.shape, jnp.int32),
            pltpu.SMEM(place.shape, jnp.int32),
            pltpu.SMEM(slot.shape, jnp.int32),
            pltpu.VMEM(library.shape, BF16),
            pltpu.VMEM((owners * per, T), F32),
            pltpu.VMEM((owners + 1, size, T), F32),
            pltpu.VMEM((blocks * size, entries * T), F32),
            pltpu.VMEM((blocks, size, T), BF16),
            pltpu.SemaphoreType.DMA((4,)),
            pltpu.SemaphoreType.DMA((2,)),
        ],
        compiler_params=params(),
        cost_estimate=pl.CostEstimate(
            flops=2 * 256 * size * T * T, bytes_accessed=8 * 2**20, transcendentals=0
        ),
        name="adjoint_tiles",
    )(*map(in_hbm, (entry, place, slot)), count, theirs, returned, in_hbm(library))


def residual_call(phase, stripe, forward):
    per = stripe.shape[0]

    def kernel(phase_ref, stripe_ref, forward_ref, residual_ref):
        for b in range(per):
            where = slice(b * T, (b + 1) * T)
            corrected = (phase_ref[:, where].astype(F32) - stripe_ref[b]).astype(BF16)
            residual_ref[:, where] = (corrected.astype(F32) - forward_ref[:, where]).astype(BF16)

    return pl.pallas_call(
        kernel,
        out_shape=jax.ShapeDtypeStruct(phase.shape, BF16),
        in_specs=[VMEM] * 3,
        out_specs=VMEM,
        compiler_params=params(),
        cost_estimate=pl.CostEstimate(flops=2**19, bytes_accessed=2**21, transcendentals=0),
        name="residual",
    )(phase, stripe, forward)


def image_call(quarter, image, parts, quarters):
    slices, pixels = image.shape
    held = pixels // quarters
    mine = held // T

    def kernel(q_ref, image_ref, parts_ref, out_ref):
        for i in range(mine):
            total = parts_ref[i].astype(F32)
            for q in range(1, quarters):
                total += parts_ref[q * mine + i].astype(F32)
            own = image_ref[:, lanes(q_ref[0] * mine + i)].astype(F32)
            out_ref[:, i * T : (i + 1) * T] = own + RELAX * total

    return pl.pallas_call(
        kernel,
        out_shape=jax.ShapeDtypeStruct((slices, held), F32),
        in_specs=[SMEM, VMEM, VMEM],
        out_specs=VMEM,
        compiler_params=params(),
        cost_estimate=pl.CostEstimate(flops=2**18, bytes_accessed=2**20, transcendentals=0),
        name="image_step",
    )(quarter, image, parts)


def in_hbm(array):
    return pltpu.with_memory_space_constraint(array, pltpu.HBM)


def exchanged(array, axis):
    return lax.all_to_all(array, axis, split_axis=0, concat_axis=0, tiled=True)


def shards(projections, phase_kernel, image, tile_library, tile_entry, tile_image, tile_slot, tile_count, slot_block):
    projections = projections[0]
    library = tile_library[0, 0]
    image = image.T
    slices = projections.shape[0]
    quarters = lax.axis_size("ray")
    quarter = lax.axis_index("ray").astype(jnp.int32).reshape(1)
    tiles = (tile_entry[0], tile_image[0], tile_slot[0], tile_count)
    carried = slot_block[0]

    left = lax.ppermute(projections[:, -T:], "ray", [(i, i + 1) for i in range(quarters - 1)])
    right = lax.ppermute(projections[:, :T], "ray", [(i + 1, i) for i in range(quarters - 1)])
    taps = jnp.pad(phase_kernel[None].astype(F32), ((0, 0), (0, 3 * T - phase_kernel.shape[0])))
    phase, send = first_call(*tiles, carried, projections, left, right, taps, image, library)
    arrived = exchanged(send, "dom")
    numbers = lax.dynamic_slice_in_dim(arrived[:, slices + 18, :], lax.axis_index("dom"), 1, axis=1)
    theirs = numbers[:, 0].astype(jnp.int32)
    forward, back = back_call(carried, quarter, arrived, phase, quarters)
    returned = exchanged(back, "dom")
    update, stripe = adjoint_call(*tiles, theirs, returned, library, image.shape[1] // T)
    parts = exchanged(update, "ray")
    residual = residual_call(phase, stripe, forward)
    image_next = image_call(quarter, image, parts, quarters)
    return residual[None], image_next.T


def solution(mesh):
    return jax.shard_map(
        shards,
        mesh=mesh,
        in_specs=(
            P("dom", None, "ray"),
            P(),
            P("dom", None),
            P("dom", "ray", None, None, None),
            P("dom", "ray", None),
            P("dom", "ray", None),
            P("dom", "ray", None),
            P("dom", "ray"),
            P("dom", "ray", None),
        ),
        out_specs=(P("dom", None, "ray"), P(("dom", "ray"), None)),
        check_vma=False,
    )
```

```python
import jax
import jax.numpy as jnp
from jax import lax
from jax.experimental import pallas as pl
from jax.experimental.pallas import tpu as pltpu
from jax.sharding import PartitionSpec as P

T = 128
SMOOTH = 8
RELAX = 0.25
SECTION = 32
MIB = 2**20
F32, BF16 = jnp.float32, jnp.bfloat16
NT = (((1,), (1,)), ((), ()))
VMEM = pl.BlockSpec(memory_space=pltpu.VMEM)
SMEM = pl.BlockSpec(memory_space=pltpu.SMEM)
HBM = pl.BlockSpec(memory_space=pltpu.HBM)


def params(limit=32):
    return pltpu.CompilerParams(vmem_limit_bytes=limit * MIB)


def middle_network(n):
    pairs = []
    p = 1
    while p < n:
        k = p
        while k >= 1:
            for j in range(k % p, n - k, 2 * k):
                for i in range(min(k, n - j - k)):
                    if (i + j) // (2 * p) == (i + j + k) // (2 * p):
                        pairs.append((i + j, i + j + k))
            k //= 2
        p *= 2
    needed = {n // 2 - 1, n // 2}
    kept = []
    for a, b in reversed(pairs):
        if a in needed or b in needed:
            kept.append((a, b, a in needed, b in needed))
            needed |= {a, b}
    return kept[::-1]


def lanes(block):
    return pl.ds(pl.multiple_of(block * T, T), T)


def first_call(entry, place, slot, count, numbers, projections, left, right, taps, image, library):
    slices, columns = projections.shape
    entries, capacity = library.shape[0], entry.shape[1]
    blocks = image.shape[1] // T
    owners = slices
    per = columns // T
    rows = slices + SECTION
    parts = 4
    loads = per + blocks + 5

    def kernel(
        entry_hbm, place_hbm, slot_hbm, count_ref, n_hbm, x_hbm, l_ref, r_ref, taps_ref, image_hbm, library_hbm,
        phase_ref, send_ref, entry_ref, place_ref, slot_ref, n_ref, library_ref, wide, band, spread, row, line,
        stacked, product, total, packed, section, sems, load_sems,
    ):
        def block(n):
            return pl.ds(n * slices, slices)

        pairs = [(x_hbm.at[:, pl.ds(b * T, T)], wide.at[block(b + 2)]) for b in range(per)]
        pairs += [(n_hbm, n_ref)]
        early = len(pairs)
        pairs += [(library_hbm, library_ref)]
        pairs += [(image_hbm.at[:, pl.ds(i * T, T)], stacked.at[block(i)]) for i in range(blocks)]
        late = len(pairs)
        pairs += [(entry_hbm, entry_ref), (place_hbm, place_ref), (slot_hbm, slot_ref)]
        fetches = [pltpu.make_async_copy(a, b, load_sems.at[n]) for n, (a, b) in enumerate(pairs)]
        for fetch in fetches:
            fetch.start()

        spread[...] = jnp.zeros_like(spread)
        row[...] = jnp.zeros_like(row)
        wide[block(0), :] = jnp.zeros((slices, T), BF16)
        wide[block(1), :] = l_ref[...]
        wide[block(per + 2), :] = r_ref[...]
        wide[block(per + 3), :] = jnp.zeros((slices, T), BF16)
        line[...] = jnp.zeros_like(line)
        line[0:1, : taps_ref.shape[1]] = taps_ref[...].astype(F32)
        spun = pltpu.roll(jnp.broadcast_to(line[0:1, :], (T, 3 * T)), T // 2, 1, stride=1, stride_axis=0)
        band[...] = spun.astype(BF16)
        for fetch in fetches[:early]:
            fetch.wait()
        filtered = sum(
            lax.dot_general(
                wide[n * slices : (n + per + 2) * slices, :],
                band[:, n * T : (n + 1) * T],
                NT,
                preferred_element_type=F32,
            )
            for n in range(3)
        ).astype(BF16)

        def put(at, value):
            spread[pl.ds(at, slices, stride=SECTION), :] = value.astype(F32)

        for b in range(per):
            value = filtered[(b + 1) * slices : (b + 2) * slices]
            phase_ref[:, b * T : (b + 1) * T] = value
            put(b, value)
        put(per, filtered[:slices])
        put(per + 1, filtered[(per + 1) * slices :])
        row[0:1, :owners] = n_ref[...].astype(F32)
        put(per + 2, jnp.broadcast_to(row[0:1, :], (slices, T)))
        section[...] = spread[...].astype(BF16).reshape(slices, SECTION, T)
        copies = [pltpu.make_async_copy(section, send_ref.at[:, pl.ds(slices, SECTION), :], sems.at[parts])]
        copies[0].start()

        total[...] = jnp.zeros_like(total)
        for fetch in fetches[early:late]:
            fetch.wait()
        for e in range(0, entries, 2):
            product[:, e * T : (e + 2) * T] = lax.dot_general(
                stacked[...], library_ref[e : e + 2].reshape(2 * T, T), NT, preferred_element_type=F32
            )
        for fetch in fetches[late:]:
            fetch.wait()

        def add(k):
            live = k < count_ref[0, 0]
            e = jnp.where(live, entry_ref[0, k], 0)
            i = jnp.where(live, place_ref[0, k], 0)
            s = jnp.where(live, slot_ref[0, k], owners)
            total[s] += product[pl.ds(pl.multiple_of(i * slices, slices), slices), lanes(e)]

        def group(g, carry):
            for u in range(8):
                add(g * 8 + u)
            return carry

        lax.fori_loop(0, (count_ref[0, 0] + 7) // 8, group, 0)
        step = owners // parts
        for n in range(parts):
            packed[n * step : (n + 1) * step] = total[n * step : (n + 1) * step].astype(BF16)
            here = pl.ds(n * step, step)
            copies.append(
                pltpu.make_async_copy(packed.at[here], send_ref.at[here, pl.ds(0, slices), :], sems.at[n])
            )
            copies[-1].start()
        for copy in copies:
            copy.wait()

    return pl.pallas_call(
        kernel,
        out_shape=[
            jax.ShapeDtypeStruct((slices, columns), BF16),
            pltpu.HBM((owners, rows, T), BF16),
        ],
        in_specs=[HBM] * 3 + [SMEM] + [HBM] * 2 + [VMEM] * 3 + [HBM] * 2,
        out_specs=[VMEM, HBM],
        scratch_shapes=[
            pltpu.SMEM(entry.shape, jnp.int32),
            pltpu.SMEM(place.shape, jnp.int32),
            pltpu.SMEM(slot.shape, jnp.int32),
            pltpu.VMEM(numbers.shape, jnp.int32),
            pltpu.VMEM(library.shape, BF16),
            pltpu.VMEM(((per + 4) * slices, T), BF16),
            pltpu.VMEM((T, 3 * T), BF16),
            pltpu.VMEM((slices * SECTION, T), F32),
            pltpu.VMEM((8, T), F32),
            pltpu.VMEM((8, 3 * T), F32),
            pltpu.VMEM((blocks * slices, T), BF16),
            pltpu.VMEM((blocks * slices, entries * T), F32),
            pltpu.VMEM((owners + 1, slices, T), F32),
            pltpu.VMEM((owners, slices, T), BF16),
            pltpu.VMEM((slices, SECTION, T), BF16),
            pltpu.SemaphoreType.DMA((parts + 1,)),
            pltpu.SemaphoreType.DMA((loads,)),
        ],
        compiler_params=params(),
        cost_estimate=pl.CostEstimate(
            flops=2 * capacity * slices * T * T, bytes_accessed=8 * 2**20, transcendentals=0
        ),
        name="filter_and_forward",
    )(*map(in_hbm, (entry, place, slot)), count, *map(in_hbm, (numbers, projections)), left, right, taps,
      *map(in_hbm, (image, library)))


def stripe_of(quarter, quarters, arrived_ref, offset, values, rimmed):
    angles = arrived_ref.shape[0]
    values[...] = arrived_ref[:, offset:, :].astype(F32)
    network = middle_network(angles)

    def middle(g, carry):
        rows = pl.ds(pl.multiple_of(g * 8, 8), 8)
        v = [values[a, rows, :] for a in range(angles)]
        for a, b, low, high in network:
            x, y = v[a], v[b]
            if low:
                v[a] = jnp.minimum(x, y)
            if high:
                v[b] = jnp.maximum(x, y)
        rimmed[pl.ds(g * 8 + 1, 8), :] = (v[angles // 2 - 1] + v[angles // 2]) * 0.5
        return carry

    lax.fori_loop(0, 3, middle, 0)
    before, after = rimmed[17:18, :], rimmed[18:19, :]
    rimmed[0:1, :] = jnp.where(quarter == 0, jnp.zeros_like(before), before)
    rimmed[17:18, :] = jnp.where(quarter == quarters - 1, jnp.zeros_like(after), after)
    prev, cur, nxt = rimmed[0:16, :], rimmed[1:17, :], rimmed[2:18, :]
    lane = lax.broadcasted_iota(jnp.int32, (16, T), 1)
    total = cur
    for o in range(1, SMOOTH + 1):
        total += pltpu.roll(jnp.where(lane < o, nxt, cur), T - o, 1)
        total += pltpu.roll(jnp.where(lane >= T - o, prev, cur), o, 1)
    place = quarter * (16 * T) + lax.broadcasted_iota(jnp.int32, (16, T), 0) * T + lane
    last = quarters * 16 * T - 1
    count = jnp.minimum(place + SMOOTH, last) - jnp.maximum(place - SMOOTH, 0) + 1
    return cur - total / count.astype(F32)


def back_call(carried, quarter, arrived, phase, quarters):
    owners = arrived.shape[0]
    size, columns = phase.shape
    rows = size + 16
    parts = 4

    def kernel(
        c_ref, q_ref, arrived_ref, phase_ref, forward_hbm, send_ref, values, rimmed, forward, less, packed, sems
    ):
        forward[...] = jnp.zeros_like(forward)
        for d in range(owners):
            forward[:, lanes(c_ref[0, d])] += arrived_ref[d, :size, :].astype(F32)
        copies = [pltpu.make_async_copy(forward, forward_hbm, sems.at[parts])]
        copies[0].start()
        stripe = stripe_of(q_ref[0], quarters, arrived_ref, size, values, rimmed).astype(BF16)
        less[...] = (phase_ref[...].astype(F32) - forward[...]).astype(BF16)
        step = owners // parts
        for n in range(parts):
            for d in range(n * step, (n + 1) * step):
                packed[d, :size, :] = less[:, lanes(c_ref[0, d])]
                packed[d, size:, :] = stripe
            here = pl.ds(n * step, step)
            copies.append(pltpu.make_async_copy(packed.at[here], send_ref.at[here], sems.at[n]))
            copies[-1].start()
        for copy in copies:
            copy.wait()

    return pl.pallas_call(
        kernel,
        out_shape=[
            pltpu.HBM((size, columns), F32),
            pltpu.HBM((owners, rows, T), BF16),
        ],
        in_specs=[SMEM, SMEM, VMEM, VMEM],
        out_specs=[HBM, HBM],
        scratch_shapes=[
            pltpu.VMEM((owners, SECTION, T), F32),
            pltpu.VMEM((32, T), F32),
            pltpu.VMEM((size, columns), F32),
            pltpu.VMEM((size, columns), BF16),
            pltpu.VMEM((owners, rows, T), BF16),
            pltpu.SemaphoreType.DMA((parts + 1,)),
        ],
        compiler_params=params(),
        cost_estimate=pl.CostEstimate(flops=2**24, bytes_accessed=8 * 2**20, transcendentals=0),
        name="sum_and_stripe",
    )(carried, quarter, arrived, phase)


def counts_call(entry, place, slot, count, owner, arrived, entries, blocks):
    capacity = entry.shape[1]
    owners = arrived.shape[0]
    size = arrived.shape[1] - SECTION

    def kernel(
        entry_hbm, place_hbm, slot_hbm, count_ref, owner_ref, arrived_ref,
        weights_ref, entry_ref, place_ref, slot_ref, loads,
    ):
        pairs = [(entry_hbm, entry_ref), (place_hbm, place_ref), (slot_hbm, slot_ref)]
        fetches = [pltpu.make_async_copy(a, b, loads.at[n]) for n, (a, b) in enumerate(pairs)]
        for fetch in fetches:
            fetch.start()
        lane = lax.broadcasted_iota(jnp.int32, (owners, T), 1)
        numbers = arrived_ref[:, size + 16 :, :].astype(F32)[:, 2, :]
        theirs = jnp.sum(jnp.where(lane == owner_ref[0], numbers, 0.0), axis=1, keepdims=True)
        carries = (theirs.astype(jnp.int32) + owners == lane).astype(F32).astype(BF16)

        def ones(rows, match):
            return (lax.broadcasted_iota(jnp.int32, (rows, match.shape[1]), 0) == match).astype(F32).astype(BF16)

        for fetch in fetches:
            fetch.wait()
        live = lax.broadcasted_iota(jnp.int32, (1, capacity), 1) < count_ref[0, 0]
        of_bin = ones(entries * blocks, jnp.where(live, entry_ref[...] * blocks + place_ref[...], -1))
        of_slot = ones(T, slot_ref[...])
        met = lax.dot_general(of_bin, of_slot, NT, preferred_element_type=F32)
        stripe_met = jnp.dot(met[:, :owners].astype(BF16), carries, preferred_element_type=F32)
        weights_ref[...] = (met - stripe_met).astype(BF16)

    return pl.pallas_call(
        kernel,
        out_shape=jax.ShapeDtypeStruct((entries * blocks, T), BF16),
        in_specs=[HBM] * 3 + [SMEM, SMEM, VMEM],
        out_specs=VMEM,
        scratch_shapes=[
            pltpu.VMEM(entry.shape, jnp.int32),
            pltpu.VMEM(place.shape, jnp.int32),
            pltpu.VMEM(slot.shape, jnp.int32),
            pltpu.SemaphoreType.DMA((3,)),
        ],
        compiler_params=params(),
        cost_estimate=pl.CostEstimate(flops=2**24, bytes_accessed=2**20, transcendentals=0),
        name="tile_counts",
    )(*map(in_hbm, (entry, place, slot)), count, owner, arrived)


def adjoint_call(weights, returned, library, blocks):
    entries = library.shape[0]
    owners = returned.shape[0]
    per = 16
    size = returned.shape[1] - per
    parts = 4

    def kernel(
        weights_ref, returned_ref, library_hbm, update_hbm, stripe_ref, library_ref, stripes, terms, bins, whole,
        update, load, sems,
    ):
        fetch = pltpu.make_async_copy(library_hbm, library_ref, load)
        fetch.start()
        stripes[...] = returned_ref[:, size:, :].astype(F32).reshape(owners * per, T)
        terms[...] = returned_ref[:, :size, :].astype(F32).reshape(owners * size, T)
        weights = weights_ref[:, : owners + per]

        def both(n):
            here = terms[pl.ds(n, owners, stride=size), :].astype(BF16)
            return jnp.concatenate([here, returned_ref[n, size:, :]], axis=0)

        for n in range(0, size, 2):
            made = jnp.dot(
                weights, jnp.concatenate([both(n), both(n + 1)], axis=1), preferred_element_type=F32
            ).astype(BF16)
            for u in range(2):
                for e in range(entries):
                    bins[(n + u) * blocks : (n + u + 1) * blocks, e * T : (e + 1) * T] = made[
                        e * blocks : (e + 1) * blocks, u * T : (u + 1) * T
                    ]
        fetch.wait()
        held = size // parts
        copies = []
        for h in range(parts):
            rows = slice(h * held * blocks, (h + 1) * held * blocks)
            whole[rows, :] = jnp.dot(
                bins[rows, :], library_ref[...].reshape(entries * T, T), preferred_element_type=F32
            )
            for i in range(blocks):
                update[i, h * held : (h + 1) * held, :] = whole[
                    pl.ds(h * held * blocks + i, held, stride=blocks), :
                ].astype(BF16)
            here = pl.ds(h * held, held)
            copies.append(
                pltpu.make_async_copy(update.at[:, here, :], update_hbm.at[:, here, :], sems.at[h])
            )
            copies[-1].start()
        for b in range(per):
            stripe_ref[b] = stripes[pl.ds(b, size, stride=per), :]
        for copy in copies:
            copy.wait()

    return pl.pallas_call(
        kernel,
        out_shape=[
            pltpu.HBM((blocks, size, T), BF16),
            jax.ShapeDtypeStruct((per, size, T), F32),
        ],
        in_specs=[VMEM, VMEM, HBM],
        out_specs=[HBM, VMEM],
        scratch_shapes=[
            pltpu.VMEM(library.shape, BF16),
            pltpu.VMEM((owners * per, T), F32),
            pltpu.VMEM((owners * size, T), F32),
            pltpu.VMEM((size * blocks, entries * T), BF16),
            pltpu.VMEM((size * blocks, T), F32),
            pltpu.VMEM((blocks, size, T), BF16),
            pltpu.SemaphoreType.DMA,
            pltpu.SemaphoreType.DMA((parts,)),
        ],
        compiler_params=params(),
        cost_estimate=pl.CostEstimate(
            flops=2 * 256 * size * T * T, bytes_accessed=8 * 2**20, transcendentals=0
        ),
        name="adjoint_tiles",
    )(weights, returned, in_hbm(library))


def residual_call(phase, stripe, forward):
    per = stripe.shape[0]

    def kernel(phase_ref, stripe_ref, forward_ref, residual_ref):
        for b in range(per):
            where = slice(b * T, (b + 1) * T)
            corrected = (phase_ref[:, where].astype(F32) - stripe_ref[b]).astype(BF16)
            residual_ref[:, where] = (corrected.astype(F32) - forward_ref[:, where]).astype(BF16)

    return pl.pallas_call(
        kernel,
        out_shape=jax.ShapeDtypeStruct(phase.shape, BF16),
        in_specs=[VMEM] * 3,
        out_specs=VMEM,
        compiler_params=params(),
        cost_estimate=pl.CostEstimate(flops=2**19, bytes_accessed=2**21, transcendentals=0),
        name="residual",
    )(phase, stripe, forward)


def image_call(quarter, image, parts, quarters):
    slices, pixels = image.shape
    held = pixels // quarters
    mine = held // T

    def kernel(q_ref, image_ref, parts_ref, out_ref):
        for i in range(mine):
            total = parts_ref[i].astype(F32)
            for q in range(1, quarters):
                total += parts_ref[q * mine + i].astype(F32)
            own = image_ref[:, lanes(q_ref[0] * mine + i)].astype(F32)
            out_ref[:, i * T : (i + 1) * T] = own + RELAX * total

    return pl.pallas_call(
        kernel,
        out_shape=jax.ShapeDtypeStruct((slices, held), F32),
        in_specs=[SMEM, VMEM, VMEM],
        out_specs=VMEM,
        compiler_params=params(),
        cost_estimate=pl.CostEstimate(flops=2**18, bytes_accessed=2**20, transcendentals=0),
        name="image_step",
    )(quarter, image, parts)


def in_hbm(array):
    return pltpu.with_memory_space_constraint(array, pltpu.HBM)


def exchanged(array, axis):
    return lax.all_to_all(array, axis, split_axis=0, concat_axis=0, tiled=True)


def shards(projections, phase_kernel, image, tile_library, tile_entry, tile_image, tile_slot, tile_count, slot_block):
    projections = projections[0]
    library = tile_library[0, 0]
    image = image.T
    slices = projections.shape[0]
    quarters = lax.axis_size("ray")
    quarter = lax.axis_index("ray").astype(jnp.int32).reshape(1)
    tiles = (tile_entry[0], tile_image[0], tile_slot[0], tile_count)
    carried = slot_block[0]

    left = lax.ppermute(projections[:, -T:], "ray", [(i, i + 1) for i in range(quarters - 1)])
    right = lax.ppermute(projections[:, :T], "ray", [(i + 1, i) for i in range(quarters - 1)])
    taps = phase_kernel.reshape(1, -1)
    phase, send = first_call(*tiles, carried, projections, left, right, taps, image, library)
    arrived = exchanged(send, "dom")
    forward, back = back_call(carried, quarter, arrived, phase, quarters)
    owner = lax.axis_index("dom").astype(jnp.int32).reshape(1)
    blocks = image.shape[1] // T
    weights = counts_call(*tiles, owner, arrived, library.shape[0], blocks)
    returned = exchanged(back, "dom")
    update, stripe = adjoint_call(weights, returned, library, blocks)
    parts = exchanged(update, "ray")
    residual = residual_call(phase, stripe, forward)
    image_next = image_call(quarter, image, parts, quarters)
    return residual[None], image_next.T


def solution(mesh):
    return jax.shard_map(
        shards,
        mesh=mesh,
        in_specs=(
            P("dom", None, "ray"),
            P(),
            P("dom", None),
            P("dom", "ray", None, None, None),
            P("dom", "ray", None),
            P("dom", "ray", None),
            P("dom", "ray", None),
            P("dom", "ray"),
            P("dom", "ray", None),
        ),
        out_specs=(P("dom", None, "ray"), P(("dom", "ray"), None)),
        check_vma=False,
    )
```

```python
import jax
import jax.numpy as jnp
from jax import lax
from jax.experimental import pallas as pl
from jax.experimental.pallas import tpu as pltpu
from jax.sharding import PartitionSpec as P

T = 128
SMOOTH = 8
RELAX = 0.25
SECTION = 32
MIB = 2**20
F32, BF16 = jnp.float32, jnp.bfloat16
NT = (((1,), (1,)), ((), ()))
VMEM = pl.BlockSpec(memory_space=pltpu.VMEM)
SMEM = pl.BlockSpec(memory_space=pltpu.SMEM)
HBM = pl.BlockSpec(memory_space=pltpu.HBM)


def params(limit=32):
    return pltpu.CompilerParams(vmem_limit_bytes=limit * MIB)


def middle_network(n):
    pairs = []
    p = 1
    while p < n:
        k = p
        while k >= 1:
            for j in range(k % p, n - k, 2 * k):
                for i in range(min(k, n - j - k)):
                    if (i + j) // (2 * p) == (i + j + k) // (2 * p):
                        pairs.append((i + j, i + j + k))
            k //= 2
        p *= 2
    needed = {n // 2 - 1, n // 2}
    kept = []
    for a, b in reversed(pairs):
        if a in needed or b in needed:
            kept.append((a, b, a in needed, b in needed))
            needed |= {a, b}
    return kept[::-1]


def lanes(block):
    return pl.ds(pl.multiple_of(block * T, T), T)


def first_call(entry, place, slot, count, numbers, projections, left, right, taps, image, library):
    slices, columns = projections.shape
    entries, capacity = library.shape[0], entry.shape[1]
    blocks = image.shape[1] // T
    owners = slices
    per = columns // T
    rows = slices + SECTION
    parts = 4
    loads = per + blocks + 5

    def kernel(
        entry_hbm, place_hbm, slot_hbm, count_ref, n_hbm, x_hbm, l_ref, r_ref, taps_ref, image_hbm, library_hbm,
        phase_ref, send_ref, entry_ref, place_ref, slot_ref, n_ref, library_ref, wide, band, spread, row, line,
        stacked, product, total, packed, section, sems, load_sems,
    ):
        def block(n):
            return pl.ds(n * slices, slices)

        pairs = [(x_hbm.at[:, pl.ds(b * T, T)], wide.at[block(b + 2)]) for b in range(per)]
        pairs += [(n_hbm, n_ref)]
        early = len(pairs)
        pairs += [(library_hbm, library_ref)]
        pairs += [(image_hbm.at[:, pl.ds(i * T, T)], stacked.at[block(i)]) for i in range(blocks)]
        late = len(pairs)
        pairs += [(entry_hbm, entry_ref), (place_hbm, place_ref), (slot_hbm, slot_ref)]
        fetches = [pltpu.make_async_copy(a, b, load_sems.at[n]) for n, (a, b) in enumerate(pairs)]
        for fetch in fetches:
            fetch.start()

        spread[...] = jnp.zeros_like(spread)
        row[...] = jnp.zeros_like(row)
        wide[block(0), :] = jnp.zeros((slices, T), BF16)
        wide[block(1), :] = l_ref[...]
        wide[block(per + 2), :] = r_ref[...]
        wide[block(per + 3), :] = jnp.zeros((slices, T), BF16)
        line[...] = jnp.zeros_like(line)
        line[0:1, : taps_ref.shape[1]] = taps_ref[...].astype(F32)
        spun = pltpu.roll(jnp.broadcast_to(line[0:1, :], (T, 3 * T)), T // 2, 1, stride=1, stride_axis=0)
        band[...] = spun.astype(BF16)
        for fetch in fetches[:early]:
            fetch.wait()
        filtered = sum(
            lax.dot_general(
                wide[n * slices : (n + per + 2) * slices, :],
                band[:, n * T : (n + 1) * T],
                NT,
                preferred_element_type=F32,
            )
            for n in range(3)
        ).astype(BF16)

        def put(at, value):
            spread[pl.ds(at, slices, stride=SECTION), :] = value.astype(F32)

        for b in range(per):
            value = filtered[(b + 1) * slices : (b + 2) * slices]
            phase_ref[:, b * T : (b + 1) * T] = value
            put(b, value)
        put(per, filtered[:slices])
        put(per + 1, filtered[(per + 1) * slices :])
        row[0:1, :owners] = n_ref[...].astype(F32)
        put(per + 2, jnp.broadcast_to(row[0:1, :], (slices, T)))
        section[...] = spread[...].astype(BF16).reshape(slices, SECTION, T)
        copies = [pltpu.make_async_copy(section, send_ref.at[:, pl.ds(slices, SECTION), :], sems.at[parts])]
        copies[0].start()

        total[...] = jnp.zeros_like(total)
        for fetch in fetches[early:late]:
            fetch.wait()
        for e in range(0, entries, 2):
            product[:, e * T : (e + 2) * T] = lax.dot_general(
                stacked[...], library_ref[e : e + 2].reshape(2 * T, T), NT, preferred_element_type=F32
            )
        for fetch in fetches[late:]:
            fetch.wait()

        def add(k):
            live = k < count_ref[0, 0]
            e = jnp.where(live, entry_ref[0, k], 0)
            i = jnp.where(live, place_ref[0, k], 0)
            s = jnp.where(live, slot_ref[0, k], owners)
            total[s] += product[pl.ds(pl.multiple_of(i * slices, slices), slices), lanes(e)]

        def group(g, carry):
            for u in range(8):
                add(g * 8 + u)
            return carry

        lax.fori_loop(0, (count_ref[0, 0] + 7) // 8, group, 0)
        step = owners // parts
        for n in range(parts):
            packed[n * step : (n + 1) * step] = total[n * step : (n + 1) * step].astype(BF16)
            here = pl.ds(n * step, step)
            copies.append(
                pltpu.make_async_copy(packed.at[here], send_ref.at[here, pl.ds(0, slices), :], sems.at[n])
            )
            copies[-1].start()
        for copy in copies:
            copy.wait()

    return pl.pallas_call(
        kernel,
        out_shape=[
            jax.ShapeDtypeStruct((slices, columns), BF16),
            pltpu.HBM((owners, rows, T), BF16),
        ],
        in_specs=[HBM] * 3 + [SMEM] + [HBM] * 2 + [VMEM] * 3 + [HBM] * 2,
        out_specs=[VMEM, HBM],
        scratch_shapes=[
            pltpu.SMEM(entry.shape, jnp.int32),
            pltpu.SMEM(place.shape, jnp.int32),
            pltpu.SMEM(slot.shape, jnp.int32),
            pltpu.VMEM(numbers.shape, jnp.int32),
            pltpu.VMEM(library.shape, BF16),
            pltpu.VMEM(((per + 4) * slices, T), BF16),
            pltpu.VMEM((T, 3 * T), BF16),
            pltpu.VMEM((slices * SECTION, T), F32),
            pltpu.VMEM((8, T), F32),
            pltpu.VMEM((8, 3 * T), F32),
            pltpu.VMEM((blocks * slices, T), BF16),
            pltpu.VMEM((blocks * slices, entries * T), F32),
            pltpu.VMEM((owners + 1, slices, T), F32),
            pltpu.VMEM((owners, slices, T), BF16),
            pltpu.VMEM((slices, SECTION, T), BF16),
            pltpu.SemaphoreType.DMA((parts + 1,)),
            pltpu.SemaphoreType.DMA((loads,)),
        ],
        compiler_params=params(),
        cost_estimate=pl.CostEstimate(
            flops=2 * capacity * slices * T * T, bytes_accessed=8 * 2**20, transcendentals=0
        ),
        name="filter_and_forward",
    )(*map(in_hbm, (entry, place, slot)), count, *map(in_hbm, (numbers, projections)), left, right, taps,
      *map(in_hbm, (image, library)))


def stripe_of(quarter, quarters, arrived_ref, offset, values, rimmed):
    angles = arrived_ref.shape[0]
    values[...] = arrived_ref[:, offset:, :].astype(F32)
    network = middle_network(angles)

    def middle(g, carry):
        rows = pl.ds(pl.multiple_of(g * 8, 8), 8)
        v = [values[a, rows, :] for a in range(angles)]
        for a, b, low, high in network:
            x, y = v[a], v[b]
            if low:
                v[a] = jnp.minimum(x, y)
            if high:
                v[b] = jnp.maximum(x, y)
        rimmed[pl.ds(g * 8 + 1, 8), :] = (v[angles // 2 - 1] + v[angles // 2]) * 0.5
        return carry

    lax.fori_loop(0, 3, middle, 0)
    before, after = rimmed[17:18, :], rimmed[18:19, :]
    rimmed[0:1, :] = jnp.where(quarter == 0, jnp.zeros_like(before), before)
    rimmed[17:18, :] = jnp.where(quarter == quarters - 1, jnp.zeros_like(after), after)
    prev, cur, nxt = rimmed[0:16, :], rimmed[1:17, :], rimmed[2:18, :]
    lane = lax.broadcasted_iota(jnp.int32, (16, T), 1)
    total = cur
    for o in range(1, SMOOTH + 1):
        total += pltpu.roll(jnp.where(lane < o, nxt, cur), T - o, 1)
        total += pltpu.roll(jnp.where(lane >= T - o, prev, cur), o, 1)
    place = quarter * (16 * T) + lax.broadcasted_iota(jnp.int32, (16, T), 0) * T + lane
    last = quarters * 16 * T - 1
    count = jnp.minimum(place + SMOOTH, last) - jnp.maximum(place - SMOOTH, 0) + 1
    return cur - total / count.astype(F32)


def back_call(carried, quarter, arrived, phase, quarters):
    owners = arrived.shape[0]
    size, columns = phase.shape
    rows = size + 16
    parts = 4

    def kernel(
        c_ref, q_ref, arrived_ref, phase_ref, forward_hbm, send_ref, values, rimmed, forward, less, packed, sems
    ):
        forward[...] = jnp.zeros_like(forward)
        for d in range(owners):
            forward[:, lanes(c_ref[0, d])] += arrived_ref[d, :size, :].astype(F32)
        copies = [pltpu.make_async_copy(forward, forward_hbm, sems.at[parts])]
        copies[0].start()
        stripe = stripe_of(q_ref[0], quarters, arrived_ref, size, values, rimmed).astype(BF16)
        less[...] = (phase_ref[...].astype(F32) - forward[...]).astype(BF16)
        step = owners // parts
        for n in range(parts):
            for d in range(n * step, (n + 1) * step):
                packed[d, :size, :] = less[:, lanes(c_ref[0, d])]
                packed[d, size:, :] = stripe
            here = pl.ds(n * step, step)
            copies.append(pltpu.make_async_copy(packed.at[here], send_ref.at[here], sems.at[n]))
            copies[-1].start()
        for copy in copies:
            copy.wait()

    return pl.pallas_call(
        kernel,
        out_shape=[
            pltpu.HBM((size, columns), F32),
            pltpu.HBM((owners, rows, T), BF16),
        ],
        in_specs=[SMEM, SMEM, VMEM, VMEM],
        out_specs=[HBM, HBM],
        scratch_shapes=[
            pltpu.VMEM((owners, SECTION, T), F32),
            pltpu.VMEM((32, T), F32),
            pltpu.VMEM((size, columns), F32),
            pltpu.VMEM((size, columns), BF16),
            pltpu.VMEM((owners, rows, T), BF16),
            pltpu.SemaphoreType.DMA((parts + 1,)),
        ],
        compiler_params=params(),
        cost_estimate=pl.CostEstimate(flops=2**24, bytes_accessed=8 * 2**20, transcendentals=0),
        name="sum_and_stripe",
    )(carried, quarter, arrived, phase)


def counts_call(entry, place, slot, count, owner, arrived, entries, blocks):
    capacity = entry.shape[1]
    owners = arrived.shape[0]
    size = arrived.shape[1] - SECTION

    def kernel(
        entry_hbm, place_hbm, slot_hbm, count_ref, owner_ref, arrived_ref,
        weights_ref, entry_ref, place_ref, slot_ref, loads,
    ):
        pairs = [(entry_hbm, entry_ref), (place_hbm, place_ref), (slot_hbm, slot_ref)]
        fetches = [pltpu.make_async_copy(a, b, loads.at[n]) for n, (a, b) in enumerate(pairs)]
        for fetch in fetches:
            fetch.start()
        lane = lax.broadcasted_iota(jnp.int32, (owners, T), 1)
        numbers = arrived_ref[:, size + 16 :, :].astype(F32)[:, 2, :]
        theirs = jnp.sum(jnp.where(lane == owner_ref[0], numbers, 0.0), axis=1, keepdims=True)
        carries = (theirs.astype(jnp.int32) + owners == lane).astype(F32).astype(BF16)

        def ones(rows, match):
            return (lax.broadcasted_iota(jnp.int32, (rows, match.shape[1]), 0) == match).astype(F32).astype(BF16)

        for fetch in fetches:
            fetch.wait()
        live = lax.broadcasted_iota(jnp.int32, (1, capacity), 1) < count_ref[0, 0]
        of_bin = ones(entries * blocks, jnp.where(live, entry_ref[...] * blocks + place_ref[...], -1))
        of_slot = ones(T, slot_ref[...])
        met = lax.dot_general(of_bin, of_slot, NT, preferred_element_type=F32)
        stripe_met = jnp.dot(met[:, :owners].astype(BF16), carries, preferred_element_type=F32)
        weights_ref[...] = (met - stripe_met).astype(BF16)

    return pl.pallas_call(
        kernel,
        out_shape=jax.ShapeDtypeStruct((entries * blocks, T), BF16),
        in_specs=[HBM] * 3 + [SMEM, SMEM, VMEM],
        out_specs=VMEM,
        scratch_shapes=[
            pltpu.VMEM(entry.shape, jnp.int32),
            pltpu.VMEM(place.shape, jnp.int32),
            pltpu.VMEM(slot.shape, jnp.int32),
            pltpu.SemaphoreType.DMA((3,)),
        ],
        compiler_params=params(),
        cost_estimate=pl.CostEstimate(flops=2**24, bytes_accessed=2**20, transcendentals=0),
        name="tile_counts",
    )(*map(in_hbm, (entry, place, slot)), count, owner, arrived)


def adjoint_call(quarter, weights, returned, library, blocks, quarters):
    entries = library.shape[0]
    owners = returned.shape[0]
    per = 16
    size = returned.shape[1] - per
    held = blocks // quarters

    def kernel(q_ref, weights_ref, returned_ref, library_hbm, *refs):
        outs, (stripe_ref, library_ref, stripes, terms, bins, whole, load) = refs[:quarters], refs[quarters:]
        fetch = pltpu.make_async_copy(library_hbm, library_ref, load)
        fetch.start()
        stripes[...] = returned_ref[:, size:, :].astype(F32).reshape(owners * per, T)
        terms[...] = returned_ref[:, :size, :].astype(F32).reshape(owners * size, T)
        weights = weights_ref[:, : owners + per]

        def both(n):
            here = terms[pl.ds(n, owners, stride=size), :].astype(BF16)
            return jnp.concatenate([here, returned_ref[n, size:, :]], axis=0)

        for n in range(0, size, 2):
            made = jnp.dot(
                weights, jnp.concatenate([both(n), both(n + 1)], axis=1), preferred_element_type=F32
            ).astype(BF16)
            for u in range(2):
                for e in range(entries):
                    bins[(n + u) * blocks : (n + u + 1) * blocks, e * T : (e + 1) * T] = made[
                        e * blocks : (e + 1) * blocks, u * T : (u + 1) * T
                    ]
        fetch.wait()
        whole[...] = jnp.dot(bins[...], library_ref[...].reshape(entries * T, T), preferred_element_type=F32)
        for m, out_ref in enumerate(outs):
            start = lax.rem(q_ref[0] + m, quarters) * held
            for t in range(held):
                out_ref[t] = whole[pl.ds(start + t, size, stride=blocks), :].astype(out_ref.dtype)
        for b in range(per):
            stripe_ref[b] = stripes[pl.ds(b, size, stride=per), :]

    return pl.pallas_call(
        kernel,
        out_shape=[
            *(jax.ShapeDtypeStruct((held, size, T), BF16 if m else F32) for m in range(quarters)),
            jax.ShapeDtypeStruct((per, size, T), F32),
        ],
        in_specs=[SMEM, VMEM, VMEM, HBM],
        out_specs=[VMEM] * (quarters + 1),
        scratch_shapes=[
            pltpu.VMEM(library.shape, BF16),
            pltpu.VMEM((owners * per, T), F32),
            pltpu.VMEM((owners * size, T), F32),
            pltpu.VMEM((size * blocks, entries * T), BF16),
            pltpu.VMEM((size * blocks, T), F32),
            pltpu.SemaphoreType.DMA,
        ],
        compiler_params=params(),
        cost_estimate=pl.CostEstimate(
            flops=2 * 256 * size * T * T, bytes_accessed=8 * 2**20, transcendentals=0
        ),
        name="adjoint_tiles",
    )(quarter, weights, returned, in_hbm(library))


def residual_call(phase, stripe, forward):
    per = stripe.shape[0]

    def kernel(phase_ref, stripe_ref, forward_ref, residual_ref):
        for b in range(per):
            where = slice(b * T, (b + 1) * T)
            corrected = (phase_ref[:, where].astype(F32) - stripe_ref[b]).astype(BF16)
            residual_ref[:, where] = (corrected.astype(F32) - forward_ref[:, where]).astype(BF16)

    return pl.pallas_call(
        kernel,
        out_shape=jax.ShapeDtypeStruct(phase.shape, BF16),
        in_specs=[VMEM] * 3,
        out_specs=VMEM,
        compiler_params=params(),
        cost_estimate=pl.CostEstimate(flops=2**19, bytes_accessed=2**21, transcendentals=0),
        name="residual",
    )(phase, stripe, forward)


def image_call(quarter, image, own, others):
    slices = image.shape[0]
    mine = own.shape[0]

    def kernel(q_ref, image_ref, own_ref, *refs):
        others_refs, out_ref = refs[:-1], refs[-1]
        for i in range(mine):
            total = own_ref[i]
            for ref in others_refs:
                total += ref[i].astype(F32)
            pixels = image_ref[:, lanes(q_ref[0] * mine + i)].astype(F32)
            out_ref[:, i * T : (i + 1) * T] = pixels + RELAX * total

    return pl.pallas_call(
        kernel,
        out_shape=jax.ShapeDtypeStruct((slices, mine * T), F32),
        in_specs=[SMEM, VMEM, VMEM] + [VMEM] * len(others),
        out_specs=VMEM,
        compiler_params=params(),
        cost_estimate=pl.CostEstimate(flops=2**18, bytes_accessed=2**20, transcendentals=0),
        name="image_step",
    )(quarter, image, own, *others)


def in_hbm(array):
    return pltpu.with_memory_space_constraint(array, pltpu.HBM)


def exchanged(array, axis):
    return lax.all_to_all(array, axis, split_axis=0, concat_axis=0, tiled=True)


def shards(projections, phase_kernel, image, tile_library, tile_entry, tile_image, tile_slot, tile_count, slot_block):
    projections = projections[0]
    library = tile_library[0, 0]
    image = image.T
    slices = projections.shape[0]
    quarters = lax.axis_size("ray")
    quarter = lax.axis_index("ray").astype(jnp.int32).reshape(1)
    tiles = (tile_entry[0], tile_image[0], tile_slot[0], tile_count)
    carried = slot_block[0]

    left = lax.ppermute(projections[:, -T:], "ray", [(i, i + 1) for i in range(quarters - 1)])
    right = lax.ppermute(projections[:, :T], "ray", [(i + 1, i) for i in range(quarters - 1)])
    taps = phase_kernel.reshape(1, -1)
    phase, send = first_call(*tiles, carried, projections, left, right, taps, image, library)
    arrived = exchanged(send, "dom")
    forward, back = back_call(carried, quarter, arrived, phase, quarters)
    owner = lax.axis_index("dom").astype(jnp.int32).reshape(1)
    blocks = image.shape[1] // T
    weights = counts_call(*tiles, owner, arrived, library.shape[0], blocks)
    returned = exchanged(back, "dom")
    own, *sent, stripe = adjoint_call(quarter, weights, returned, library, blocks, quarters)
    others = [
        lax.ppermute(part, "ray", [(i, (i + m) % quarters) for i in range(quarters)])
        for m, part in enumerate(sent, 1)
    ]
    residual = residual_call(phase, stripe, forward)
    image_next = image_call(quarter, image, own, others)
    return residual[None], image_next.T


def solution(mesh):
    return jax.shard_map(
        shards,
        mesh=mesh,
        in_specs=(
            P("dom", None, "ray"),
            P(),
            P("dom", None),
            P("dom", "ray", None, None, None),
            P("dom", "ray", None),
            P("dom", "ray", None),
            P("dom", "ray", None),
            P("dom", "ray"),
            P("dom", "ray", None),
        ),
        out_specs=(P("dom", None, "ray"), P(("dom", "ray"), None)),
        check_vma=False,
    )
```

```python
import jax
import jax.numpy as jnp
from jax import lax
from jax.experimental import pallas as pl
from jax.experimental.pallas import tpu as pltpu
from jax.sharding import PartitionSpec as P

T = 128
SMOOTH = 8
RELAX = 0.25
SECTION = 32
MIB = 2**20
F32, BF16 = jnp.float32, jnp.bfloat16
NT = (((1,), (1,)), ((), ()))
VMEM = pl.BlockSpec(memory_space=pltpu.VMEM)
SMEM = pl.BlockSpec(memory_space=pltpu.SMEM)
HBM = pl.BlockSpec(memory_space=pltpu.HBM)


def params(limit=32):
    return pltpu.CompilerParams(vmem_limit_bytes=limit * MIB)


def middle_network(n):
    pairs = []
    p = 1
    while p < n:
        k = p
        while k >= 1:
            for j in range(k % p, n - k, 2 * k):
                for i in range(min(k, n - j - k)):
                    if (i + j) // (2 * p) == (i + j + k) // (2 * p):
                        pairs.append((i + j, i + j + k))
            k //= 2
        p *= 2
    needed = {n // 2 - 1, n // 2}
    kept = []
    for a, b in reversed(pairs):
        if a in needed or b in needed:
            kept.append((a, b, a in needed, b in needed))
            needed |= {a, b}
    return kept[::-1]


def lanes(block):
    return pl.ds(pl.multiple_of(block * T, T), T)


def first_call(entry, place, slot, count, numbers, projections, left, right, taps, image, library):
    slices, columns = projections.shape
    entries, capacity = library.shape[0], entry.shape[1]
    blocks = image.shape[1] // T
    owners = slices
    per = columns // T
    rows = slices + SECTION
    parts = 4
    loads = per + blocks + 6

    def kernel(
        entry_hbm, place_hbm, slot_hbm, count_ref, n_hbm, x_hbm, l_ref, r_ref, taps_hbm, image_hbm, library_hbm,
        phase_ref, send_ref, entry_ref, place_ref, slot_ref, n_ref, taps_ref, library_ref, wide, band, spread, row, line,
        stacked, product, total, packed, section, sems, load_sems,
    ):
        def block(n):
            return pl.ds(n * slices, slices)

        pairs = [(x_hbm.at[:, pl.ds(b * T, T)], wide.at[block(b + 2)]) for b in range(per)]
        pairs += [(n_hbm, n_ref), (taps_hbm, taps_ref)]
        early = len(pairs)
        pairs += [(library_hbm, library_ref)]
        pairs += [(image_hbm.at[:, pl.ds(i * T, T)], stacked.at[block(i)]) for i in range(blocks)]
        late = len(pairs)
        pairs += [(entry_hbm, entry_ref), (place_hbm, place_ref), (slot_hbm, slot_ref)]
        fetches = [pltpu.make_async_copy(a, b, load_sems.at[n]) for n, (a, b) in enumerate(pairs)]
        for fetch in fetches:
            fetch.start()

        spread[...] = jnp.zeros_like(spread)
        row[...] = jnp.zeros_like(row)
        wide[block(0), :] = jnp.zeros((slices, T), BF16)
        wide[block(1), :] = l_ref[...]
        wide[block(per + 2), :] = r_ref[...]
        wide[block(per + 3), :] = jnp.zeros((slices, T), BF16)
        for fetch in fetches[:early]:
            fetch.wait()
        line[...] = jnp.zeros_like(line)
        line[0:1, : taps_ref.shape[0]] = taps_ref[...].astype(F32).reshape(1, -1)
        spun = pltpu.roll(jnp.broadcast_to(line[0:1, :], (T, 3 * T)), T // 2, 1, stride=1, stride_axis=0)
        band[...] = spun.astype(BF16)
        filtered = sum(
            lax.dot_general(
                wide[n * slices : (n + per + 2) * slices, :],
                band[:, n * T : (n + 1) * T],
                NT,
                preferred_element_type=F32,
            )
            for n in range(3)
        ).astype(BF16)

        def put(at, value):
            spread[pl.ds(at, slices, stride=SECTION), :] = value.astype(F32)

        for b in range(per):
            value = filtered[(b + 1) * slices : (b + 2) * slices]
            phase_ref[:, b * T : (b + 1) * T] = value
            put(b, value)
        put(per, filtered[:slices])
        put(per + 1, filtered[(per + 1) * slices :])
        row[0:1, :owners] = n_ref[...].astype(F32)
        put(per + 2, jnp.broadcast_to(row[0:1, :], (slices, T)))
        section[...] = spread[...].astype(BF16).reshape(slices, SECTION, T)
        copies = [pltpu.make_async_copy(section, send_ref.at[:, pl.ds(slices, SECTION), :], sems.at[parts])]
        copies[0].start()

        total[...] = jnp.zeros_like(total)
        for fetch in fetches[early:late]:
            fetch.wait()
        for e in range(0, entries, 2):
            product[:, e * T : (e + 2) * T] = lax.dot_general(
                stacked[...], library_ref[e : e + 2].reshape(2 * T, T), NT, preferred_element_type=F32
            )
        for fetch in fetches[late:]:
            fetch.wait()

        def add(k):
            live = k < count_ref[0, 0]
            e = jnp.where(live, entry_ref[0, k], 0)
            i = jnp.where(live, place_ref[0, k], 0)
            s = jnp.where(live, slot_ref[0, k], owners)
            total[s] += product[pl.ds(pl.multiple_of(i * slices, slices), slices), lanes(e)]

        def group(g, carry):
            for u in range(8):
                add(g * 8 + u)
            return carry

        lax.fori_loop(0, (count_ref[0, 0] + 7) // 8, group, 0)
        step = owners // parts
        for n in range(parts):
            packed[n * step : (n + 1) * step] = total[n * step : (n + 1) * step].astype(BF16)
            here = pl.ds(n * step, step)
            copies.append(
                pltpu.make_async_copy(packed.at[here], send_ref.at[here, pl.ds(0, slices), :], sems.at[n])
            )
            copies[-1].start()
        for copy in copies:
            copy.wait()

    return pl.pallas_call(
        kernel,
        out_shape=[
            jax.ShapeDtypeStruct((slices, columns), BF16),
            pltpu.HBM((owners, rows, T), BF16),
        ],
        in_specs=[HBM] * 3 + [SMEM] + [HBM] * 2 + [VMEM] * 2 + [HBM] * 3,
        out_specs=[VMEM, HBM],
        scratch_shapes=[
            pltpu.SMEM(entry.shape, jnp.int32),
            pltpu.SMEM(place.shape, jnp.int32),
            pltpu.SMEM(slot.shape, jnp.int32),
            pltpu.VMEM(numbers.shape, jnp.int32),
            pltpu.VMEM(taps.shape, BF16),
            pltpu.VMEM(library.shape, BF16),
            pltpu.VMEM(((per + 4) * slices, T), BF16),
            pltpu.VMEM((T, 3 * T), BF16),
            pltpu.VMEM((slices * SECTION, T), F32),
            pltpu.VMEM((8, T), F32),
            pltpu.VMEM((8, 3 * T), F32),
            pltpu.VMEM((blocks * slices, T), BF16),
            pltpu.VMEM((blocks * slices, entries * T), F32),
            pltpu.VMEM((owners + 1, slices, T), F32),
            pltpu.VMEM((owners, slices, T), BF16),
            pltpu.VMEM((slices, SECTION, T), BF16),
            pltpu.SemaphoreType.DMA((parts + 1,)),
            pltpu.SemaphoreType.DMA((loads,)),
        ],
        compiler_params=params(),
        cost_estimate=pl.CostEstimate(
            flops=2 * capacity * slices * T * T, bytes_accessed=8 * 2**20, transcendentals=0
        ),
        name="filter_and_forward",
    )(*map(in_hbm, (entry, place, slot)), count, *map(in_hbm, (numbers, projections)), left, right,
      *map(in_hbm, (taps, image, library)))


def stripe_of(quarter, quarters, arrived_ref, offset, values, rimmed):
    angles = arrived_ref.shape[0]
    values[...] = arrived_ref[:, offset:, :].astype(F32)
    network = middle_network(angles)

    def middle(g, carry):
        rows = pl.ds(pl.multiple_of(g * 8, 8), 8)
        v = [values[a, rows, :] for a in range(angles)]
        for a, b, low, high in network:
            x, y = v[a], v[b]
            if low:
                v[a] = jnp.minimum(x, y)
            if high:
                v[b] = jnp.maximum(x, y)
        rimmed[pl.ds(g * 8 + 1, 8), :] = (v[angles // 2 - 1] + v[angles // 2]) * 0.5
        return carry

    lax.fori_loop(0, 3, middle, 0)
    before, after = rimmed[17:18, :], rimmed[18:19, :]
    rimmed[0:1, :] = jnp.where(quarter == 0, jnp.zeros_like(before), before)
    rimmed[17:18, :] = jnp.where(quarter == quarters - 1, jnp.zeros_like(after), after)
    prev, cur, nxt = rimmed[0:16, :], rimmed[1:17, :], rimmed[2:18, :]
    lane = lax.broadcasted_iota(jnp.int32, (16, T), 1)
    total = cur
    for o in range(1, SMOOTH + 1):
        total += pltpu.roll(jnp.where(lane < o, nxt, cur), T - o, 1)
        total += pltpu.roll(jnp.where(lane >= T - o, prev, cur), o, 1)
    place = quarter * (16 * T) + lax.broadcasted_iota(jnp.int32, (16, T), 0) * T + lane
    last = quarters * 16 * T - 1
    count = jnp.minimum(place + SMOOTH, last) - jnp.maximum(place - SMOOTH, 0) + 1
    return cur - total / count.astype(F32)


def back_call(carried, quarter, arrived, phase, quarters):
    owners = arrived.shape[0]
    size, columns = phase.shape
    rows = size + 16
    parts = 4

    def kernel(
        c_ref, q_ref, arrived_ref, phase_ref, forward_hbm, send_ref, values, rimmed, forward, less, packed, repeated,
        sems,
    ):
        forward[...] = jnp.zeros_like(forward)
        for d in range(owners):
            forward[:, lanes(c_ref[0, d])] += arrived_ref[d, :size, :].astype(F32)
        copies = [pltpu.make_async_copy(forward, forward_hbm, sems.at[parts])]
        copies[0].start()
        less[...] = (phase_ref[...].astype(F32) - forward[...]).astype(BF16)
        step = owners // parts
        for n in range(parts):
            for d in range(n * step, (n + 1) * step):
                packed[d] = less[:, lanes(c_ref[0, d])]
            here = pl.ds(n * step, step)
            copies.append(pltpu.make_async_copy(packed.at[here], send_ref.at[here, pl.ds(0, size), :], sems.at[n]))
            copies[-1].start()
        stripe = stripe_of(q_ref[0], quarters, arrived_ref, size, values, rimmed).astype(BF16)
        repeated[...] = jnp.broadcast_to(stripe[None], repeated.shape)
        copies.append(pltpu.make_async_copy(repeated, send_ref.at[:, pl.ds(size, 16), :], sems.at[parts + 1]))
        copies[-1].start()
        for copy in copies:
            copy.wait()

    return pl.pallas_call(
        kernel,
        out_shape=[
            pltpu.HBM((size, columns), F32),
            pltpu.HBM((owners, rows, T), BF16),
        ],
        in_specs=[SMEM, SMEM, VMEM, VMEM],
        out_specs=[HBM, HBM],
        scratch_shapes=[
            pltpu.VMEM((owners, SECTION, T), F32),
            pltpu.VMEM((32, T), F32),
            pltpu.VMEM((size, columns), F32),
            pltpu.VMEM((size, columns), BF16),
            pltpu.VMEM((owners, size, T), BF16),
            pltpu.VMEM((owners, 16, T), BF16),
            pltpu.SemaphoreType.DMA((parts + 2,)),
        ],
        compiler_params=params(),
        cost_estimate=pl.CostEstimate(flops=2**24, bytes_accessed=8 * 2**20, transcendentals=0),
        name="sum_and_stripe",
    )(carried, quarter, arrived, phase)


def counts_call(entry, place, slot, count, owner, arrived, entries, blocks):
    capacity = entry.shape[1]
    owners = arrived.shape[0]
    size = arrived.shape[1] - SECTION

    def kernel(
        entry_hbm, place_hbm, slot_hbm, count_ref, owner_ref, arrived_ref,
        weights_ref, entry_ref, place_ref, slot_ref, loads,
    ):
        pairs = [(entry_hbm, entry_ref), (place_hbm, place_ref), (slot_hbm, slot_ref)]
        fetches = [pltpu.make_async_copy(a, b, loads.at[n]) for n, (a, b) in enumerate(pairs)]
        for fetch in fetches:
            fetch.start()
        lane = lax.broadcasted_iota(jnp.int32, (owners, T), 1)
        numbers = arrived_ref[:, size + 16 :, :].astype(F32)[:, 2, :]
        theirs = jnp.sum(jnp.where(lane == owner_ref[0], numbers, 0.0), axis=1, keepdims=True)
        carries = (theirs.astype(jnp.int32) + owners == lane).astype(F32).astype(BF16)

        def ones(rows, match):
            return (lax.broadcasted_iota(jnp.int32, (rows, match.shape[1]), 0) == match).astype(F32).astype(BF16)

        for fetch in fetches:
            fetch.wait()
        live = lax.broadcasted_iota(jnp.int32, (1, capacity), 1) < count_ref[0, 0]
        of_bin = ones(entries * blocks, jnp.where(live, entry_ref[...] * blocks + place_ref[...], -1))
        of_slot = ones(T, slot_ref[...])
        met = lax.dot_general(of_bin, of_slot, NT, preferred_element_type=F32)
        stripe_met = jnp.dot(met[:, :owners].astype(BF16), carries, preferred_element_type=F32)
        weights_ref[...] = (met - stripe_met).astype(BF16)

    return pl.pallas_call(
        kernel,
        out_shape=jax.ShapeDtypeStruct((entries * blocks, T), BF16),
        in_specs=[HBM] * 3 + [SMEM, SMEM, VMEM],
        out_specs=VMEM,
        scratch_shapes=[
            pltpu.VMEM(entry.shape, jnp.int32),
            pltpu.VMEM(place.shape, jnp.int32),
            pltpu.VMEM(slot.shape, jnp.int32),
            pltpu.SemaphoreType.DMA((3,)),
        ],
        compiler_params=params(),
        cost_estimate=pl.CostEstimate(flops=2**24, bytes_accessed=2**20, transcendentals=0),
        name="tile_counts",
    )(*map(in_hbm, (entry, place, slot)), count, owner, arrived)


def adjoint_call(quarter, weights, returned, library, blocks, quarters):
    entries = library.shape[0]
    owners = returned.shape[0]
    per = 16
    size = returned.shape[1] - per
    held = blocks // quarters

    def kernel(q_ref, weights_ref, returned_ref, library_hbm, *refs):
        outs, (stripe_ref, library_ref, stripes, terms, bins, whole, load) = refs[:quarters], refs[quarters:]
        fetch = pltpu.make_async_copy(library_hbm, library_ref, load)
        fetch.start()
        stripes[...] = returned_ref[:, size:, :].astype(F32).reshape(owners * per, T)
        terms[...] = returned_ref[:, :size, :].astype(F32).reshape(owners * size, T)
        weights = weights_ref[:, : owners + per]

        def both(n):
            here = terms[pl.ds(n, owners, stride=size), :].astype(BF16)
            return jnp.concatenate([here, returned_ref[n, size:, :]], axis=0)

        for n in range(0, size, 2):
            made = jnp.dot(
                weights, jnp.concatenate([both(n), both(n + 1)], axis=1), preferred_element_type=F32
            ).astype(BF16)
            for u in range(2):
                for e in range(entries):
                    bins[(n + u) * blocks : (n + u + 1) * blocks, e * T : (e + 1) * T] = made[
                        e * blocks : (e + 1) * blocks, u * T : (u + 1) * T
                    ]
        fetch.wait()
        whole[...] = jnp.dot(bins[...], library_ref[...].reshape(entries * T, T), preferred_element_type=F32)
        for m, out_ref in enumerate(outs):
            start = lax.rem(q_ref[0] + m, quarters) * held
            for t in range(held):
                out_ref[t] = whole[pl.ds(start + t, size, stride=blocks), :].astype(out_ref.dtype)
        for b in range(per):
            stripe_ref[b] = stripes[pl.ds(b, size, stride=per), :]

    return pl.pallas_call(
        kernel,
        out_shape=[
            *(jax.ShapeDtypeStruct((held, size, T), BF16 if m else F32) for m in range(quarters)),
            jax.ShapeDtypeStruct((per, size, T), F32),
        ],
        in_specs=[SMEM, VMEM, VMEM, HBM],
        out_specs=[VMEM] * (quarters + 1),
        scratch_shapes=[
            pltpu.VMEM(library.shape, BF16),
            pltpu.VMEM((owners * per, T), F32),
            pltpu.VMEM((owners * size, T), F32),
            pltpu.VMEM((size * blocks, entries * T), BF16),
            pltpu.VMEM((size * blocks, T), F32),
            pltpu.SemaphoreType.DMA,
        ],
        compiler_params=params(),
        cost_estimate=pl.CostEstimate(
            flops=2 * 256 * size * T * T, bytes_accessed=8 * 2**20, transcendentals=0
        ),
        name="adjoint_tiles",
    )(quarter, weights, returned, in_hbm(library))


def residual_call(phase, stripe, forward):
    per = stripe.shape[0]

    def kernel(phase_ref, stripe_ref, forward_ref, residual_ref):
        for b in range(per):
            where = slice(b * T, (b + 1) * T)
            corrected = (phase_ref[:, where].astype(F32) - stripe_ref[b]).astype(BF16)
            residual_ref[:, where] = (corrected.astype(F32) - forward_ref[:, where]).astype(BF16)

    return pl.pallas_call(
        kernel,
        out_shape=jax.ShapeDtypeStruct(phase.shape, BF16),
        in_specs=[VMEM] * 3,
        out_specs=VMEM,
        compiler_params=params(),
        cost_estimate=pl.CostEstimate(flops=2**19, bytes_accessed=2**21, transcendentals=0),
        name="residual",
    )(phase, stripe, forward)


def image_call(quarter, image, own, others):
    slices = image.shape[0]
    mine = own.shape[0]

    def kernel(q_ref, image_ref, own_ref, *refs):
        others_refs, out_ref = refs[:-1], refs[-1]
        for i in range(mine):
            total = own_ref[i]
            for ref in others_refs:
                total += ref[i].astype(F32)
            pixels = image_ref[:, lanes(q_ref[0] * mine + i)].astype(F32)
            out_ref[:, i * T : (i + 1) * T] = pixels + RELAX * total

    return pl.pallas_call(
        kernel,
        out_shape=jax.ShapeDtypeStruct((slices, mine * T), F32),
        in_specs=[SMEM, VMEM, VMEM] + [VMEM] * len(others),
        out_specs=VMEM,
        compiler_params=params(),
        cost_estimate=pl.CostEstimate(flops=2**18, bytes_accessed=2**20, transcendentals=0),
        name="image_step",
    )(quarter, image, own, *others)


def in_hbm(array):
    return pltpu.with_memory_space_constraint(array, pltpu.HBM)


def exchanged(array, axis):
    return lax.all_to_all(array, axis, split_axis=0, concat_axis=0, tiled=True)


def shards(projections, phase_kernel, image, tile_library, tile_entry, tile_image, tile_slot, tile_count, slot_block):
    projections = projections[0]
    library = tile_library[0, 0]
    image = image.T
    slices = projections.shape[0]
    quarters = lax.axis_size("ray")
    quarter = lax.axis_index("ray").astype(jnp.int32).reshape(1)
    tiles = (tile_entry[0], tile_image[0], tile_slot[0], tile_count)
    carried = slot_block[0]

    left = lax.ppermute(projections[:, -T:], "ray", [(i, i + 1) for i in range(quarters - 1)])
    right = lax.ppermute(projections[:, :T], "ray", [(i + 1, i) for i in range(quarters - 1)])
    taps = phase_kernel
    phase, send = first_call(*tiles, carried, projections, left, right, taps, image, library)
    arrived = exchanged(send, "dom")
    forward, back = back_call(carried, quarter, arrived, phase, quarters)
    owner = lax.axis_index("dom").astype(jnp.int32).reshape(1)
    blocks = image.shape[1] // T
    weights = counts_call(*tiles, owner, arrived, library.shape[0], blocks)
    returned = exchanged(back, "dom")
    own, *sent, stripe = adjoint_call(quarter, weights, returned, library, blocks, quarters)
    others = [
        lax.ppermute(part, "ray", [(i, (i + m) % quarters) for i in range(quarters)])
        for m, part in enumerate(sent, 1)
    ]
    residual = residual_call(phase, stripe, forward)
    image_next = image_call(quarter, image, own, others)
    return residual[None], image_next.T


def solution(mesh):
    return jax.shard_map(
        shards,
        mesh=mesh,
        in_specs=(
            P("dom", None, "ray"),
            P(),
            P("dom", None),
            P("dom", "ray", None, None, None),
            P("dom", "ray", None),
            P("dom", "ray", None),
            P("dom", "ray", None),
            P("dom", "ray"),
            P("dom", "ray", None),
        ),
        out_specs=(P("dom", None, "ray"), P(("dom", "ray"), None)),
        check_vma=False,
    )
```

```python
import jax
import jax.numpy as jnp
from jax import lax
from jax.experimental import pallas as pl
from jax.experimental.pallas import tpu as pltpu
from jax.sharding import PartitionSpec as P

T = 128
SMOOTH = 8
RELAX = 0.25
PER = 16
ROOM = 32
MIB = 2**20
F32, BF16 = jnp.float32, jnp.bfloat16
NT = (((1,), (1,)), ((), ()))
VMEM = pl.BlockSpec(memory_space=pltpu.VMEM)
SMEM = pl.BlockSpec(memory_space=pltpu.SMEM)
HBM = pl.BlockSpec(memory_space=pltpu.HBM)


def params(limit=32):
    return pltpu.CompilerParams(vmem_limit_bytes=limit * MIB)


def middle_network(n):
    pairs = []
    p = 1
    while p < n:
        k = p
        while k >= 1:
            for j in range(k % p, n - k, 2 * k):
                for i in range(min(k, n - j - k)):
                    if (i + j) // (2 * p) == (i + j + k) // (2 * p):
                        pairs.append((i + j, i + j + k))
            k //= 2
        p *= 2
    needed = {n // 2 - 1, n // 2}
    kept = []
    for a, b in reversed(pairs):
        if a in needed or b in needed:
            kept.append((a, b, a in needed, b in needed))
            needed |= {a, b}
    return kept[::-1]


def lanes(block):
    return pl.ds(pl.multiple_of(block * T, T), T)


def first_call(entry, place, slot, count, numbers, projections, image, library):
    slices, columns = projections.shape
    entries, capacity = library.shape[0], entry.shape[1]
    blocks = image.shape[1] // T
    owners = slices
    rows = slices + PER
    parts = 4
    loads = blocks + 6

    def kernel(
        entry_hbm, place_hbm, slot_hbm, count_ref, n_hbm, x_hbm, image_hbm, library_hbm,
        send_ref, head_ref, tail_ref, row_ref, entry_ref, place_ref, slot_ref, n_ref, library_ref, x_ref, spread,
        stacked, product, total, packed, section, sems, load_sems,
    ):
        pairs = [(x_hbm, x_ref), (n_hbm, n_ref), (library_hbm, library_ref)]
        pairs += [
            (image_hbm.at[:, pl.ds(i * T, T)], stacked.at[pl.ds(i * slices, slices)]) for i in range(blocks)
        ]
        pairs += [(entry_hbm, entry_ref), (place_hbm, place_ref), (slot_hbm, slot_ref)]
        fetches = [pltpu.make_async_copy(a, b, load_sems.at[n]) for n, (a, b) in enumerate(pairs)]
        for fetch in fetches:
            fetch.start()
        total[...] = jnp.zeros_like(total)
        row_ref[...] = jnp.zeros_like(row_ref)
        for fetch in fetches[:2]:
            fetch.wait()
        head_ref[...] = x_ref[:, :T]
        tail_ref[...] = x_ref[:, columns - T :]
        row_ref[0:1, :owners] = n_ref[...]
        for b in range(PER):
            spread[pl.ds(b, slices, stride=PER), :] = x_ref[:, b * T : (b + 1) * T].astype(F32)
        section[...] = spread[...].astype(BF16).reshape(slices, PER, T)
        copies = [pltpu.make_async_copy(section, send_ref.at[:, pl.ds(slices, PER), :], sems.at[parts])]
        copies[0].start()
        for fetch in fetches[2:]:
            fetch.wait()
        for e in range(0, entries, 2):
            product[:, e * T : (e + 2) * T] = lax.dot_general(
                stacked[...], library_ref[e : e + 2].reshape(2 * T, T), NT, preferred_element_type=F32
            )

        def add(k):
            live = k < count_ref[0, 0]
            e = jnp.where(live, entry_ref[0, k], 0)
            i = jnp.where(live, place_ref[0, k], 0)
            s = jnp.where(live, slot_ref[0, k], owners)
            total[s] += product[pl.ds(pl.multiple_of(i * slices, slices), slices), lanes(e)]

        def group(g, carry):
            for u in range(8):
                add(g * 8 + u)
            return carry

        lax.fori_loop(0, (count_ref[0, 0] + 7) // 8, group, 0)
        step = owners // parts
        for n in range(parts):
            packed[n * step : (n + 1) * step] = total[n * step : (n + 1) * step].astype(BF16)
            here = pl.ds(n * step, step)
            copies.append(
                pltpu.make_async_copy(packed.at[here], send_ref.at[here, pl.ds(0, slices), :], sems.at[n])
            )
            copies[-1].start()
        for copy in copies:
            copy.wait()

    return pl.pallas_call(
        kernel,
        out_shape=[
            pltpu.HBM((owners, rows, T), BF16),
            jax.ShapeDtypeStruct((slices, T), BF16),
            jax.ShapeDtypeStruct((slices, T), BF16),
            jax.ShapeDtypeStruct((8, T), jnp.int32),
        ],
        in_specs=[HBM] * 3 + [SMEM] + [HBM] * 4,
        out_specs=[HBM] + [VMEM] * 3,
        scratch_shapes=[
            pltpu.SMEM(entry.shape, jnp.int32),
            pltpu.SMEM(place.shape, jnp.int32),
            pltpu.SMEM(slot.shape, jnp.int32),
            pltpu.VMEM(numbers.shape, jnp.int32),
            pltpu.VMEM(library.shape, BF16),
            pltpu.VMEM((slices, columns), BF16),
            pltpu.VMEM((slices * PER, T), F32),
            pltpu.VMEM((blocks * slices, T), BF16),
            pltpu.VMEM((blocks * slices, entries * T), F32),
            pltpu.VMEM((owners + 1, slices, T), F32),
            pltpu.VMEM((owners, slices, T), BF16),
            pltpu.VMEM((slices, PER, T), BF16),
            pltpu.SemaphoreType.DMA((parts + 1,)),
            pltpu.SemaphoreType.DMA((loads,)),
        ],
        compiler_params=params(),
        cost_estimate=pl.CostEstimate(
            flops=2 * capacity * slices * T * T, bytes_accessed=8 * 2**20, transcendentals=0
        ),
        name="forward_tiles",
    )(*map(in_hbm, (entry, place, slot)), count, *map(in_hbm, (numbers, projections, image, library)))


def phase_call(projections, left, right, taps):
    slices, columns = projections.shape
    per = columns // T

    def kernel(x_hbm, l_ref, r_ref, taps_hbm, phase_ref, band_ref, taps_ref, line, wide, sems):
        fetches = [
            pltpu.make_async_copy(x_hbm, wide.at[:, pl.ds(T, columns)], sems.at[0]),
            pltpu.make_async_copy(taps_hbm, taps_ref, sems.at[1]),
        ]
        for fetch in fetches:
            fetch.start()
        wide[:, :T] = l_ref[...]
        wide[:, T + columns :] = r_ref[...]
        line[...] = jnp.zeros_like(line)
        for fetch in fetches:
            fetch.wait()
        line[0:1, : taps_ref.shape[0]] = taps_ref[...].astype(F32).reshape(1, -1)
        spun = pltpu.roll(jnp.broadcast_to(line[0:1, :], (T, 3 * T)), T // 2, 1, stride=1, stride_axis=0)
        band_ref[...] = spun.astype(BF16)
        for b in range(per):
            phase_ref[:, b * T : (b + 1) * T] = lax.dot_general(
                wide[:, b * T : (b + 3) * T], band_ref[...], NT, preferred_element_type=F32
            ).astype(BF16)

    return pl.pallas_call(
        kernel,
        out_shape=[
            jax.ShapeDtypeStruct((slices, columns), BF16),
            jax.ShapeDtypeStruct((T, 3 * T), BF16),
        ],
        in_specs=[HBM, VMEM, VMEM, HBM],
        out_specs=[VMEM, VMEM],
        scratch_shapes=[
            pltpu.VMEM(taps.shape, BF16),
            pltpu.VMEM((8, 3 * T), F32),
            pltpu.VMEM((slices, columns + 2 * T), BF16),
            pltpu.SemaphoreType.DMA((2,)),
        ],
        compiler_params=params(),
        cost_estimate=pl.CostEstimate(flops=2**26, bytes_accessed=2**20, transcendentals=0),
        name="phase_filter",
    )(in_hbm(projections), left, right, in_hbm(taps))


def rim_call(arrived, band, rows_by_z):
    angles = arrived.shape[0]
    size = arrived.shape[1] - PER

    def kernel(arrived_ref, _, *refs):
        n = len(rows_by_z)
        z_refs, (head_ref, tail_ref, stack_ref, flat) = refs[:n], refs[n:]
        for m, ref in enumerate(z_refs):
            stack_ref[m : m + 1, :] = ref[0:1, :]
        flat[...] = arrived_ref[:, size:, :].astype(F32).reshape(angles * PER, T)
        head_ref[...] = flat[pl.ds(0, angles, stride=PER), :].astype(BF16)
        tail_ref[...] = flat[pl.ds(PER - 1, angles, stride=PER), :].astype(BF16)

    return pl.pallas_call(
        kernel,
        out_shape=[jax.ShapeDtypeStruct((angles, T), BF16)] * 2 + [jax.ShapeDtypeStruct((8, T), jnp.int32)],
        in_specs=[VMEM, HBM] + [VMEM] * len(rows_by_z),
        out_specs=[VMEM] * 3,
        scratch_shapes=[pltpu.VMEM((angles * PER, T), F32)],
        compiler_params=params(),
        cost_estimate=pl.CostEstimate(flops=2**17, bytes_accessed=2**18, transcendentals=0),
        name="rim",
    )(arrived, band, *rows_by_z)


def stripe_of(quarter, quarters, angles, values, rimmed):
    network = middle_network(angles)

    def middle(g, carry):
        v = [values[pl.ds(pl.multiple_of(a * ROOM + g * 8, 8), 8), :] for a in range(angles)]
        for a, b, low, high in network:
            x, y = v[a], v[b]
            if low:
                v[a] = jnp.minimum(x, y)
            if high:
                v[b] = jnp.maximum(x, y)
        rimmed[pl.ds(g * 8 + 1, 8), :] = (v[angles // 2 - 1] + v[angles // 2]) * 0.5
        return carry

    lax.fori_loop(0, 3, middle, 0)
    before, after = rimmed[17:18, :], rimmed[18:19, :]
    rimmed[0:1, :] = jnp.where(quarter == 0, jnp.zeros_like(before), before)
    rimmed[17:18, :] = jnp.where(quarter == quarters - 1, jnp.zeros_like(after), after)
    prev, cur, nxt = rimmed[0:16, :], rimmed[1:17, :], rimmed[2:18, :]
    lane = lax.broadcasted_iota(jnp.int32, (16, T), 1)
    total = cur
    for o in range(1, SMOOTH + 1):
        total += pltpu.roll(jnp.where(lane < o, nxt, cur), T - o, 1)
        total += pltpu.roll(jnp.where(lane >= T - o, prev, cur), o, 1)
    place = quarter * (16 * T) + lax.broadcasted_iota(jnp.int32, (16, T), 0) * T + lane
    last = quarters * 16 * T - 1
    count = jnp.minimum(place + SMOOTH, last) - jnp.maximum(place - SMOOTH, 0) + 1
    return cur - total / count.astype(F32)


def back_call(carried, arrived, phase, stacked):
    owners = arrived.shape[0]
    size, columns = phase.shape
    rows = size + PER
    parts = 4

    def kernel(
        c_ref, arrived_ref, phase_ref, stacked_ref, forward_hbm, send_ref, stack_ref, forward, less, packed, sems
    ):
        forward[...] = jnp.zeros_like(forward)
        for d in range(owners):
            forward[:, lanes(c_ref[0, d])] += arrived_ref[d, :size, :].astype(F32)
        copies = [pltpu.make_async_copy(forward, forward_hbm, sems.at[parts])]
        copies[0].start()
        less[...] = (phase_ref[...].astype(F32) - forward[...]).astype(BF16)
        step = owners // parts
        for n in range(parts):
            for d in range(n * step, (n + 1) * step):
                packed[d] = less[:, lanes(c_ref[0, d])]
            here = pl.ds(n * step, step)
            copies.append(pltpu.make_async_copy(packed.at[here], send_ref.at[here, pl.ds(0, size), :], sems.at[n]))
            copies[-1].start()
        stack_ref[...] = stacked_ref[...]
        for copy in copies:
            copy.wait()

    return pl.pallas_call(
        kernel,
        out_shape=[
            pltpu.HBM((size, columns), F32),
            pltpu.HBM((owners, rows, T), BF16),
            jax.ShapeDtypeStruct((8, T), jnp.int32),
        ],
        in_specs=[SMEM] + [VMEM] * 3,
        out_specs=[HBM, HBM, VMEM],
        scratch_shapes=[
            pltpu.VMEM((size, columns), F32),
            pltpu.VMEM((size, columns), BF16),
            pltpu.VMEM((owners, size, T), BF16),
            pltpu.SemaphoreType.DMA((parts + 1,)),
        ],
        compiler_params=params(),
        cost_estimate=pl.CostEstimate(flops=2**24, bytes_accessed=8 * 2**20, transcendentals=0),
        name="slot_sums",
    )(carried, arrived, phase, stacked)


def stripe_call(quarter, arrived, left, right, band, back, quarters):
    angles = arrived.shape[0]
    size = arrived.shape[1] - PER

    def kernel(
        q_ref, arrived_ref, l_ref, r_ref, band_ref, _, back_ref, flat, wide, values, rimmed, repeated, sem
    ):
        def block(n):
            return pl.ds(n * angles, angles)

        flat[...] = arrived_ref[:, size:, :].astype(F32).reshape(angles * PER, T)
        for b in range(PER):
            wide[block(b + 2), :] = flat[pl.ds(b, angles, stride=PER), :].astype(BF16)
        wide[block(0), :] = jnp.zeros((angles, T), BF16)
        wide[block(1), :] = l_ref[...]
        wide[block(PER + 2), :] = r_ref[...]
        wide[block(PER + 3), :] = jnp.zeros((angles, T), BF16)
        values[...] = jnp.zeros_like(values)
        filtered = sum(
            lax.dot_general(
                wide[n * angles : (n + PER + 2) * angles, :],
                band_ref[:, n * T : (n + 1) * T],
                NT,
                preferred_element_type=F32,
            )
            for n in range(3)
        ).astype(BF16)
        for at, b in enumerate([*range(1, PER + 1), 0, PER + 1]):
            values[pl.ds(at, angles, stride=ROOM), :] = filtered[b * angles : (b + 1) * angles].astype(F32)
        stripe = stripe_of(q_ref[0], quarters, angles, values, rimmed).astype(BF16)
        repeated[...] = jnp.broadcast_to(stripe[None], repeated.shape)
        copy = pltpu.make_async_copy(repeated, back_ref.at[:, pl.ds(size, PER), :], sem)
        copy.start()
        copy.wait()

    return pl.pallas_call(
        kernel,
        out_shape=pltpu.HBM(back.shape, BF16),
        in_specs=[SMEM] + [VMEM] * 4 + [HBM],
        out_specs=HBM,
        scratch_shapes=[
            pltpu.VMEM((angles * PER, T), F32),
            pltpu.VMEM(((PER + 4) * angles, T), BF16),
            pltpu.VMEM((angles * ROOM, T), F32),
            pltpu.VMEM((32, T), F32),
            pltpu.VMEM((angles, PER, T), BF16),
            pltpu.SemaphoreType.DMA,
        ],
        input_output_aliases={5: 0},
        compiler_params=params(),
        cost_estimate=pl.CostEstimate(flops=2**26, bytes_accessed=2**20, transcendentals=0),
        name="stripe",
    )(quarter, arrived, left, right, band, in_hbm(back))


def counts_call(entry, place, slot, count, owner, stacks, owners, entries, blocks):
    capacity = entry.shape[1]

    def kernel(
        entry_hbm, place_hbm, slot_hbm, count_ref, owner_ref, *refs
    ):
        n = len(stacks)
        stack_refs, (weights_ref, entry_ref, place_ref, slot_ref, loads) = refs[:n], refs[n:]
        pairs = [(entry_hbm, entry_ref), (place_hbm, place_ref), (slot_hbm, slot_ref)]
        fetches = [pltpu.make_async_copy(a, b, loads.at[n]) for n, (a, b) in enumerate(pairs)]
        for fetch in fetches:
            fetch.start()
        lane = lax.broadcasted_iota(jnp.int32, (owners, T), 1)
        numbers = jnp.concatenate([ref[...] for ref in stack_refs], axis=0).astype(F32)
        theirs = jnp.sum(jnp.where(lane == owner_ref[0], numbers, 0.0), axis=1, keepdims=True)
        carries = (theirs.astype(jnp.int32) + owners == lane).astype(F32).astype(BF16)

        def ones(rows, match):
            return (lax.broadcasted_iota(jnp.int32, (rows, match.shape[1]), 0) == match).astype(F32).astype(BF16)

        for fetch in fetches:
            fetch.wait()
        live = lax.broadcasted_iota(jnp.int32, (1, capacity), 1) < count_ref[0, 0]
        of_bin = ones(entries * blocks, jnp.where(live, entry_ref[...] * blocks + place_ref[...], -1))
        of_slot = ones(T, slot_ref[...])
        met = lax.dot_general(of_bin, of_slot, NT, preferred_element_type=F32)
        k = lax.broadcasted_iota(jnp.int32, (owners, capacity), 0)
        by_row = (owner_ref[0] ^ ((k & 7) * 8 + (k >> 3))) == slot_ref[...]
        met_by_row = lax.dot_general(of_bin, by_row.astype(F32).astype(BF16), NT, preferred_element_type=F32)
        stripe_met = jnp.dot(met_by_row.astype(BF16), carries, preferred_element_type=F32)
        weights_ref[...] = (met - stripe_met).astype(BF16)

    return pl.pallas_call(
        kernel,
        out_shape=jax.ShapeDtypeStruct((entries * blocks, T), BF16),
        in_specs=[HBM] * 3 + [SMEM, SMEM] + [VMEM] * len(stacks),
        out_specs=VMEM,
        scratch_shapes=[
            pltpu.VMEM(entry.shape, jnp.int32),
            pltpu.VMEM(place.shape, jnp.int32),
            pltpu.VMEM(slot.shape, jnp.int32),
            pltpu.SemaphoreType.DMA((3,)),
        ],
        compiler_params=params(),
        cost_estimate=pl.CostEstimate(flops=2**24, bytes_accessed=2**20, transcendentals=0),
        name="tile_counts",
    )(*map(in_hbm, (entry, place, slot)), count, owner, *stacks)


def adjoint_call(quarter, weights, returned, library, blocks, quarters):
    entries = library.shape[0]
    owners = returned.shape[0]
    per = 16
    size = returned.shape[1] - per
    held = blocks // quarters

    def kernel(q_ref, weights_ref, returned_ref, library_hbm, *refs):
        outs, (stripe_ref, library_ref, stripes, terms, bins, whole, load) = refs[:quarters], refs[quarters:]
        fetch = pltpu.make_async_copy(library_hbm, library_ref, load)
        fetch.start()
        stripes[...] = returned_ref[:, size:, :].astype(F32).reshape(owners * per, T)
        terms[...] = returned_ref[:, :size, :].astype(F32).reshape(owners * size, T)
        weights = weights_ref[:, : owners + per]

        def both(n):
            here = terms[pl.ds(n, owners, stride=size), :].astype(BF16)
            return jnp.concatenate([here, returned_ref[n, size:, :]], axis=0)

        for n in range(0, size, 2):
            made = jnp.dot(
                weights, jnp.concatenate([both(n), both(n + 1)], axis=1), preferred_element_type=F32
            ).astype(BF16)
            for u in range(2):
                for e in range(entries):
                    bins[(n + u) * blocks : (n + u + 1) * blocks, e * T : (e + 1) * T] = made[
                        e * blocks : (e + 1) * blocks, u * T : (u + 1) * T
                    ]
        fetch.wait()
        whole[...] = jnp.dot(bins[...], library_ref[...].reshape(entries * T, T), preferred_element_type=F32)
        for m, out_ref in enumerate(outs):
            start = lax.rem(q_ref[0] + m, quarters) * held
            for t in range(held):
                out_ref[t] = whole[pl.ds(start + t, size, stride=blocks), :].astype(out_ref.dtype)
        for b in range(per):
            stripe_ref[b] = stripes[pl.ds(b, size, stride=per), :]

    return pl.pallas_call(
        kernel,
        out_shape=[
            *(jax.ShapeDtypeStruct((held, size, T), BF16 if m else F32) for m in range(quarters)),
            jax.ShapeDtypeStruct((per, size, T), F32),
        ],
        in_specs=[SMEM, VMEM, VMEM, HBM],
        out_specs=[VMEM] * (quarters + 1),
        scratch_shapes=[
            pltpu.VMEM(library.shape, BF16),
            pltpu.VMEM((owners * per, T), F32),
            pltpu.VMEM((owners * size, T), F32),
            pltpu.VMEM((size * blocks, entries * T), BF16),
            pltpu.VMEM((size * blocks, T), F32),
            pltpu.SemaphoreType.DMA,
        ],
        compiler_params=params(),
        cost_estimate=pl.CostEstimate(
            flops=2 * 256 * size * T * T, bytes_accessed=8 * 2**20, transcendentals=0
        ),
        name="adjoint_tiles",
    )(quarter, weights, returned, in_hbm(library))


def residual_call(phase, stripe, forward):
    per = stripe.shape[0]

    def kernel(phase_ref, stripe_ref, forward_ref, residual_ref):
        for b in range(per):
            where = slice(b * T, (b + 1) * T)
            corrected = (phase_ref[:, where].astype(F32) - stripe_ref[b]).astype(BF16)
            residual_ref[:, where] = (corrected.astype(F32) - forward_ref[:, where]).astype(BF16)

    return pl.pallas_call(
        kernel,
        out_shape=jax.ShapeDtypeStruct(phase.shape, BF16),
        in_specs=[VMEM] * 3,
        out_specs=VMEM,
        compiler_params=params(),
        cost_estimate=pl.CostEstimate(flops=2**19, bytes_accessed=2**21, transcendentals=0),
        name="residual",
    )(phase, stripe, forward)


def image_call(quarter, image, own, others):
    slices = image.shape[0]
    mine = own.shape[0]

    def kernel(q_ref, image_ref, own_ref, *refs):
        others_refs, out_ref = refs[:-1], refs[-1]
        for i in range(mine):
            total = own_ref[i]
            for ref in others_refs:
                total += ref[i].astype(F32)
            pixels = image_ref[:, lanes(q_ref[0] * mine + i)].astype(F32)
            out_ref[:, i * T : (i + 1) * T] = pixels + RELAX * total

    return pl.pallas_call(
        kernel,
        out_shape=jax.ShapeDtypeStruct((slices, mine * T), F32),
        in_specs=[SMEM, VMEM, VMEM] + [VMEM] * len(others),
        out_specs=VMEM,
        compiler_params=params(),
        cost_estimate=pl.CostEstimate(flops=2**18, bytes_accessed=2**20, transcendentals=0),
        name="image_step",
    )(quarter, image, own, *others)


def in_hbm(array):
    return pltpu.with_memory_space_constraint(array, pltpu.HBM)


def exchanged(array, axis):
    return lax.all_to_all(array, axis, split_axis=0, concat_axis=0, tiled=True)


def shards(projections, phase_kernel, image, tile_library, tile_entry, tile_image, tile_slot, tile_count, slot_block):
    projections = projections[0]
    library = tile_library[0, 0]
    image = image.T
    slices = projections.shape[0]
    quarters = lax.axis_size("ray")
    quarter = lax.axis_index("ray").astype(jnp.int32).reshape(1)
    tiles = (tile_entry[0], tile_image[0], tile_slot[0], tile_count)
    carried = slot_block[0]

    owners = lax.axis_size("dom")
    owner = lax.axis_index("dom").astype(jnp.int32).reshape(1)
    blocks = image.shape[1] // T

    def rims(head, tail):
        left = lax.ppermute(tail, "ray", [(i, i + 1) for i in range(quarters - 1)])
        right = lax.ppermute(head, "ray", [(i + 1, i) for i in range(quarters - 1)])
        return left, right

    def swapped(array, m):
        return lax.ppermute(array, "dom", [(i, i ^ m) for i in range(owners)])

    send, head, tail, row = first_call(*tiles, carried, projections, image, library)
    arrived = exchanged(send, "dom")
    phase, band = phase_call(projections, *rims(head, tail), phase_kernel)
    rows_by_z = [row] + [swapped(row, m * 8) for m in range(1, 8)]
    head, tail, stacked = rim_call(arrived, band, rows_by_z)
    left, right = rims(head, tail)
    forward, back, stack = back_call(carried, arrived, phase, stacked)
    back = stripe_call(quarter, arrived, left, right, band, back, quarters)
    returned = exchanged(back, "dom")
    stacks = [stack] + [swapped(stack, m) for m in range(1, 8)]
    weights = counts_call(*tiles, owner, stacks, owners, library.shape[0], blocks)
    own, *sent, stripe = adjoint_call(quarter, weights, returned, library, blocks, quarters)
    others = [
        lax.ppermute(part, "ray", [(i, (i + m) % quarters) for i in range(quarters)])
        for m, part in enumerate(sent, 1)
    ]
    residual = residual_call(phase, stripe, forward)
    image_next = image_call(quarter, image, own, others)
    return residual[None], image_next.T


def solution(mesh):
    return jax.shard_map(
        shards,
        mesh=mesh,
        in_specs=(
            P("dom", None, "ray"),
            P(),
            P("dom", None),
            P("dom", "ray", None, None, None),
            P("dom", "ray", None),
            P("dom", "ray", None),
            P("dom", "ray", None),
            P("dom", "ray"),
            P("dom", "ray", None),
        ),
        out_specs=(P("dom", None, "ray"), P(("dom", "ray"), None)),
        check_vma=False,
    )
```

```python
import jax
import jax.numpy as jnp
from jax import lax
from jax.experimental import pallas as pl
from jax.experimental.pallas import tpu as pltpu
from jax.sharding import PartitionSpec as P

T = 128
SMOOTH = 8
RELAX = 0.25
PER = 16
ROOM = 32
EARLY = 4
MIB = 2**20
F32, BF16 = jnp.float32, jnp.bfloat16
NT = (((1,), (1,)), ((), ()))
VMEM = pl.BlockSpec(memory_space=pltpu.VMEM)
SMEM = pl.BlockSpec(memory_space=pltpu.SMEM)
HBM = pl.BlockSpec(memory_space=pltpu.HBM)


def params(limit=32):
    return pltpu.CompilerParams(vmem_limit_bytes=limit * MIB)


def middle_network(n):
    pairs = []
    p = 1
    while p < n:
        k = p
        while k >= 1:
            for j in range(k % p, n - k, 2 * k):
                for i in range(min(k, n - j - k)):
                    if (i + j) // (2 * p) == (i + j + k) // (2 * p):
                        pairs.append((i + j, i + j + k))
            k //= 2
        p *= 2
    needed = {n // 2 - 1, n // 2}
    kept = []
    for a, b in reversed(pairs):
        if a in needed or b in needed:
            kept.append((a, b, a in needed, b in needed))
            needed |= {a, b}
    return kept[::-1]


def lanes(block):
    return pl.ds(pl.multiple_of(block * T, T), T)


def first_call(entry, place, slot, count, numbers, projections, image, library):
    slices, columns = projections.shape
    entries, capacity = library.shape[0], entry.shape[1]
    blocks = image.shape[1] // T
    owners = slices
    rows = slices + PER
    parts = 4
    loads = blocks + 6

    def kernel(
        entry_hbm, place_hbm, slot_hbm, count_ref, n_hbm, x_hbm, image_hbm, library_hbm,
        send_ref, head_ref, tail_ref, row_ref, entry_ref, place_ref, slot_ref, n_ref, library_ref, x_ref, spread,
        stacked, product, total, packed, section, sems, load_sems,
    ):
        pairs = [(x_hbm, x_ref), (n_hbm, n_ref), (library_hbm, library_ref)]
        pairs += [
            (image_hbm.at[:, pl.ds(i * T, T)], stacked.at[pl.ds(i * slices, slices)]) for i in range(blocks)
        ]
        pairs += [(entry_hbm, entry_ref), (place_hbm, place_ref), (slot_hbm, slot_ref)]
        fetches = [pltpu.make_async_copy(a, b, load_sems.at[n]) for n, (a, b) in enumerate(pairs)]
        for fetch in fetches:
            fetch.start()
        total[...] = jnp.zeros_like(total)
        row_ref[...] = jnp.zeros_like(row_ref)
        for fetch in fetches[:2]:
            fetch.wait()
        head_ref[...] = x_ref[:, :T]
        tail_ref[...] = x_ref[:, columns - T :]
        row_ref[0:1, :owners] = n_ref[...]
        for b in range(PER):
            spread[pl.ds(b, slices, stride=PER), :] = x_ref[:, b * T : (b + 1) * T].astype(F32)
        section[...] = spread[...].astype(BF16).reshape(slices, PER, T)
        copies = [pltpu.make_async_copy(section, send_ref.at[:, pl.ds(slices, PER), :], sems.at[parts])]
        copies[0].start()
        for fetch in fetches[2:]:
            fetch.wait()
        for e in range(0, entries, 2):
            product[:, e * T : (e + 2) * T] = lax.dot_general(
                stacked[...], library_ref[e : e + 2].reshape(2 * T, T), NT, preferred_element_type=F32
            )

        def add(k):
            live = k < count_ref[0, 0]
            e = jnp.where(live, entry_ref[0, k], 0)
            i = jnp.where(live, place_ref[0, k], 0)
            s = jnp.where(live, slot_ref[0, k], owners)
            total[s] += product[pl.ds(pl.multiple_of(i * slices, slices), slices), lanes(e)]

        def group(g, carry):
            for u in range(8):
                add(g * 8 + u)
            return carry

        lax.fori_loop(0, (count_ref[0, 0] + 7) // 8, group, 0)
        step = owners // parts
        for n in range(parts):
            packed[n * step : (n + 1) * step] = total[n * step : (n + 1) * step].astype(BF16)
            here = pl.ds(n * step, step)
            copies.append(
                pltpu.make_async_copy(packed.at[here], send_ref.at[here, pl.ds(0, slices), :], sems.at[n])
            )
            copies[-1].start()
        for copy in copies:
            copy.wait()

    return pl.pallas_call(
        kernel,
        out_shape=[
            pltpu.HBM((owners, rows, T), BF16),
            jax.ShapeDtypeStruct((slices, T), BF16),
            jax.ShapeDtypeStruct((slices, T), BF16),
            jax.ShapeDtypeStruct((8, T), jnp.int32),
        ],
        in_specs=[HBM] * 3 + [SMEM] + [HBM] * 4,
        out_specs=[HBM] + [VMEM] * 3,
        scratch_shapes=[
            pltpu.SMEM(entry.shape, jnp.int32),
            pltpu.SMEM(place.shape, jnp.int32),
            pltpu.SMEM(slot.shape, jnp.int32),
            pltpu.VMEM(numbers.shape, jnp.int32),
            pltpu.VMEM(library.shape, BF16),
            pltpu.VMEM((slices, columns), BF16),
            pltpu.VMEM((slices * PER, T), F32),
            pltpu.VMEM((blocks * slices, T), BF16),
            pltpu.VMEM((blocks * slices, entries * T), F32),
            pltpu.VMEM((owners + 1, slices, T), F32),
            pltpu.VMEM((owners, slices, T), BF16),
            pltpu.VMEM((slices, PER, T), BF16),
            pltpu.SemaphoreType.DMA((parts + 1,)),
            pltpu.SemaphoreType.DMA((loads,)),
        ],
        compiler_params=params(),
        cost_estimate=pl.CostEstimate(
            flops=2 * capacity * slices * T * T, bytes_accessed=8 * 2**20, transcendentals=0
        ),
        name="forward_tiles",
    )(*map(in_hbm, (entry, place, slot)), count, *map(in_hbm, (numbers, projections, image, library)))


def phase_call(projections, left, right, taps, rows):
    slices, columns = projections.shape
    per = columns // T

    def kernel(x_hbm, l_ref, r_ref, taps_hbm, *refs):
        n = len(rows)
        row_refs, (phase_ref, band_ref, stack_ref, taps_ref, line, wide, sems) = refs[:n], refs[n:]
        for m, ref in enumerate(row_refs):
            stack_ref[m : m + 1, :] = ref[0:1, :]
        fetches = [
            pltpu.make_async_copy(x_hbm, wide.at[:, pl.ds(T, columns)], sems.at[0]),
            pltpu.make_async_copy(taps_hbm, taps_ref, sems.at[1]),
        ]
        for fetch in fetches:
            fetch.start()
        wide[:, :T] = l_ref[...]
        wide[:, T + columns :] = r_ref[...]
        line[...] = jnp.zeros_like(line)
        for fetch in fetches:
            fetch.wait()
        line[0:1, : taps_ref.shape[0]] = taps_ref[...].astype(F32).reshape(1, -1)
        spun = pltpu.roll(jnp.broadcast_to(line[0:1, :], (T, 3 * T)), T // 2, 1, stride=1, stride_axis=0)
        band_ref[...] = spun.astype(BF16)
        for b in range(per):
            phase_ref[:, b * T : (b + 1) * T] = lax.dot_general(
                wide[:, b * T : (b + 3) * T], band_ref[...], NT, preferred_element_type=F32
            ).astype(BF16)

    return pl.pallas_call(
        kernel,
        out_shape=[
            jax.ShapeDtypeStruct((slices, columns), BF16),
            jax.ShapeDtypeStruct((T, 3 * T), BF16),
            jax.ShapeDtypeStruct((8, T), jnp.int32),
        ],
        in_specs=[HBM, VMEM, VMEM, HBM] + [VMEM] * len(rows),
        out_specs=[VMEM] * 3,
        scratch_shapes=[
            pltpu.VMEM(taps.shape, BF16),
            pltpu.VMEM((8, 3 * T), F32),
            pltpu.VMEM((slices, columns + 2 * T), BF16),
            pltpu.SemaphoreType.DMA((2,)),
        ],
        compiler_params=params(),
        cost_estimate=pl.CostEstimate(flops=2**26, bytes_accessed=2**20, transcendentals=0),
        name="phase_filter",
    )(in_hbm(projections), left, right, in_hbm(taps), *rows)


def rim_call(arrived, band, stacks):
    angles = arrived.shape[0]
    size = arrived.shape[1] - PER

    def kernel(arrived_ref, _, *refs):
        n = len(stacks)
        stack_refs, (head_ref, tail_ref, near_ref, flat) = refs[:n], refs[n:]
        for m, ref in enumerate(stack_refs):
            near_ref[m * 8 : (m + 1) * 8, :] = ref[...]
        flat[...] = arrived_ref[:, size:, :].astype(F32).reshape(angles * PER, T)
        head_ref[...] = flat[pl.ds(0, angles, stride=PER), :].astype(BF16)
        tail_ref[...] = flat[pl.ds(PER - 1, angles, stride=PER), :].astype(BF16)

    return pl.pallas_call(
        kernel,
        out_shape=[jax.ShapeDtypeStruct((angles, T), BF16)] * 2
        + [jax.ShapeDtypeStruct((8 * len(stacks), T), jnp.int32)],
        in_specs=[VMEM, HBM] + [VMEM] * len(stacks),
        out_specs=[VMEM] * 3,
        scratch_shapes=[pltpu.VMEM((angles * PER, T), F32)],
        compiler_params=params(),
        cost_estimate=pl.CostEstimate(flops=2**17, bytes_accessed=2**18, transcendentals=0),
        name="rim",
    )(arrived, band, *stacks)


def stripe_of(quarter, quarters, angles, values, rimmed):
    network = middle_network(angles)

    def middle(g, carry):
        v = [values[pl.ds(pl.multiple_of(a * ROOM + g * 8, 8), 8), :] for a in range(angles)]
        for a, b, low, high in network:
            x, y = v[a], v[b]
            if low:
                v[a] = jnp.minimum(x, y)
            if high:
                v[b] = jnp.maximum(x, y)
        rimmed[pl.ds(g * 8 + 1, 8), :] = (v[angles // 2 - 1] + v[angles // 2]) * 0.5
        return carry

    lax.fori_loop(0, 3, middle, 0)
    before, after = rimmed[17:18, :], rimmed[18:19, :]
    rimmed[0:1, :] = jnp.where(quarter == 0, jnp.zeros_like(before), before)
    rimmed[17:18, :] = jnp.where(quarter == quarters - 1, jnp.zeros_like(after), after)
    prev, cur, nxt = rimmed[0:16, :], rimmed[1:17, :], rimmed[2:18, :]
    lane = lax.broadcasted_iota(jnp.int32, (16, T), 1)
    total = cur
    for o in range(1, SMOOTH + 1):
        total += pltpu.roll(jnp.where(lane < o, nxt, cur), T - o, 1)
        total += pltpu.roll(jnp.where(lane >= T - o, prev, cur), o, 1)
    place = quarter * (16 * T) + lax.broadcasted_iota(jnp.int32, (16, T), 0) * T + lane
    last = quarters * 16 * T - 1
    count = jnp.minimum(place + SMOOTH, last) - jnp.maximum(place - SMOOTH, 0) + 1
    return cur - total / count.astype(F32)


def back_call(carried, arrived, phase, stacked):
    owners = arrived.shape[0]
    size, columns = phase.shape
    rows = size + PER
    parts = 4

    def kernel(
        c_ref, arrived_ref, phase_ref, stacked_ref, forward_hbm, send_ref, stack_ref, forward, less, packed, sems
    ):
        forward[...] = jnp.zeros_like(forward)
        for d in range(owners):
            forward[:, lanes(c_ref[0, d])] += arrived_ref[d, :size, :].astype(F32)
        copies = [pltpu.make_async_copy(forward, forward_hbm, sems.at[parts])]
        copies[0].start()
        less[...] = (phase_ref[...].astype(F32) - forward[...]).astype(BF16)
        step = owners // parts
        for n in range(parts):
            for d in range(n * step, (n + 1) * step):
                packed[d] = less[:, lanes(c_ref[0, d])]
            here = pl.ds(n * step, step)
            copies.append(pltpu.make_async_copy(packed.at[here], send_ref.at[here, pl.ds(0, size), :], sems.at[n]))
            copies[-1].start()
        stack_ref[...] = stacked_ref[...]
        for copy in copies:
            copy.wait()

    return pl.pallas_call(
        kernel,
        out_shape=[
            pltpu.HBM((size, columns), F32),
            pltpu.HBM((owners, rows, T), BF16),
            jax.ShapeDtypeStruct((8, T), jnp.int32),
        ],
        in_specs=[SMEM] + [VMEM] * 3,
        out_specs=[HBM, HBM, VMEM],
        scratch_shapes=[
            pltpu.VMEM((size, columns), F32),
            pltpu.VMEM((size, columns), BF16),
            pltpu.VMEM((owners, size, T), BF16),
            pltpu.SemaphoreType.DMA((parts + 1,)),
        ],
        compiler_params=params(),
        cost_estimate=pl.CostEstimate(flops=2**24, bytes_accessed=8 * 2**20, transcendentals=0),
        name="slot_sums",
    )(carried, arrived, phase, stacked)


def stripe_call(quarter, arrived, left, right, band, back, quarters):
    angles = arrived.shape[0]
    size = arrived.shape[1] - PER

    def kernel(
        q_ref, arrived_ref, l_ref, r_ref, band_ref, _, back_ref, flat, wide, values, rimmed, repeated, sem
    ):
        def block(n):
            return pl.ds(n * angles, angles)

        flat[...] = arrived_ref[:, size:, :].astype(F32).reshape(angles * PER, T)
        for b in range(PER):
            wide[block(b + 2), :] = flat[pl.ds(b, angles, stride=PER), :].astype(BF16)
        wide[block(0), :] = jnp.zeros((angles, T), BF16)
        wide[block(1), :] = l_ref[...]
        wide[block(PER + 2), :] = r_ref[...]
        wide[block(PER + 3), :] = jnp.zeros((angles, T), BF16)
        values[...] = jnp.zeros_like(values)
        filtered = sum(
            lax.dot_general(
                wide[n * angles : (n + PER + 2) * angles, :],
                band_ref[:, n * T : (n + 1) * T],
                NT,
                preferred_element_type=F32,
            )
            for n in range(3)
        ).astype(BF16)
        for at, b in enumerate([*range(1, PER + 1), 0, PER + 1]):
            values[pl.ds(at, angles, stride=ROOM), :] = filtered[b * angles : (b + 1) * angles].astype(F32)
        stripe = stripe_of(q_ref[0], quarters, angles, values, rimmed).astype(BF16)
        repeated[...] = jnp.broadcast_to(stripe[None], repeated.shape)
        copy = pltpu.make_async_copy(repeated, back_ref.at[:, pl.ds(size, PER), :], sem)
        copy.start()
        copy.wait()

    return pl.pallas_call(
        kernel,
        out_shape=pltpu.HBM(back.shape, BF16),
        in_specs=[SMEM] + [VMEM] * 4 + [HBM],
        out_specs=HBM,
        scratch_shapes=[
            pltpu.VMEM((angles * PER, T), F32),
            pltpu.VMEM(((PER + 4) * angles, T), BF16),
            pltpu.VMEM((angles * ROOM, T), F32),
            pltpu.VMEM((32, T), F32),
            pltpu.VMEM((angles, PER, T), BF16),
            pltpu.SemaphoreType.DMA,
        ],
        input_output_aliases={5: 0},
        compiler_params=params(),
        cost_estimate=pl.CostEstimate(flops=2**26, bytes_accessed=2**20, transcendentals=0),
        name="stripe",
    )(quarter, arrived, left, right, band, in_hbm(back))


def counts_call(entry, place, slot, count, owner, stacks, owners, entries, blocks):
    capacity = entry.shape[1]

    def kernel(
        entry_hbm, place_hbm, slot_hbm, count_ref, owner_ref, *refs
    ):
        n = len(stacks)
        stack_refs, (weights_ref, entry_ref, place_ref, slot_ref, loads) = refs[:n], refs[n:]
        pairs = [(entry_hbm, entry_ref), (place_hbm, place_ref), (slot_hbm, slot_ref)]
        fetches = [pltpu.make_async_copy(a, b, loads.at[n]) for n, (a, b) in enumerate(pairs)]
        for fetch in fetches:
            fetch.start()
        lane = lax.broadcasted_iota(jnp.int32, (owners, T), 1)
        numbers = jnp.concatenate([ref[...] for ref in stack_refs], axis=0).astype(F32)
        theirs = jnp.sum(jnp.where(lane == owner_ref[0], numbers, 0.0), axis=1, keepdims=True)
        carries = (theirs.astype(jnp.int32) + owners == lane).astype(F32).astype(BF16)

        def ones(rows, match):
            return (lax.broadcasted_iota(jnp.int32, (rows, match.shape[1]), 0) == match).astype(F32).astype(BF16)

        for fetch in fetches:
            fetch.wait()
        live = lax.broadcasted_iota(jnp.int32, (1, capacity), 1) < count_ref[0, 0]
        of_bin = ones(entries * blocks, jnp.where(live, entry_ref[...] * blocks + place_ref[...], -1))
        of_slot = ones(T, slot_ref[...])
        met = lax.dot_general(of_bin, of_slot, NT, preferred_element_type=F32)
        k = lax.broadcasted_iota(jnp.int32, (owners, capacity), 0)
        by_row = (owner_ref[0] ^ k) == slot_ref[...]
        met_by_row = lax.dot_general(of_bin, by_row.astype(F32).astype(BF16), NT, preferred_element_type=F32)
        stripe_met = jnp.dot(met_by_row.astype(BF16), carries, preferred_element_type=F32)
        weights_ref[...] = (met - stripe_met).astype(BF16)

    return pl.pallas_call(
        kernel,
        out_shape=jax.ShapeDtypeStruct((entries * blocks, T), BF16),
        in_specs=[HBM] * 3 + [SMEM, SMEM] + [VMEM] * len(stacks),
        out_specs=VMEM,
        scratch_shapes=[
            pltpu.VMEM(entry.shape, jnp.int32),
            pltpu.VMEM(place.shape, jnp.int32),
            pltpu.VMEM(slot.shape, jnp.int32),
            pltpu.SemaphoreType.DMA((3,)),
        ],
        compiler_params=params(),
        cost_estimate=pl.CostEstimate(flops=2**24, bytes_accessed=2**20, transcendentals=0),
        name="tile_counts",
    )(*map(in_hbm, (entry, place, slot)), count, owner, *stacks)


def adjoint_call(quarter, weights, returned, library, blocks, quarters):
    entries = library.shape[0]
    owners = returned.shape[0]
    per = 16
    size = returned.shape[1] - per
    held = blocks // quarters

    def kernel(q_ref, weights_ref, returned_ref, library_hbm, *refs):
        outs, (stripe_ref, library_ref, stripes, terms, bins, whole, load) = refs[:quarters], refs[quarters:]
        fetch = pltpu.make_async_copy(library_hbm, library_ref, load)
        fetch.start()
        stripes[...] = returned_ref[:, size:, :].astype(F32).reshape(owners * per, T)
        terms[...] = returned_ref[:, :size, :].astype(F32).reshape(owners * size, T)
        weights = weights_ref[:, : owners + per]

        def both(n):
            here = terms[pl.ds(n, owners, stride=size), :].astype(BF16)
            return jnp.concatenate([here, returned_ref[n, size:, :]], axis=0)

        for n in range(0, size, 2):
            made = jnp.dot(
                weights, jnp.concatenate([both(n), both(n + 1)], axis=1), preferred_element_type=F32
            ).astype(BF16)
            for u in range(2):
                for e in range(entries):
                    bins[(n + u) * blocks : (n + u + 1) * blocks, e * T : (e + 1) * T] = made[
                        e * blocks : (e + 1) * blocks, u * T : (u + 1) * T
                    ]
        fetch.wait()
        whole[...] = jnp.dot(bins[...], library_ref[...].reshape(entries * T, T), preferred_element_type=F32)
        for m, out_ref in enumerate(outs):
            start = lax.rem(q_ref[0] + m, quarters) * held
            for t in range(held):
                out_ref[t] = whole[pl.ds(start + t, size, stride=blocks), :].astype(out_ref.dtype)
        for b in range(per):
            stripe_ref[b] = stripes[pl.ds(b, size, stride=per), :]

    return pl.pallas_call(
        kernel,
        out_shape=[
            *(jax.ShapeDtypeStruct((held, size, T), BF16 if m else F32) for m in range(quarters)),
            jax.ShapeDtypeStruct((per, size, T), F32),
        ],
        in_specs=[SMEM, VMEM, VMEM, HBM],
        out_specs=[VMEM] * (quarters + 1),
        scratch_shapes=[
            pltpu.VMEM(library.shape, BF16),
            pltpu.VMEM((owners * per, T), F32),
            pltpu.VMEM((owners * size, T), F32),
            pltpu.VMEM((size * blocks, entries * T), BF16),
            pltpu.VMEM((size * blocks, T), F32),
            pltpu.SemaphoreType.DMA,
        ],
        compiler_params=params(),
        cost_estimate=pl.CostEstimate(
            flops=2 * 256 * size * T * T, bytes_accessed=8 * 2**20, transcendentals=0
        ),
        name="adjoint_tiles",
    )(quarter, weights, returned, in_hbm(library))


def residual_call(phase, stripe, forward):
    per = stripe.shape[0]

    def kernel(phase_ref, stripe_ref, forward_ref, residual_ref):
        for b in range(per):
            where = slice(b * T, (b + 1) * T)
            corrected = (phase_ref[:, where].astype(F32) - stripe_ref[b]).astype(BF16)
            residual_ref[:, where] = (corrected.astype(F32) - forward_ref[:, where]).astype(BF16)

    return pl.pallas_call(
        kernel,
        out_shape=jax.ShapeDtypeStruct(phase.shape, BF16),
        in_specs=[VMEM] * 3,
        out_specs=VMEM,
        compiler_params=params(),
        cost_estimate=pl.CostEstimate(flops=2**19, bytes_accessed=2**21, transcendentals=0),
        name="residual",
    )(phase, stripe, forward)


def image_call(quarter, image, own, others):
    slices = image.shape[0]
    mine = own.shape[0]

    def kernel(q_ref, image_ref, own_ref, *refs):
        others_refs, out_ref = refs[:-1], refs[-1]
        for i in range(mine):
            total = own_ref[i]
            for ref in others_refs:
                total += ref[i].astype(F32)
            pixels = image_ref[:, lanes(q_ref[0] * mine + i)].astype(F32)
            out_ref[:, i * T : (i + 1) * T] = pixels + RELAX * total

    return pl.pallas_call(
        kernel,
        out_shape=jax.ShapeDtypeStruct((slices, mine * T), F32),
        in_specs=[SMEM, VMEM, VMEM] + [VMEM] * len(others),
        out_specs=VMEM,
        compiler_params=params(),
        cost_estimate=pl.CostEstimate(flops=2**18, bytes_accessed=2**20, transcendentals=0),
        name="image_step",
    )(quarter, image, own, *others)


def in_hbm(array):
    return pltpu.with_memory_space_constraint(array, pltpu.HBM)


def exchanged(array, axis):
    return lax.all_to_all(array, axis, split_axis=0, concat_axis=0, tiled=True)


def shards(projections, phase_kernel, image, tile_library, tile_entry, tile_image, tile_slot, tile_count, slot_block):
    projections = projections[0]
    library = tile_library[0, 0]
    image = image.T
    slices = projections.shape[0]
    quarters = lax.axis_size("ray")
    quarter = lax.axis_index("ray").astype(jnp.int32).reshape(1)
    tiles = (tile_entry[0], tile_image[0], tile_slot[0], tile_count)
    carried = slot_block[0]

    owners = lax.axis_size("dom")
    owner = lax.axis_index("dom").astype(jnp.int32).reshape(1)
    blocks = image.shape[1] // T

    def rims(head, tail):
        left = lax.ppermute(tail, "ray", [(i, i + 1) for i in range(quarters - 1)])
        right = lax.ppermute(head, "ray", [(i + 1, i) for i in range(quarters - 1)])
        return left, right

    def swapped(array, m):
        return lax.ppermute(array, "dom", [(i, i ^ m) for i in range(owners)])

    send, head, tail, row = first_call(*tiles, carried, projections, image, library)
    arrived = exchanged(send, "dom")
    rows = [row] + [swapped(row, m) for m in range(1, 8)]
    phase, band, stack = phase_call(projections, *rims(head, tail), phase_kernel, rows)
    stacks = [stack] + [swapped(stack, m * 8) for m in range(1, EARLY)]
    head, tail, near = rim_call(arrived, band, stacks)
    left, right = rims(head, tail)
    forward, back, stack = back_call(carried, arrived, phase, stack)
    back = stripe_call(quarter, arrived, left, right, band, back, quarters)
    returned = exchanged(back, "dom")
    stacks = [near] + [swapped(stack, m * 8) for m in range(EARLY, 8)]
    weights = counts_call(*tiles, owner, stacks, owners, library.shape[0], blocks)
    own, *sent, stripe = adjoint_call(quarter, weights, returned, library, blocks, quarters)
    others = [
        lax.ppermute(part, "ray", [(i, (i + m) % quarters) for i in range(quarters)])
        for m, part in enumerate(sent, 1)
    ]
    residual = residual_call(phase, stripe, forward)
    image_next = image_call(quarter, image, own, others)
    return residual[None], image_next.T


def solution(mesh):
    return jax.shard_map(
        shards,
        mesh=mesh,
        in_specs=(
            P("dom", None, "ray"),
            P(),
            P("dom", None),
            P("dom", "ray", None, None, None),
            P("dom", "ray", None),
            P("dom", "ray", None),
            P("dom", "ray", None),
            P("dom", "ray"),
            P("dom", "ray", None),
        ),
        out_specs=(P("dom", None, "ray"), P(("dom", "ray"), None)),
        check_vma=False,
    )
```

```python
import jax
import jax.numpy as jnp
from jax import lax
from jax.experimental import pallas as pl
from jax.experimental.pallas import tpu as pltpu
from jax.sharding import PartitionSpec as P

T = 128
SMOOTH = 8
RELAX = 0.25
PER = 16
ROOM = 32
MIB = 2**20
F32, BF16 = jnp.float32, jnp.bfloat16
NT = (((1,), (1,)), ((), ()))
VMEM = pl.BlockSpec(memory_space=pltpu.VMEM)
SMEM = pl.BlockSpec(memory_space=pltpu.SMEM)
HBM = pl.BlockSpec(memory_space=pltpu.HBM)


def params(limit=32):
    return pltpu.CompilerParams(vmem_limit_bytes=limit * MIB)


def middle_network(n):
    pairs = []
    p = 1
    while p < n:
        k = p
        while k >= 1:
            for j in range(k % p, n - k, 2 * k):
                for i in range(min(k, n - j - k)):
                    if (i + j) // (2 * p) == (i + j + k) // (2 * p):
                        pairs.append((i + j, i + j + k))
            k //= 2
        p *= 2
    needed = {n // 2 - 1, n // 2}
    kept = []
    for a, b in reversed(pairs):
        if a in needed or b in needed:
            kept.append((a, b, a in needed, b in needed))
            needed |= {a, b}
    return kept[::-1]


def lanes(block):
    return pl.ds(pl.multiple_of(block * T, T), T)


def first_call(entry, place, slot, count, numbers, projections, image, library):
    slices, columns = projections.shape
    entries, capacity = library.shape[0], entry.shape[1]
    blocks = image.shape[1] // T
    owners = slices
    rows = slices + PER
    parts = 4
    loads = blocks + 6

    def kernel(
        entry_hbm, place_hbm, slot_hbm, count_ref, n_hbm, x_hbm, image_hbm, library_hbm,
        send_ref, head_ref, tail_ref, row_ref, entry_ref, place_ref, slot_ref, n_ref, library_ref, x_ref, spread,
        stacked, product, total, packed, section, sems, load_sems,
    ):
        pairs = [(x_hbm, x_ref), (n_hbm, n_ref), (library_hbm, library_ref)]
        pairs += [
            (image_hbm.at[:, pl.ds(i * T, T)], stacked.at[pl.ds(i * slices, slices)]) for i in range(blocks)
        ]
        pairs += [(entry_hbm, entry_ref), (place_hbm, place_ref), (slot_hbm, slot_ref)]
        fetches = [pltpu.make_async_copy(a, b, load_sems.at[n]) for n, (a, b) in enumerate(pairs)]
        for fetch in fetches:
            fetch.start()
        total[...] = jnp.zeros_like(total)
        row_ref[...] = jnp.zeros_like(row_ref)
        for fetch in fetches[:2]:
            fetch.wait()
        head_ref[...] = x_ref[:, :T]
        tail_ref[...] = x_ref[:, columns - T :]
        row_ref[0:1, :owners] = n_ref[...]
        for b in range(PER):
            spread[pl.ds(b, slices, stride=PER), :] = x_ref[:, b * T : (b + 1) * T].astype(F32)
        section[...] = spread[...].astype(BF16).reshape(slices, PER, T)
        copies = [pltpu.make_async_copy(section, send_ref.at[:, pl.ds(slices, PER), :], sems.at[parts])]
        copies[0].start()
        for fetch in fetches[2:]:
            fetch.wait()
        for e in range(0, entries, 2):
            product[:, e * T : (e + 2) * T] = lax.dot_general(
                stacked[...], library_ref[e : e + 2].reshape(2 * T, T), NT, preferred_element_type=F32
            )

        def add(k):
            live = k < count_ref[0, 0]
            e = jnp.where(live, entry_ref[0, k], 0)
            i = jnp.where(live, place_ref[0, k], 0)
            s = jnp.where(live, slot_ref[0, k], owners)
            total[s] += product[pl.ds(pl.multiple_of(i * slices, slices), slices), lanes(e)]

        def group(g, carry):
            for u in range(8):
                add(g * 8 + u)
            return carry

        lax.fori_loop(0, (count_ref[0, 0] + 7) // 8, group, 0)
        step = owners // parts
        for n in range(parts):
            packed[n * step : (n + 1) * step] = total[n * step : (n + 1) * step].astype(BF16)
            here = pl.ds(n * step, step)
            copies.append(
                pltpu.make_async_copy(packed.at[here], send_ref.at[here, pl.ds(0, slices), :], sems.at[n])
            )
            copies[-1].start()
        for copy in copies:
            copy.wait()

    return pl.pallas_call(
        kernel,
        out_shape=[
            pltpu.HBM((owners, rows, T), BF16),
            jax.ShapeDtypeStruct((slices, T), BF16),
            jax.ShapeDtypeStruct((slices, T), BF16),
            jax.ShapeDtypeStruct((8, T), jnp.int32),
        ],
        in_specs=[HBM] * 3 + [SMEM] + [HBM] * 4,
        out_specs=[HBM] + [VMEM] * 3,
        scratch_shapes=[
            pltpu.SMEM(entry.shape, jnp.int32),
            pltpu.SMEM(place.shape, jnp.int32),
            pltpu.SMEM(slot.shape, jnp.int32),
            pltpu.VMEM(numbers.shape, jnp.int32),
            pltpu.VMEM(library.shape, BF16),
            pltpu.VMEM((slices, columns), BF16),
            pltpu.VMEM((slices * PER, T), F32),
            pltpu.VMEM((blocks * slices, T), BF16),
            pltpu.VMEM((blocks * slices, entries * T), F32),
            pltpu.VMEM((owners + 1, slices, T), F32),
            pltpu.VMEM((owners, slices, T), BF16),
            pltpu.VMEM((slices, PER, T), BF16),
            pltpu.SemaphoreType.DMA((parts + 1,)),
            pltpu.SemaphoreType.DMA((loads,)),
        ],
        compiler_params=params(),
        cost_estimate=pl.CostEstimate(
            flops=2 * capacity * slices * T * T, bytes_accessed=8 * 2**20, transcendentals=0
        ),
        name="forward_tiles",
    )(*map(in_hbm, (entry, place, slot)), count, *map(in_hbm, (numbers, projections, image, library)))


def phase_call(projections, left, right, taps, rows):
    slices, columns = projections.shape
    per = columns // T

    def kernel(x_hbm, l_ref, r_ref, taps_hbm, *refs):
        n = len(rows)
        row_refs, (phase_ref, band_ref, stack_ref, taps_ref, line, wide, sems) = refs[:n], refs[n:]
        for m, ref in enumerate(row_refs):
            stack_ref[m : m + 1, :] = ref[0:1, :]
        fetches = [
            pltpu.make_async_copy(x_hbm, wide.at[:, pl.ds(T, columns)], sems.at[0]),
            pltpu.make_async_copy(taps_hbm, taps_ref, sems.at[1]),
        ]
        for fetch in fetches:
            fetch.start()
        wide[:, :T] = l_ref[...]
        wide[:, T + columns :] = r_ref[...]
        line[...] = jnp.zeros_like(line)
        for fetch in fetches:
            fetch.wait()
        line[0:1, : taps_ref.shape[0]] = taps_ref[...].astype(F32).reshape(1, -1)
        spun = pltpu.roll(jnp.broadcast_to(line[0:1, :], (T, 3 * T)), T // 2, 1, stride=1, stride_axis=0)
        band_ref[...] = spun.astype(BF16)
        for b in range(per):
            phase_ref[:, b * T : (b + 1) * T] = lax.dot_general(
                wide[:, b * T : (b + 3) * T], band_ref[...], NT, preferred_element_type=F32
            ).astype(BF16)

    return pl.pallas_call(
        kernel,
        out_shape=[
            jax.ShapeDtypeStruct((slices, columns), BF16),
            jax.ShapeDtypeStruct((T, 3 * T), BF16),
            jax.ShapeDtypeStruct((8, T), jnp.int32),
        ],
        in_specs=[HBM, VMEM, VMEM, HBM] + [VMEM] * len(rows),
        out_specs=[VMEM] * 3,
        scratch_shapes=[
            pltpu.VMEM(taps.shape, BF16),
            pltpu.VMEM((8, 3 * T), F32),
            pltpu.VMEM((slices, columns + 2 * T), BF16),
            pltpu.SemaphoreType.DMA((2,)),
        ],
        compiler_params=params(),
        cost_estimate=pl.CostEstimate(flops=2**26, bytes_accessed=2**20, transcendentals=0),
        name="phase_filter",
    )(in_hbm(projections), left, right, in_hbm(taps), *rows)


def rim_call(arrived, after):
    angles = arrived.shape[0]
    size = arrived.shape[1] - PER

    def kernel(arrived_ref, _, head_ref, tail_ref, flat):
        flat[...] = arrived_ref[:, size:, :].astype(F32).reshape(angles * PER, T)
        head_ref[...] = flat[pl.ds(0, angles, stride=PER), :].astype(BF16)
        tail_ref[...] = flat[pl.ds(PER - 1, angles, stride=PER), :].astype(BF16)

    return pl.pallas_call(
        kernel,
        out_shape=[jax.ShapeDtypeStruct((angles, T), BF16)] * 2,
        in_specs=[VMEM, VMEM],
        out_specs=[VMEM] * 2,
        scratch_shapes=[pltpu.VMEM((angles * PER, T), F32)],
        compiler_params=params(),
        cost_estimate=pl.CostEstimate(flops=2**17, bytes_accessed=2**18, transcendentals=0),
        name="rim",
    )(arrived, after)


def stripe_of(quarter, quarters, angles, values, rimmed):
    network = middle_network(angles)

    def middle(g, carry):
        v = [values[pl.ds(pl.multiple_of(a * ROOM + g * 8, 8), 8), :] for a in range(angles)]
        for a, b, low, high in network:
            x, y = v[a], v[b]
            if low:
                v[a] = jnp.minimum(x, y)
            if high:
                v[b] = jnp.maximum(x, y)
        rimmed[pl.ds(g * 8 + 1, 8), :] = (v[angles // 2 - 1] + v[angles // 2]) * 0.5
        return carry

    lax.fori_loop(0, 3, middle, 0)
    before, after = rimmed[17:18, :], rimmed[18:19, :]
    rimmed[0:1, :] = jnp.where(quarter == 0, jnp.zeros_like(before), before)
    rimmed[17:18, :] = jnp.where(quarter == quarters - 1, jnp.zeros_like(after), after)
    prev, cur, nxt = rimmed[0:16, :], rimmed[1:17, :], rimmed[2:18, :]
    lane = lax.broadcasted_iota(jnp.int32, (16, T), 1)
    total = cur
    for o in range(1, SMOOTH + 1):
        total += pltpu.roll(jnp.where(lane < o, nxt, cur), T - o, 1)
        total += pltpu.roll(jnp.where(lane >= T - o, prev, cur), o, 1)
    place = quarter * (16 * T) + lax.broadcasted_iota(jnp.int32, (16, T), 0) * T + lane
    last = quarters * 16 * T - 1
    count = jnp.minimum(place + SMOOTH, last) - jnp.maximum(place - SMOOTH, 0) + 1
    return cur - total / count.astype(F32)


def back_call(carried, arrived, phase, stacked):
    owners = arrived.shape[0]
    size, columns = phase.shape
    parts = 4

    def kernel(
        c_ref, arrived_ref, phase_ref, stacked_ref, forward_hbm, send_ref, stack_ref, forward, less, packed, sems
    ):
        forward[...] = jnp.zeros_like(forward)
        for d in range(owners):
            forward[:, lanes(c_ref[0, d])] += arrived_ref[d, :size, :].astype(F32)
        copies = [pltpu.make_async_copy(forward, forward_hbm, sems.at[parts])]
        copies[0].start()
        less[...] = (phase_ref[...].astype(F32) - forward[...]).astype(BF16)
        step = owners // parts
        for n in range(parts):
            for d in range(n * step, (n + 1) * step):
                packed[d] = less[:, lanes(c_ref[0, d])]
            here = pl.ds(n * step, step)
            copies.append(pltpu.make_async_copy(packed.at[here], send_ref.at[here], sems.at[n]))
            copies[-1].start()
        stack_ref[...] = stacked_ref[...]
        for copy in copies:
            copy.wait()

    return pl.pallas_call(
        kernel,
        out_shape=[
            pltpu.HBM((size, columns), F32),
            pltpu.HBM((owners, size, T), BF16),
            jax.ShapeDtypeStruct((8, T), jnp.int32),
        ],
        in_specs=[SMEM] + [VMEM] * 3,
        out_specs=[HBM, HBM, VMEM],
        scratch_shapes=[
            pltpu.VMEM((size, columns), F32),
            pltpu.VMEM((size, columns), BF16),
            pltpu.VMEM((owners, size, T), BF16),
            pltpu.SemaphoreType.DMA((parts + 1,)),
        ],
        compiler_params=params(),
        cost_estimate=pl.CostEstimate(flops=2**24, bytes_accessed=8 * 2**20, transcendentals=0),
        name="slot_sums",
    )(carried, arrived, phase, stacked)


def stripe_call(quarter, arrived, left, right, band, quarters):
    angles = arrived.shape[0]
    size = arrived.shape[1] - PER

    def kernel(
        q_ref, arrived_ref, l_ref, r_ref, band_ref, stripe_ref, flat, wide, values, rimmed
    ):
        def block(n):
            return pl.ds(n * angles, angles)

        flat[...] = arrived_ref[:, size:, :].astype(F32).reshape(angles * PER, T)
        for b in range(PER):
            wide[block(b + 2), :] = flat[pl.ds(b, angles, stride=PER), :].astype(BF16)
        wide[block(0), :] = jnp.zeros((angles, T), BF16)
        wide[block(1), :] = l_ref[...]
        wide[block(PER + 2), :] = r_ref[...]
        wide[block(PER + 3), :] = jnp.zeros((angles, T), BF16)
        values[...] = jnp.zeros_like(values)
        filtered = sum(
            lax.dot_general(
                wide[n * angles : (n + PER + 2) * angles, :],
                band_ref[:, n * T : (n + 1) * T],
                NT,
                preferred_element_type=F32,
            )
            for n in range(3)
        ).astype(BF16)
        for at, b in enumerate([*range(1, PER + 1), 0, PER + 1]):
            values[pl.ds(at, angles, stride=ROOM), :] = filtered[b * angles : (b + 1) * angles].astype(F32)
        stripe_ref[...] = stripe_of(q_ref[0], quarters, angles, values, rimmed).astype(BF16)

    return pl.pallas_call(
        kernel,
        out_shape=jax.ShapeDtypeStruct((PER, T), BF16),
        in_specs=[SMEM] + [VMEM] * 4,
        out_specs=VMEM,
        scratch_shapes=[
            pltpu.VMEM((angles * PER, T), F32),
            pltpu.VMEM(((PER + 4) * angles, T), BF16),
            pltpu.VMEM((angles * ROOM, T), F32),
            pltpu.VMEM((32, T), F32),
        ],
        compiler_params=params(),
        cost_estimate=pl.CostEstimate(flops=2**26, bytes_accessed=2**20, transcendentals=0),
        name="stripe",
    )(quarter, arrived, left, right, band)


def bundle_call(stripes, stack):
    count = len(stripes)

    def kernel(*refs):
        stripe_refs, (stack_ref, out_ref) = refs[:count], refs[count:]
        for m, ref in enumerate(stripe_refs):
            out_ref[m] = ref[...]
        numbers = stack_ref[...].astype(F32)
        out_ref[count] = jnp.concatenate([numbers, jnp.zeros_like(numbers)], axis=0).astype(BF16)

    return pl.pallas_call(
        kernel,
        out_shape=jax.ShapeDtypeStruct((count + 1, PER, T), BF16),
        in_specs=[VMEM] * (count + 1),
        out_specs=VMEM,
        compiler_params=params(),
        cost_estimate=pl.CostEstimate(flops=2**15, bytes_accessed=2**16, transcendentals=0),
        name="bundle",
    )(*stripes, stack)


def counts_call(entry, place, slot, count, owner, after, owners, entries, blocks):
    capacity = entry.shape[1]

    def kernel(
        entry_hbm, place_hbm, slot_hbm, count_ref, owner_ref, _,
        met_ref, by_row_ref, entry_ref, place_ref, slot_ref, loads,
    ):
        pairs = [(entry_hbm, entry_ref), (place_hbm, place_ref), (slot_hbm, slot_ref)]
        fetches = [pltpu.make_async_copy(a, b, loads.at[n]) for n, (a, b) in enumerate(pairs)]
        for fetch in fetches:
            fetch.start()

        def ones(rows, match):
            return (lax.broadcasted_iota(jnp.int32, (rows, match.shape[1]), 0) == match).astype(F32).astype(BF16)

        for fetch in fetches:
            fetch.wait()
        live = lax.broadcasted_iota(jnp.int32, (1, capacity), 1) < count_ref[0, 0]
        of_bin = ones(entries * blocks, jnp.where(live, entry_ref[...] * blocks + place_ref[...], -1))
        met = lax.dot_general(of_bin, ones(T, slot_ref[...]), NT, preferred_element_type=F32)
        met_ref[...] = met.astype(BF16)
        k = lax.broadcasted_iota(jnp.int32, (T, capacity), 0)
        by_row = (k < owners) & ((owner_ref[0] ^ k) == slot_ref[...])
        by_row = lax.dot_general(of_bin, by_row.astype(F32).astype(BF16), NT, preferred_element_type=F32)
        by_row_ref[...] = by_row.astype(BF16)

    return pl.pallas_call(
        kernel,
        out_shape=[jax.ShapeDtypeStruct((entries * blocks, T), BF16)] * 2,
        in_specs=[HBM] * 3 + [SMEM, SMEM, VMEM],
        out_specs=[VMEM, VMEM],
        scratch_shapes=[
            pltpu.VMEM(entry.shape, jnp.int32),
            pltpu.VMEM(place.shape, jnp.int32),
            pltpu.VMEM(slot.shape, jnp.int32),
            pltpu.SemaphoreType.DMA((3,)),
        ],
        compiler_params=params(),
        cost_estimate=pl.CostEstimate(flops=2**24, bytes_accessed=2**20, transcendentals=0),
        name="tile_counts",
    )(*map(in_hbm, (entry, place, slot)), count, owner, after)


def adjoint_call(quarter, owner, met, by_row, returned, bundles, library, blocks, quarters):
    entries = library.shape[0]
    owners = returned.shape[0]
    per = PER
    size = returned.shape[1]
    near = bundles[0].shape[0] - 1
    held = blocks // quarters

    def kernel(q_ref, owner_ref, met_ref, by_row_ref, returned_ref, library_hbm, *refs):
        bundle_refs, refs = refs[: len(bundles)], refs[len(bundles) :]
        outs, refs = refs[:quarters], refs[quarters:]
        stripe_ref, library_ref, every, stripes, terms, bins, whole, load = refs
        fetch = pltpu.make_async_copy(library_hbm, library_ref, load)
        fetch.start()
        terms[...] = returned_ref[...].astype(F32).reshape(owners * size, T)
        for m, ref in enumerate(bundle_refs):
            every[m * near : (m + 1) * near] = ref[:near]
        numbers = jnp.concatenate([ref[near].astype(F32)[:near] for ref in bundle_refs], axis=0)
        lane = lax.broadcasted_iota(jnp.int32, (owners, T), 1)
        theirs = jnp.sum(jnp.where(lane == owner_ref[0], numbers, 0.0), axis=1, keepdims=True)
        carries = (theirs.astype(jnp.int32) + owners == lane).astype(F32).astype(BF16)
        stripe_met = jnp.dot(by_row_ref[:, :owners], carries, preferred_element_type=F32)
        weights = (met_ref[...].astype(F32) - stripe_met).astype(BF16)[:, : owners + per]

        def both(n):
            here = terms[pl.ds(n, owners, stride=size), :].astype(BF16)
            return jnp.concatenate([here, every[owner_ref[0] ^ n]], axis=0)

        for n in range(0, size, 2):
            made = jnp.dot(
                weights, jnp.concatenate([both(n), both(n + 1)], axis=1), preferred_element_type=F32
            ).astype(BF16)
            for u in range(2):
                for e in range(entries):
                    bins[(n + u) * blocks : (n + u + 1) * blocks, e * T : (e + 1) * T] = made[
                        e * blocks : (e + 1) * blocks, u * T : (u + 1) * T
                    ]
        fetch.wait()
        whole[...] = jnp.dot(bins[...], library_ref[...].reshape(entries * T, T), preferred_element_type=F32)
        for m, out_ref in enumerate(outs):
            start = lax.rem(q_ref[0] + m, quarters) * held
            for t in range(held):
                out_ref[t] = whole[pl.ds(start + t, size, stride=blocks), :].astype(out_ref.dtype)
        for n in range(size):
            stripes[n * per : (n + 1) * per, :] = every[owner_ref[0] ^ n].astype(F32)
        for b in range(per):
            stripe_ref[b] = stripes[pl.ds(b, size, stride=per), :]

    return pl.pallas_call(
        kernel,
        out_shape=[
            *(jax.ShapeDtypeStruct((held, size, T), BF16 if m else F32) for m in range(quarters)),
            jax.ShapeDtypeStruct((per, size, T), F32),
        ],
        in_specs=[SMEM, SMEM, VMEM, VMEM, VMEM, HBM] + [VMEM] * len(bundles),
        out_specs=[VMEM] * (quarters + 1),
        scratch_shapes=[
            pltpu.VMEM(library.shape, BF16),
            pltpu.VMEM((owners, per, T), BF16),
            pltpu.VMEM((owners * per, T), F32),
            pltpu.VMEM((owners * size, T), F32),
            pltpu.VMEM((size * blocks, entries * T), BF16),
            pltpu.VMEM((size * blocks, T), F32),
            pltpu.SemaphoreType.DMA,
        ],
        compiler_params=params(),
        cost_estimate=pl.CostEstimate(
            flops=2 * 256 * size * T * T, bytes_accessed=8 * 2**20, transcendentals=0
        ),
        name="adjoint_tiles",
    )(quarter, owner, met, by_row, returned, in_hbm(library), *bundles)


def residual_call(phase, stripe, forward):
    per = stripe.shape[0]

    def kernel(phase_ref, stripe_ref, forward_ref, residual_ref):
        for b in range(per):
            where = slice(b * T, (b + 1) * T)
            corrected = (phase_ref[:, where].astype(F32) - stripe_ref[b]).astype(BF16)
            residual_ref[:, where] = (corrected.astype(F32) - forward_ref[:, where]).astype(BF16)

    return pl.pallas_call(
        kernel,
        out_shape=jax.ShapeDtypeStruct(phase.shape, BF16),
        in_specs=[VMEM] * 3,
        out_specs=VMEM,
        compiler_params=params(),
        cost_estimate=pl.CostEstimate(flops=2**19, bytes_accessed=2**21, transcendentals=0),
        name="residual",
    )(phase, stripe, forward)


def image_call(quarter, image, own, others):
    slices = image.shape[0]
    mine = own.shape[0]

    def kernel(q_ref, image_ref, own_ref, *refs):
        others_refs, out_ref = refs[:-1], refs[-1]
        for i in range(mine):
            total = own_ref[i]
            for ref in others_refs:
                total += ref[i].astype(F32)
            pixels = image_ref[:, lanes(q_ref[0] * mine + i)].astype(F32)
            out_ref[:, i * T : (i + 1) * T] = pixels + RELAX * total

    return pl.pallas_call(
        kernel,
        out_shape=jax.ShapeDtypeStruct((slices, mine * T), F32),
        in_specs=[SMEM, VMEM, VMEM] + [VMEM] * len(others),
        out_specs=VMEM,
        compiler_params=params(),
        cost_estimate=pl.CostEstimate(flops=2**18, bytes_accessed=2**20, transcendentals=0),
        name="image_step",
    )(quarter, image, own, *others)


def in_hbm(array):
    return pltpu.with_memory_space_constraint(array, pltpu.HBM)


def exchanged(array, axis):
    return lax.all_to_all(array, axis, split_axis=0, concat_axis=0, tiled=True)


def shards(projections, phase_kernel, image, tile_library, tile_entry, tile_image, tile_slot, tile_count, slot_block):
    projections = projections[0]
    library = tile_library[0, 0]
    image = image.T
    slices = projections.shape[0]
    quarters = lax.axis_size("ray")
    quarter = lax.axis_index("ray").astype(jnp.int32).reshape(1)
    tiles = (tile_entry[0], tile_image[0], tile_slot[0], tile_count)
    carried = slot_block[0]

    owners = lax.axis_size("dom")
    owner = lax.axis_index("dom").astype(jnp.int32).reshape(1)
    blocks = image.shape[1] // T

    def rims(head, tail):
        left = lax.ppermute(tail, "ray", [(i, i + 1) for i in range(quarters - 1)])
        right = lax.ppermute(head, "ray", [(i + 1, i) for i in range(quarters - 1)])
        return left, right

    def swapped(array, m):
        return lax.ppermute(array, "dom", [(i, i ^ m) for i in range(owners)])

    send, head, tail, row = first_call(*tiles, carried, projections, image, library)
    arrived = exchanged(send, "dom")
    rows = [row] + [swapped(row, m) for m in range(1, 8)]
    phase, band, stack = phase_call(projections, *rims(head, tail), phase_kernel, rows)
    forward, back, stack = back_call(carried, arrived, phase, stack)
    returned = exchanged(back, "dom")
    met, by_row = counts_call(*tiles, owner, stack, owners, library.shape[0], blocks)
    stripe = stripe_call(quarter, arrived, *rims(*rim_call(arrived, stack)), band, quarters)
    bundle = bundle_call([stripe] + [swapped(stripe, m) for m in range(1, 8)], stack)
    bundles = [bundle] + [swapped(bundle, m * 8) for m in range(1, 8)]
    own, *sent, stripe = adjoint_call(quarter, owner, met, by_row, returned, bundles, library, blocks, quarters)
    others = [
        lax.ppermute(part, "ray", [(i, (i + m) % quarters) for i in range(quarters)])
        for m, part in enumerate(sent, 1)
    ]
    residual = residual_call(phase, stripe, forward)
    image_next = image_call(quarter, image, own, others)
    return residual[None], image_next.T


def solution(mesh):
    return jax.shard_map(
        shards,
        mesh=mesh,
        in_specs=(
            P("dom", None, "ray"),
            P(),
            P("dom", None),
            P("dom", "ray", None, None, None),
            P("dom", "ray", None),
            P("dom", "ray", None),
            P("dom", "ray", None),
            P("dom", "ray"),
            P("dom", "ray", None),
        ),
        out_specs=(P("dom", None, "ray"), P(("dom", "ray"), None)),
        check_vma=False,
    )
```

```python
import jax
import jax.numpy as jnp
from jax import lax
from jax.experimental import pallas as pl
from jax.experimental.pallas import tpu as pltpu
from jax.sharding import PartitionSpec as P

T = 128
SMOOTH = 8
RELAX = 0.25
PER = 16
ROOM = 32
MIB = 2**20
F32, BF16 = jnp.float32, jnp.bfloat16
NT = (((1,), (1,)), ((), ()))
VMEM = pl.BlockSpec(memory_space=pltpu.VMEM)
SMEM = pl.BlockSpec(memory_space=pltpu.SMEM)
HBM = pl.BlockSpec(memory_space=pltpu.HBM)


def params(limit=32):
    return pltpu.CompilerParams(vmem_limit_bytes=limit * MIB)


def middle_network(n):
    pairs = []
    p = 1
    while p < n:
        k = p
        while k >= 1:
            for j in range(k % p, n - k, 2 * k):
                for i in range(min(k, n - j - k)):
                    if (i + j) // (2 * p) == (i + j + k) // (2 * p):
                        pairs.append((i + j, i + j + k))
            k //= 2
        p *= 2
    needed = {n // 2 - 1, n // 2}
    kept = []
    for a, b in reversed(pairs):
        if a in needed or b in needed:
            kept.append((a, b, a in needed, b in needed))
            needed |= {a, b}
    return kept[::-1]


def lanes(block):
    return pl.ds(pl.multiple_of(block * T, T), T)


def first_call(entry, place, slot, count, numbers, projections, image, library):
    slices, columns = projections.shape
    entries, capacity = library.shape[0], entry.shape[1]
    blocks = image.shape[1] // T
    owners = slices
    rows = slices + PER
    parts = 4
    loads = blocks + 6

    def kernel(
        entry_hbm, place_hbm, slot_hbm, count_ref, n_hbm, x_hbm, image_hbm, library_hbm,
        send_ref, head_ref, tail_ref, row_ref, entry_ref, place_ref, slot_ref, n_ref, library_ref, x_ref, spread,
        stacked, product, total, packed, section, sems, load_sems,
    ):
        pairs = [(x_hbm, x_ref), (n_hbm, n_ref), (library_hbm, library_ref)]
        pairs += [
            (image_hbm.at[:, pl.ds(i * T, T)], stacked.at[pl.ds(i * slices, slices)]) for i in range(blocks)
        ]
        pairs += [(entry_hbm, entry_ref), (place_hbm, place_ref), (slot_hbm, slot_ref)]
        fetches = [pltpu.make_async_copy(a, b, load_sems.at[n]) for n, (a, b) in enumerate(pairs)]
        for fetch in fetches:
            fetch.start()
        total[...] = jnp.zeros_like(total)
        row_ref[...] = jnp.zeros_like(row_ref)
        for fetch in fetches[:2]:
            fetch.wait()
        head_ref[...] = x_ref[:, :T]
        tail_ref[...] = x_ref[:, columns - T :]
        row_ref[0:1, :owners] = n_ref[...]
        for b in range(PER):
            spread[pl.ds(b, slices, stride=PER), :] = x_ref[:, b * T : (b + 1) * T].astype(F32)
        section[...] = spread[...].astype(BF16).reshape(slices, PER, T)
        copies = [pltpu.make_async_copy(section, send_ref.at[:, pl.ds(slices, PER), :], sems.at[parts])]
        copies[0].start()
        for fetch in fetches[2:]:
            fetch.wait()
        for e in range(0, entries, 2):
            product[:, e * T : (e + 2) * T] = lax.dot_general(
                stacked[...], library_ref[e : e + 2].reshape(2 * T, T), NT, preferred_element_type=F32
            )

        def add(k):
            live = k < count_ref[0, 0]
            e = jnp.where(live, entry_ref[0, k], 0)
            i = jnp.where(live, place_ref[0, k], 0)
            s = jnp.where(live, slot_ref[0, k], owners)
            total[s] += product[pl.ds(pl.multiple_of(i * slices, slices), slices), lanes(e)]

        def group(g, carry):
            for u in range(8):
                add(g * 8 + u)
            return carry

        lax.fori_loop(0, (count_ref[0, 0] + 7) // 8, group, 0)
        step = owners // parts
        for n in range(parts):
            packed[n * step : (n + 1) * step] = total[n * step : (n + 1) * step].astype(BF16)
            here = pl.ds(n * step, step)
            copies.append(
                pltpu.make_async_copy(packed.at[here], send_ref.at[here, pl.ds(0, slices), :], sems.at[n])
            )
            copies[-1].start()
        for copy in copies:
            copy.wait()

    return pl.pallas_call(
        kernel,
        out_shape=[
            pltpu.HBM((owners, rows, T), BF16),
            jax.ShapeDtypeStruct((slices, T), BF16),
            jax.ShapeDtypeStruct((slices, T), BF16),
            jax.ShapeDtypeStruct((8, T), jnp.int32),
        ],
        in_specs=[HBM] * 3 + [SMEM] + [HBM] * 4,
        out_specs=[HBM] + [VMEM] * 3,
        scratch_shapes=[
            pltpu.SMEM(entry.shape, jnp.int32),
            pltpu.SMEM(place.shape, jnp.int32),
            pltpu.SMEM(slot.shape, jnp.int32),
            pltpu.VMEM(numbers.shape, jnp.int32),
            pltpu.VMEM(library.shape, BF16),
            pltpu.VMEM((slices, columns), BF16),
            pltpu.VMEM((slices * PER, T), F32),
            pltpu.VMEM((blocks * slices, T), BF16),
            pltpu.VMEM((blocks * slices, entries * T), F32),
            pltpu.VMEM((owners + 1, slices, T), F32),
            pltpu.VMEM((owners, slices, T), BF16),
            pltpu.VMEM((slices, PER, T), BF16),
            pltpu.SemaphoreType.DMA((parts + 1,)),
            pltpu.SemaphoreType.DMA((loads,)),
        ],
        compiler_params=params(),
        cost_estimate=pl.CostEstimate(
            flops=2 * capacity * slices * T * T, bytes_accessed=8 * 2**20, transcendentals=0
        ),
        name="forward_tiles",
    )(*map(in_hbm, (entry, place, slot)), count, *map(in_hbm, (numbers, projections, image, library)))


def phase_call(projections, left, right, taps, rows):
    slices, columns = projections.shape
    per = columns // T

    def kernel(x_hbm, l_ref, r_ref, taps_hbm, *refs):
        n = len(rows)
        row_refs, (phase_ref, band_ref, stack_ref, taps_ref, line, wide, sems) = refs[:n], refs[n:]
        for m, ref in enumerate(row_refs):
            stack_ref[m : m + 1, :] = ref[0:1, :]
        fetches = [
            pltpu.make_async_copy(x_hbm, wide.at[:, pl.ds(T, columns)], sems.at[0]),
            pltpu.make_async_copy(taps_hbm, taps_ref, sems.at[1]),
        ]
        for fetch in fetches:
            fetch.start()
        wide[:, :T] = l_ref[...]
        wide[:, T + columns :] = r_ref[...]
        line[...] = jnp.zeros_like(line)
        for fetch in fetches:
            fetch.wait()
        line[0:1, : taps_ref.shape[0]] = taps_ref[...].astype(F32).reshape(1, -1)
        spun = pltpu.roll(jnp.broadcast_to(line[0:1, :], (T, 3 * T)), T // 2, 1, stride=1, stride_axis=0)
        band_ref[...] = spun.astype(BF16)
        for b in range(per):
            phase_ref[:, b * T : (b + 1) * T] = lax.dot_general(
                wide[:, b * T : (b + 3) * T], band_ref[...], NT, preferred_element_type=F32
            ).astype(BF16)

    return pl.pallas_call(
        kernel,
        out_shape=[
            jax.ShapeDtypeStruct((slices, columns), BF16),
            jax.ShapeDtypeStruct((T, 3 * T), BF16),
            jax.ShapeDtypeStruct((8, T), jnp.int32),
        ],
        in_specs=[HBM, VMEM, VMEM, HBM] + [VMEM] * len(rows),
        out_specs=[VMEM] * 3,
        scratch_shapes=[
            pltpu.VMEM(taps.shape, BF16),
            pltpu.VMEM((8, 3 * T), F32),
            pltpu.VMEM((slices, columns + 2 * T), BF16),
            pltpu.SemaphoreType.DMA((2,)),
        ],
        compiler_params=params(),
        cost_estimate=pl.CostEstimate(flops=2**26, bytes_accessed=2**20, transcendentals=0),
        name="phase_filter",
    )(in_hbm(projections), left, right, in_hbm(taps), *rows)


def rim_call(arrived, after):
    angles = arrived.shape[0]
    size = arrived.shape[1] - PER

    def kernel(arrived_ref, _, head_ref, tail_ref, flat):
        flat[...] = arrived_ref[:, size:, :].astype(F32).reshape(angles * PER, T)
        head_ref[...] = flat[pl.ds(0, angles, stride=PER), :].astype(BF16)
        tail_ref[...] = flat[pl.ds(PER - 1, angles, stride=PER), :].astype(BF16)

    return pl.pallas_call(
        kernel,
        out_shape=[jax.ShapeDtypeStruct((angles, T), BF16)] * 2,
        in_specs=[VMEM, VMEM],
        out_specs=[VMEM] * 2,
        scratch_shapes=[pltpu.VMEM((angles * PER, T), F32)],
        compiler_params=params(),
        cost_estimate=pl.CostEstimate(flops=2**17, bytes_accessed=2**18, transcendentals=0),
        name="rim",
    )(arrived, after)


def stripe_of(quarter, quarters, angles, values, rimmed):
    network = middle_network(angles)

    def middle(g, carry):
        v = [values[pl.ds(pl.multiple_of(a * ROOM + g * 8, 8), 8), :] for a in range(angles)]
        for a, b, low, high in network:
            x, y = v[a], v[b]
            if low:
                v[a] = jnp.minimum(x, y)
            if high:
                v[b] = jnp.maximum(x, y)
        rimmed[pl.ds(g * 8 + 1, 8), :] = (v[angles // 2 - 1] + v[angles // 2]) * 0.5
        return carry

    lax.fori_loop(0, 3, middle, 0)
    before, after = rimmed[17:18, :], rimmed[18:19, :]
    rimmed[0:1, :] = jnp.where(quarter == 0, jnp.zeros_like(before), before)
    rimmed[17:18, :] = jnp.where(quarter == quarters - 1, jnp.zeros_like(after), after)
    prev, cur, nxt = rimmed[0:16, :], rimmed[1:17, :], rimmed[2:18, :]
    lane = lax.broadcasted_iota(jnp.int32, (16, T), 1)
    total = cur
    for o in range(1, SMOOTH + 1):
        total += pltpu.roll(jnp.where(lane < o, nxt, cur), T - o, 1)
        total += pltpu.roll(jnp.where(lane >= T - o, prev, cur), o, 1)
    place = quarter * (16 * T) + lax.broadcasted_iota(jnp.int32, (16, T), 0) * T + lane
    last = quarters * 16 * T - 1
    count = jnp.minimum(place + SMOOTH, last) - jnp.maximum(place - SMOOTH, 0) + 1
    return cur - total / count.astype(F32)


def back_call(carried, arrived, phase, stacked):
    owners = arrived.shape[0]
    size, columns = phase.shape
    parts = 4

    def kernel(
        c_ref, arrived_ref, phase_ref, stacked_ref, forward_hbm, send_ref, stack_ref, forward, less, packed, sems
    ):
        forward[...] = jnp.zeros_like(forward)
        for d in range(owners):
            forward[:, lanes(c_ref[0, d])] += arrived_ref[d, :size, :].astype(F32)
        copies = [pltpu.make_async_copy(forward, forward_hbm, sems.at[parts])]
        copies[0].start()
        less[...] = (phase_ref[...].astype(F32) - forward[...]).astype(BF16)
        step = owners // parts
        for n in range(parts):
            for d in range(n * step, (n + 1) * step):
                packed[d] = less[:, lanes(c_ref[0, d])]
            here = pl.ds(n * step, step)
            copies.append(pltpu.make_async_copy(packed.at[here], send_ref.at[here], sems.at[n]))
            copies[-1].start()
        stack_ref[...] = stacked_ref[...]
        for copy in copies:
            copy.wait()

    return pl.pallas_call(
        kernel,
        out_shape=[
            pltpu.HBM((size, columns), F32),
            pltpu.HBM((owners, size, T), BF16),
            jax.ShapeDtypeStruct((8, T), jnp.int32),
        ],
        in_specs=[SMEM] + [VMEM] * 3,
        out_specs=[HBM, HBM, VMEM],
        scratch_shapes=[
            pltpu.VMEM((size, columns), F32),
            pltpu.VMEM((size, columns), BF16),
            pltpu.VMEM((owners, size, T), BF16),
            pltpu.SemaphoreType.DMA((parts + 1,)),
        ],
        compiler_params=params(),
        cost_estimate=pl.CostEstimate(flops=2**24, bytes_accessed=8 * 2**20, transcendentals=0),
        name="slot_sums",
    )(carried, arrived, phase, stacked)


def stripe_call(quarter, arrived, left, right, band, quarters):
    angles = arrived.shape[0]
    size = arrived.shape[1] - PER

    def kernel(
        q_ref, arrived_ref, l_ref, r_ref, band_ref, stripe_ref, flat, wide, values, rimmed
    ):
        def block(n):
            return pl.ds(n * angles, angles)

        flat[...] = arrived_ref[:, size:, :].astype(F32).reshape(angles * PER, T)
        for b in range(PER):
            wide[block(b + 2), :] = flat[pl.ds(b, angles, stride=PER), :].astype(BF16)
        wide[block(0), :] = jnp.zeros((angles, T), BF16)
        wide[block(1), :] = l_ref[...]
        wide[block(PER + 2), :] = r_ref[...]
        wide[block(PER + 3), :] = jnp.zeros((angles, T), BF16)
        values[...] = jnp.zeros_like(values)
        filtered = sum(
            lax.dot_general(
                wide[n * angles : (n + PER + 2) * angles, :],
                band_ref[:, n * T : (n + 1) * T],
                NT,
                preferred_element_type=F32,
            )
            for n in range(3)
        ).astype(BF16)
        for at, b in enumerate([*range(1, PER + 1), 0, PER + 1]):
            values[pl.ds(at, angles, stride=ROOM), :] = filtered[b * angles : (b + 1) * angles].astype(F32)
        stripe_ref[0] = stripe_of(q_ref[0], quarters, angles, values, rimmed).astype(BF16)

    return pl.pallas_call(
        kernel,
        out_shape=jax.ShapeDtypeStruct((1, PER, T), BF16),
        in_specs=[SMEM] + [VMEM] * 4,
        out_specs=VMEM,
        scratch_shapes=[
            pltpu.VMEM((angles * PER, T), F32),
            pltpu.VMEM(((PER + 4) * angles, T), BF16),
            pltpu.VMEM((angles * ROOM, T), F32),
            pltpu.VMEM((32, T), F32),
        ],
        compiler_params=params(),
        cost_estimate=pl.CostEstimate(flops=2**26, bytes_accessed=2**20, transcendentals=0),
        name="stripe",
    )(quarter, arrived, left, right, band)


def joined_call(arrays, stack=None):
    lengths = [array.shape[0] for array in arrays]
    whole = sum(lengths)
    given = list(arrays) + ([] if stack is None else [stack])

    def kernel(*refs):
        out_ref = refs[-1]
        start = 0
        for ref, length in zip(refs, lengths):
            out_ref[start : start + length] = ref[...]
            start += length
        if stack is not None:
            numbers = refs[-2][...].astype(F32)
            out_ref[whole] = jnp.concatenate([numbers, jnp.zeros_like(numbers)], axis=0).astype(BF16)

    return pl.pallas_call(
        kernel,
        out_shape=jax.ShapeDtypeStruct((whole + (stack is not None), PER, T), BF16),
        in_specs=[VMEM] * len(given),
        out_specs=VMEM,
        compiler_params=params(),
        cost_estimate=pl.CostEstimate(flops=2**15, bytes_accessed=2**16, transcendentals=0),
        name="joined",
    )(*given)


def counts_call(entry, place, slot, count, owner, after, owners, entries, blocks):
    capacity = entry.shape[1]

    def kernel(
        entry_hbm, place_hbm, slot_hbm, count_ref, owner_ref, _,
        met_ref, by_row_ref, entry_ref, place_ref, slot_ref, loads,
    ):
        pairs = [(entry_hbm, entry_ref), (place_hbm, place_ref), (slot_hbm, slot_ref)]
        fetches = [pltpu.make_async_copy(a, b, loads.at[n]) for n, (a, b) in enumerate(pairs)]
        for fetch in fetches:
            fetch.start()

        def ones(rows, match):
            return (lax.broadcasted_iota(jnp.int32, (rows, match.shape[1]), 0) == match).astype(F32).astype(BF16)

        for fetch in fetches:
            fetch.wait()
        live = lax.broadcasted_iota(jnp.int32, (1, capacity), 1) < count_ref[0, 0]
        of_bin = ones(entries * blocks, jnp.where(live, entry_ref[...] * blocks + place_ref[...], -1))
        met = lax.dot_general(of_bin, ones(T, slot_ref[...]), NT, preferred_element_type=F32)
        met_ref[...] = met.astype(BF16)
        k = lax.broadcasted_iota(jnp.int32, (T, capacity), 0)
        by_row = (k < owners) & ((owner_ref[0] ^ k) == slot_ref[...])
        by_row = lax.dot_general(of_bin, by_row.astype(F32).astype(BF16), NT, preferred_element_type=F32)
        by_row_ref[...] = by_row.astype(BF16)

    return pl.pallas_call(
        kernel,
        out_shape=[jax.ShapeDtypeStruct((entries * blocks, T), BF16)] * 2,
        in_specs=[HBM] * 3 + [SMEM, SMEM, VMEM],
        out_specs=[VMEM, VMEM],
        scratch_shapes=[
            pltpu.VMEM(entry.shape, jnp.int32),
            pltpu.VMEM(place.shape, jnp.int32),
            pltpu.VMEM(slot.shape, jnp.int32),
            pltpu.SemaphoreType.DMA((3,)),
        ],
        compiler_params=params(),
        cost_estimate=pl.CostEstimate(flops=2**24, bytes_accessed=2**20, transcendentals=0),
        name="tile_counts",
    )(*map(in_hbm, (entry, place, slot)), count, owner, after)


def adjoint_call(quarter, owner, met, by_row, returned, bundles, library, blocks, quarters):
    entries = library.shape[0]
    owners = returned.shape[0]
    per = PER
    size = returned.shape[1]
    near = 8
    each = bundles[0].shape[0] // (near + 1)
    held = blocks // quarters

    def kernel(q_ref, owner_ref, met_ref, by_row_ref, returned_ref, library_hbm, *refs):
        bundle_refs, refs = refs[: len(bundles)], refs[len(bundles) :]
        outs, refs = refs[:quarters], refs[quarters:]
        stripe_ref, library_ref, every, stripes, terms, bins, whole, load = refs
        fetch = pltpu.make_async_copy(library_hbm, library_ref, load)
        fetch.start()
        terms[...] = returned_ref[...].astype(F32).reshape(owners * size, T)
        numbers = []
        for ref in bundle_refs:
            for t in range(0, each * (near + 1), near + 1):
                m = len(numbers)
                every[m * near : (m + 1) * near] = ref[t : t + near]
                numbers.append(ref[t + near].astype(F32)[:near])
        numbers = jnp.concatenate(numbers, axis=0)
        lane = lax.broadcasted_iota(jnp.int32, (owners, T), 1)
        theirs = jnp.sum(jnp.where(lane == owner_ref[0], numbers, 0.0), axis=1, keepdims=True)
        carries = (theirs.astype(jnp.int32) + owners == lane).astype(F32).astype(BF16)
        stripe_met = jnp.dot(by_row_ref[:, :owners], carries, preferred_element_type=F32)
        weights = (met_ref[...].astype(F32) - stripe_met).astype(BF16)[:, : owners + per]

        def both(n):
            here = terms[pl.ds(n, owners, stride=size), :].astype(BF16)
            return jnp.concatenate([here, every[owner_ref[0] ^ n]], axis=0)

        for n in range(0, size, 2):
            made = jnp.dot(
                weights, jnp.concatenate([both(n), both(n + 1)], axis=1), preferred_element_type=F32
            ).astype(BF16)
            for u in range(2):
                for e in range(entries):
                    bins[(n + u) * blocks : (n + u + 1) * blocks, e * T : (e + 1) * T] = made[
                        e * blocks : (e + 1) * blocks, u * T : (u + 1) * T
                    ]
        fetch.wait()
        whole[...] = jnp.dot(bins[...], library_ref[...].reshape(entries * T, T), preferred_element_type=F32)
        for m, out_ref in enumerate(outs):
            start = lax.rem(q_ref[0] + m, quarters) * held
            for t in range(held):
                out_ref[t] = whole[pl.ds(start + t, size, stride=blocks), :].astype(out_ref.dtype)
        for n in range(size):
            stripes[n * per : (n + 1) * per, :] = every[owner_ref[0] ^ n].astype(F32)
        for b in range(per):
            stripe_ref[b] = stripes[pl.ds(b, size, stride=per), :]

    return pl.pallas_call(
        kernel,
        out_shape=[
            *(jax.ShapeDtypeStruct((held, size, T), BF16 if m else F32) for m in range(quarters)),
            jax.ShapeDtypeStruct((per, size, T), F32),
        ],
        in_specs=[SMEM, SMEM, VMEM, VMEM, VMEM, HBM] + [VMEM] * len(bundles),
        out_specs=[VMEM] * (quarters + 1),
        scratch_shapes=[
            pltpu.VMEM(library.shape, BF16),
            pltpu.VMEM((owners, per, T), BF16),
            pltpu.VMEM((owners * per, T), F32),
            pltpu.VMEM((owners * size, T), F32),
            pltpu.VMEM((size * blocks, entries * T), BF16),
            pltpu.VMEM((size * blocks, T), F32),
            pltpu.SemaphoreType.DMA,
        ],
        compiler_params=params(),
        cost_estimate=pl.CostEstimate(
            flops=2 * 256 * size * T * T, bytes_accessed=8 * 2**20, transcendentals=0
        ),
        name="adjoint_tiles",
    )(quarter, owner, met, by_row, returned, in_hbm(library), *bundles)


def residual_call(phase, stripe, forward):
    per = stripe.shape[0]

    def kernel(phase_ref, stripe_ref, forward_ref, residual_ref):
        for b in range(per):
            where = slice(b * T, (b + 1) * T)
            corrected = (phase_ref[:, where].astype(F32) - stripe_ref[b]).astype(BF16)
            residual_ref[:, where] = (corrected.astype(F32) - forward_ref[:, where]).astype(BF16)

    return pl.pallas_call(
        kernel,
        out_shape=jax.ShapeDtypeStruct(phase.shape, BF16),
        in_specs=[VMEM] * 3,
        out_specs=VMEM,
        compiler_params=params(),
        cost_estimate=pl.CostEstimate(flops=2**19, bytes_accessed=2**21, transcendentals=0),
        name="residual",
    )(phase, stripe, forward)


def image_call(quarter, image, own, others):
    slices = image.shape[0]
    mine = own.shape[0]

    def kernel(q_ref, image_ref, own_ref, *refs):
        others_refs, out_ref = refs[:-1], refs[-1]
        for i in range(mine):
            total = own_ref[i]
            for ref in others_refs:
                total += ref[i].astype(F32)
            pixels = image_ref[:, lanes(q_ref[0] * mine + i)].astype(F32)
            out_ref[:, i * T : (i + 1) * T] = pixels + RELAX * total

    return pl.pallas_call(
        kernel,
        out_shape=jax.ShapeDtypeStruct((slices, mine * T), F32),
        in_specs=[SMEM, VMEM, VMEM] + [VMEM] * len(others),
        out_specs=VMEM,
        compiler_params=params(),
        cost_estimate=pl.CostEstimate(flops=2**18, bytes_accessed=2**20, transcendentals=0),
        name="image_step",
    )(quarter, image, own, *others)


def in_hbm(array):
    return pltpu.with_memory_space_constraint(array, pltpu.HBM)


def exchanged(array, axis):
    return lax.all_to_all(array, axis, split_axis=0, concat_axis=0, tiled=True)


def shards(projections, phase_kernel, image, tile_library, tile_entry, tile_image, tile_slot, tile_count, slot_block):
    projections = projections[0]
    library = tile_library[0, 0]
    image = image.T
    slices = projections.shape[0]
    quarters = lax.axis_size("ray")
    quarter = lax.axis_index("ray").astype(jnp.int32).reshape(1)
    tiles = (tile_entry[0], tile_image[0], tile_slot[0], tile_count)
    carried = slot_block[0]

    owners = lax.axis_size("dom")
    owner = lax.axis_index("dom").astype(jnp.int32).reshape(1)
    blocks = image.shape[1] // T

    def rims(head, tail):
        left = lax.ppermute(tail, "ray", [(i, i + 1) for i in range(quarters - 1)])
        right = lax.ppermute(head, "ray", [(i + 1, i) for i in range(quarters - 1)])
        return left, right

    def swapped(array, m):
        return lax.ppermute(array, "dom", [(i, i ^ m) for i in range(owners)])

    send, head, tail, row = first_call(*tiles, carried, projections, image, library)
    arrived = exchanged(send, "dom")
    rows = [row] + [swapped(row, m) for m in range(1, 8)]
    phase, band, stack = phase_call(projections, *rims(head, tail), phase_kernel, rows)
    forward, back, stack = back_call(carried, arrived, phase, stack)
    returned = exchanged(back, "dom")
    met, by_row = counts_call(*tiles, owner, stack, owners, library.shape[0], blocks)
    stripe = stripe_call(quarter, arrived, *rims(*rim_call(arrived, stack)), band, quarters)
    pair = joined_call([stripe, swapped(stripe, 1)])
    bundle = joined_call([pair] + [swapped(pair, m) for m in (2, 4, 6)], stack)
    twin = joined_call([bundle, swapped(bundle, 8)])
    bundles = [twin] + [swapped(twin, m) for m in (16, 32, 48)]
    own, *sent, stripe = adjoint_call(quarter, owner, met, by_row, returned, bundles, library, blocks, quarters)
    others = [
        lax.ppermute(part, "ray", [(i, (i + m) % quarters) for i in range(quarters)])
        for m, part in enumerate(sent, 1)
    ]
    residual = residual_call(phase, stripe, forward)
    image_next = image_call(quarter, image, own, others)
    return residual[None], image_next.T


def solution(mesh):
    return jax.shard_map(
        shards,
        mesh=mesh,
        in_specs=(
            P("dom", None, "ray"),
            P(),
            P("dom", None),
            P("dom", "ray", None, None, None),
            P("dom", "ray", None),
            P("dom", "ray", None),
            P("dom", "ray", None),
            P("dom", "ray"),
            P("dom", "ray", None),
        ),
        out_specs=(P("dom", None, "ray"), P(("dom", "ray"), None)),
        check_vma=False,
    )
```

```python
import jax
import jax.numpy as jnp
from jax import lax
from jax.experimental import pallas as pl
from jax.experimental.pallas import tpu as pltpu
from jax.sharding import PartitionSpec as P

T = 128
SMOOTH = 8
RELAX = 0.25
PER = 16
ROOM = 32
MIB = 2**20
F32, BF16 = jnp.float32, jnp.bfloat16
NT = (((1,), (1,)), ((), ()))
VMEM = pl.BlockSpec(memory_space=pltpu.VMEM)
SMEM = pl.BlockSpec(memory_space=pltpu.SMEM)
HBM = pl.BlockSpec(memory_space=pltpu.HBM)


def params(limit=32):
    return pltpu.CompilerParams(vmem_limit_bytes=limit * MIB)


def middle_network(n):
    pairs = []
    p = 1
    while p < n:
        k = p
        while k >= 1:
            for j in range(k % p, n - k, 2 * k):
                for i in range(min(k, n - j - k)):
                    if (i + j) // (2 * p) == (i + j + k) // (2 * p):
                        pairs.append((i + j, i + j + k))
            k //= 2
        p *= 2
    needed = {n // 2 - 1, n // 2}
    kept = []
    for a, b in reversed(pairs):
        if a in needed or b in needed:
            kept.append((a, b, a in needed, b in needed))
            needed |= {a, b}
    return kept[::-1]


def lanes(block):
    return pl.ds(pl.multiple_of(block * T, T), T)


def first_call(entry, place, slot, count, numbers, projections, image, library):
    slices, columns = projections.shape
    entries, capacity = library.shape[0], entry.shape[1]
    blocks = image.shape[1] // T
    owners = slices
    rows = slices + PER
    parts = 4
    loads = blocks + 6

    def kernel(
        entry_hbm, place_hbm, slot_hbm, count_ref, n_hbm, x_hbm, image_hbm, library_hbm,
        send_ref, head_ref, tail_ref, row_ref, entry_ref, place_ref, slot_ref, n_ref, library_ref, x_ref, spread,
        stacked, product, total, packed, section, sems, load_sems,
    ):
        pairs = [(x_hbm, x_ref), (n_hbm, n_ref), (library_hbm, library_ref)]
        pairs += [
            (image_hbm.at[:, pl.ds(i * T, T)], stacked.at[pl.ds(i * slices, slices)]) for i in range(blocks)
        ]
        pairs += [(entry_hbm, entry_ref), (place_hbm, place_ref), (slot_hbm, slot_ref)]
        fetches = [pltpu.make_async_copy(a, b, load_sems.at[n]) for n, (a, b) in enumerate(pairs)]
        for fetch in fetches:
            fetch.start()
        total[...] = jnp.zeros_like(total)
        row_ref[...] = jnp.zeros_like(row_ref)
        for fetch in fetches[:2]:
            fetch.wait()
        head_ref[...] = x_ref[:, :T]
        tail_ref[...] = x_ref[:, columns - T :]
        row_ref[0:1, :owners] = n_ref[...]
        for b in range(PER):
            spread[pl.ds(b, slices, stride=PER), :] = x_ref[:, b * T : (b + 1) * T].astype(F32)
        section[...] = spread[...].astype(BF16).reshape(slices, PER, T)
        copies = [pltpu.make_async_copy(section, send_ref.at[:, pl.ds(slices, PER), :], sems.at[parts])]
        copies[0].start()
        for fetch in fetches[2:]:
            fetch.wait()
        for e in range(0, entries, 2):
            product[:, e * T : (e + 2) * T] = lax.dot_general(
                stacked[...], library_ref[e : e + 2].reshape(2 * T, T), NT, preferred_element_type=F32
            )

        def add(k):
            live = k < count_ref[0, 0]
            e = jnp.where(live, entry_ref[0, k], 0)
            i = jnp.where(live, place_ref[0, k], 0)
            s = jnp.where(live, slot_ref[0, k], owners)
            total[s] += product[pl.ds(pl.multiple_of(i * slices, slices), slices), lanes(e)]

        def group(g, carry):
            for u in range(8):
                add(g * 8 + u)
            return carry

        lax.fori_loop(0, (count_ref[0, 0] + 7) // 8, group, 0)
        step = owners // parts
        for n in range(parts):
            packed[n * step : (n + 1) * step] = total[n * step : (n + 1) * step].astype(BF16)
            here = pl.ds(n * step, step)
            copies.append(
                pltpu.make_async_copy(packed.at[here], send_ref.at[here, pl.ds(0, slices), :], sems.at[n])
            )
            copies[-1].start()
        for copy in copies:
            copy.wait()

    return pl.pallas_call(
        kernel,
        out_shape=[
            pltpu.HBM((owners, rows, T), BF16),
            jax.ShapeDtypeStruct((slices, T), BF16),
            jax.ShapeDtypeStruct((slices, T), BF16),
            jax.ShapeDtypeStruct((8, T), jnp.int32),
        ],
        in_specs=[HBM] * 3 + [SMEM] + [HBM] * 4,
        out_specs=[HBM] + [VMEM] * 3,
        scratch_shapes=[
            pltpu.SMEM(entry.shape, jnp.int32),
            pltpu.SMEM(place.shape, jnp.int32),
            pltpu.SMEM(slot.shape, jnp.int32),
            pltpu.VMEM(numbers.shape, jnp.int32),
            pltpu.VMEM(library.shape, BF16),
            pltpu.VMEM((slices, columns), BF16),
            pltpu.VMEM((slices * PER, T), F32),
            pltpu.VMEM((blocks * slices, T), BF16),
            pltpu.VMEM((blocks * slices, entries * T), F32),
            pltpu.VMEM((owners + 1, slices, T), F32),
            pltpu.VMEM((owners, slices, T), BF16),
            pltpu.VMEM((slices, PER, T), BF16),
            pltpu.SemaphoreType.DMA((parts + 1,)),
            pltpu.SemaphoreType.DMA((loads,)),
        ],
        compiler_params=params(),
        cost_estimate=pl.CostEstimate(
            flops=2 * capacity * slices * T * T, bytes_accessed=8 * 2**20, transcendentals=0
        ),
        name="forward_tiles",
    )(*map(in_hbm, (entry, place, slot)), count, *map(in_hbm, (numbers, projections, image, library)))


def phase_call(projections, left, right, taps, rows):
    slices, columns = projections.shape
    per = columns // T

    def kernel(x_hbm, l_ref, r_ref, taps_hbm, *refs):
        n = len(rows)
        row_refs, (phase_ref, band_ref, stack_ref, taps_ref, line, wide, sems) = refs[:n], refs[n:]
        for m, ref in enumerate(row_refs):
            stack_ref[m : m + 1, :] = ref[0:1, :]
        fetches = [
            pltpu.make_async_copy(x_hbm, wide.at[:, pl.ds(T, columns)], sems.at[0]),
            pltpu.make_async_copy(taps_hbm, taps_ref, sems.at[1]),
        ]
        for fetch in fetches:
            fetch.start()
        wide[:, :T] = l_ref[...]
        wide[:, T + columns :] = r_ref[...]
        line[...] = jnp.zeros_like(line)
        for fetch in fetches:
            fetch.wait()
        line[0:1, : taps_ref.shape[0]] = taps_ref[...].astype(F32).reshape(1, -1)
        spun = pltpu.roll(jnp.broadcast_to(line[0:1, :], (T, 3 * T)), T // 2, 1, stride=1, stride_axis=0)
        band_ref[...] = spun.astype(BF16)
        for b in range(per):
            phase_ref[:, b * T : (b + 1) * T] = lax.dot_general(
                wide[:, b * T : (b + 3) * T], band_ref[...], NT, preferred_element_type=F32
            ).astype(BF16)

    return pl.pallas_call(
        kernel,
        out_shape=[
            jax.ShapeDtypeStruct((slices, columns), BF16),
            jax.ShapeDtypeStruct((T, 3 * T), BF16),
            jax.ShapeDtypeStruct((8, T), jnp.int32),
        ],
        in_specs=[HBM, VMEM, VMEM, HBM] + [VMEM] * len(rows),
        out_specs=[VMEM] * 3,
        scratch_shapes=[
            pltpu.VMEM(taps.shape, BF16),
            pltpu.VMEM((8, 3 * T), F32),
            pltpu.VMEM((slices, columns + 2 * T), BF16),
            pltpu.SemaphoreType.DMA((2,)),
        ],
        compiler_params=params(),
        cost_estimate=pl.CostEstimate(flops=2**26, bytes_accessed=2**20, transcendentals=0),
        name="phase_filter",
    )(in_hbm(projections), left, right, in_hbm(taps), *rows)


def rim_call(arrived, after):
    angles = arrived.shape[0]
    size = arrived.shape[1] - PER

    def kernel(arrived_ref, _, head_ref, tail_ref, flat):
        flat[...] = arrived_ref[:, size:, :].astype(F32).reshape(angles * PER, T)
        head_ref[...] = flat[pl.ds(0, angles, stride=PER), :].astype(BF16)
        tail_ref[...] = flat[pl.ds(PER - 1, angles, stride=PER), :].astype(BF16)

    return pl.pallas_call(
        kernel,
        out_shape=[jax.ShapeDtypeStruct((angles, T), BF16)] * 2,
        in_specs=[VMEM, VMEM],
        out_specs=[VMEM] * 2,
        scratch_shapes=[pltpu.VMEM((angles * PER, T), F32)],
        compiler_params=params(),
        cost_estimate=pl.CostEstimate(flops=2**17, bytes_accessed=2**18, transcendentals=0),
        name="rim",
    )(arrived, after)


def stripe_of(quarter, quarters, angles, values, rimmed):
    network = middle_network(angles)

    def middle(g, carry):
        v = [values[pl.ds(pl.multiple_of(a * ROOM + g * 8, 8), 8), :] for a in range(angles)]
        for a, b, low, high in network:
            x, y = v[a], v[b]
            if low:
                v[a] = jnp.minimum(x, y)
            if high:
                v[b] = jnp.maximum(x, y)
        rimmed[pl.ds(g * 8 + 1, 8), :] = (v[angles // 2 - 1] + v[angles // 2]) * 0.5
        return carry

    lax.fori_loop(0, 3, middle, 0)
    before, after = rimmed[17:18, :], rimmed[18:19, :]
    rimmed[0:1, :] = jnp.where(quarter == 0, jnp.zeros_like(before), before)
    rimmed[17:18, :] = jnp.where(quarter == quarters - 1, jnp.zeros_like(after), after)
    prev, cur, nxt = rimmed[0:16, :], rimmed[1:17, :], rimmed[2:18, :]
    lane = lax.broadcasted_iota(jnp.int32, (16, T), 1)
    total = cur
    for o in range(1, SMOOTH + 1):
        total += pltpu.roll(jnp.where(lane < o, nxt, cur), T - o, 1)
        total += pltpu.roll(jnp.where(lane >= T - o, prev, cur), o, 1)
    place = quarter * (16 * T) + lax.broadcasted_iota(jnp.int32, (16, T), 0) * T + lane
    last = quarters * 16 * T - 1
    count = jnp.minimum(place + SMOOTH, last) - jnp.maximum(place - SMOOTH, 0) + 1
    return cur - total / count.astype(F32)


def back_call(carried, arrived, phase, stacked):
    owners = arrived.shape[0]
    size, columns = phase.shape
    parts = 4

    def kernel(
        c_ref, arrived_ref, phase_ref, stacked_ref, forward_hbm, send_ref, stack_ref, forward, less, packed, sems
    ):
        forward[...] = jnp.zeros_like(forward)
        for d in range(owners):
            forward[:, lanes(c_ref[0, d])] += arrived_ref[d, :size, :].astype(F32)
        copies = [pltpu.make_async_copy(forward, forward_hbm, sems.at[parts])]
        copies[0].start()
        less[...] = (phase_ref[...].astype(F32) - forward[...]).astype(BF16)
        step = owners // parts
        for n in range(parts):
            for d in range(n * step, (n + 1) * step):
                packed[d] = less[:, lanes(c_ref[0, d])]
            here = pl.ds(n * step, step)
            copies.append(pltpu.make_async_copy(packed.at[here], send_ref.at[here], sems.at[n]))
            copies[-1].start()
        stack_ref[...] = stacked_ref[...]
        for copy in copies:
            copy.wait()

    return pl.pallas_call(
        kernel,
        out_shape=[
            pltpu.HBM((size, columns), F32),
            pltpu.HBM((owners, size, T), BF16),
            jax.ShapeDtypeStruct((8, T), jnp.int32),
        ],
        in_specs=[SMEM] + [VMEM] * 3,
        out_specs=[HBM, HBM, VMEM],
        scratch_shapes=[
            pltpu.VMEM((size, columns), F32),
            pltpu.VMEM((size, columns), BF16),
            pltpu.VMEM((owners, size, T), BF16),
            pltpu.SemaphoreType.DMA((parts + 1,)),
        ],
        compiler_params=params(),
        cost_estimate=pl.CostEstimate(flops=2**24, bytes_accessed=8 * 2**20, transcendentals=0),
        name="slot_sums",
    )(carried, arrived, phase, stacked)


def stripe_call(quarter, arrived, left, right, band, quarters):
    angles = arrived.shape[0]
    size = arrived.shape[1] - PER

    def kernel(
        q_ref, arrived_ref, l_ref, r_ref, band_ref, stripe_ref, flat, wide, values, rimmed
    ):
        def block(n):
            return pl.ds(n * angles, angles)

        flat[...] = arrived_ref[:, size:, :].astype(F32).reshape(angles * PER, T)
        for b in range(PER):
            wide[block(b + 2), :] = flat[pl.ds(b, angles, stride=PER), :].astype(BF16)
        wide[block(0), :] = jnp.zeros((angles, T), BF16)
        wide[block(1), :] = l_ref[...]
        wide[block(PER + 2), :] = r_ref[...]
        wide[block(PER + 3), :] = jnp.zeros((angles, T), BF16)
        values[...] = jnp.zeros_like(values)
        filtered = sum(
            lax.dot_general(
                wide[n * angles : (n + PER + 2) * angles, :],
                band_ref[:, n * T : (n + 1) * T],
                NT,
                preferred_element_type=F32,
            )
            for n in range(3)
        ).astype(BF16)
        for at, b in enumerate([*range(1, PER + 1), 0, PER + 1]):
            values[pl.ds(at, angles, stride=ROOM), :] = filtered[b * angles : (b + 1) * angles].astype(F32)
        stripe_ref[0] = stripe_of(q_ref[0], quarters, angles, values, rimmed).astype(BF16)

    return pl.pallas_call(
        kernel,
        out_shape=jax.ShapeDtypeStruct((1, PER, T), BF16),
        in_specs=[SMEM] + [VMEM] * 4,
        out_specs=VMEM,
        scratch_shapes=[
            pltpu.VMEM((angles * PER, T), F32),
            pltpu.VMEM(((PER + 4) * angles, T), BF16),
            pltpu.VMEM((angles * ROOM, T), F32),
            pltpu.VMEM((32, T), F32),
        ],
        compiler_params=params(),
        cost_estimate=pl.CostEstimate(flops=2**26, bytes_accessed=2**20, transcendentals=0),
        name="stripe",
    )(quarter, arrived, left, right, band)


def joined_call(arrays, stack=None):
    lengths = [array.shape[0] for array in arrays]
    whole = sum(lengths)
    given = list(arrays) + ([] if stack is None else [stack])

    def kernel(*refs):
        out_ref = refs[-1]
        start = 0
        for ref, length in zip(refs, lengths):
            out_ref[start : start + length] = ref[...]
            start += length
        if stack is not None:
            numbers = refs[-2][...].astype(F32)
            out_ref[whole] = jnp.concatenate([numbers, jnp.zeros_like(numbers)], axis=0).astype(BF16)

    return pl.pallas_call(
        kernel,
        out_shape=jax.ShapeDtypeStruct((whole + (stack is not None), PER, T), BF16),
        in_specs=[VMEM] * len(given),
        out_specs=VMEM,
        compiler_params=params(),
        cost_estimate=pl.CostEstimate(flops=2**15, bytes_accessed=2**16, transcendentals=0),
        name="joined",
    )(*given)


def counts_call(entry, place, slot, count, owner, after, owners, entries, blocks):
    capacity = entry.shape[1]

    def kernel(
        entry_hbm, place_hbm, slot_hbm, count_ref, owner_ref, _,
        met_ref, by_row_ref, entry_ref, place_ref, slot_ref, loads,
    ):
        pairs = [(entry_hbm, entry_ref), (place_hbm, place_ref), (slot_hbm, slot_ref)]
        fetches = [pltpu.make_async_copy(a, b, loads.at[n]) for n, (a, b) in enumerate(pairs)]
        for fetch in fetches:
            fetch.start()

        def ones(rows, match):
            return (lax.broadcasted_iota(jnp.int32, (rows, match.shape[1]), 0) == match).astype(F32).astype(BF16)

        for fetch in fetches:
            fetch.wait()
        live = lax.broadcasted_iota(jnp.int32, (1, capacity), 1) < count_ref[0, 0]
        of_bin = ones(entries * blocks, jnp.where(live, entry_ref[...] * blocks + place_ref[...], -1))
        met = lax.dot_general(of_bin, ones(T, slot_ref[...]), NT, preferred_element_type=F32)
        met_ref[...] = met.astype(BF16)
        k = lax.broadcasted_iota(jnp.int32, (T, capacity), 0)
        by_row = (k < owners) & ((owner_ref[0] ^ k) == slot_ref[...])
        by_row = lax.dot_general(of_bin, by_row.astype(F32).astype(BF16), NT, preferred_element_type=F32)
        by_row_ref[...] = by_row.astype(BF16)

    return pl.pallas_call(
        kernel,
        out_shape=[jax.ShapeDtypeStruct((entries * blocks, T), BF16)] * 2,
        in_specs=[HBM] * 3 + [SMEM, SMEM, VMEM],
        out_specs=[VMEM, VMEM],
        scratch_shapes=[
            pltpu.VMEM(entry.shape, jnp.int32),
            pltpu.VMEM(place.shape, jnp.int32),
            pltpu.VMEM(slot.shape, jnp.int32),
            pltpu.SemaphoreType.DMA((3,)),
        ],
        compiler_params=params(),
        cost_estimate=pl.CostEstimate(flops=2**24, bytes_accessed=2**20, transcendentals=0),
        name="tile_counts",
    )(*map(in_hbm, (entry, place, slot)), count, owner, after)


def adjoint_call(quarter, owner, met, by_row, returned, bundles, library, blocks, quarters):
    entries = library.shape[0]
    owners = returned.shape[0]
    per = PER
    size = returned.shape[1]
    near = 8
    each = bundles[0].shape[0] // (near + 1)
    held = blocks // quarters

    def kernel(q_ref, owner_ref, met_ref, by_row_ref, returned_ref, library_hbm, *refs):
        bundle_refs, refs = refs[: len(bundles)], refs[len(bundles) :]
        outs, refs = refs[:quarters], refs[quarters:]
        stripe_ref, library_ref, every, stripes, terms, bins, whole, load = refs
        fetch = pltpu.make_async_copy(library_hbm, library_ref, load)
        fetch.start()
        terms[...] = returned_ref[...].astype(F32).reshape(owners * size, T)
        numbers = []
        for ref in bundle_refs:
            for t in range(0, each * (near + 1), near + 1):
                m = len(numbers)
                every[m * near : (m + 1) * near] = ref[t : t + near]
                numbers.append(ref[t + near].astype(F32)[:near])
        numbers = jnp.concatenate(numbers, axis=0)
        lane = lax.broadcasted_iota(jnp.int32, (owners, T), 1)
        theirs = jnp.sum(jnp.where(lane == owner_ref[0], numbers, 0.0), axis=1, keepdims=True)
        carries = (theirs.astype(jnp.int32) + owners == lane).astype(F32).astype(BF16)
        stripe_met = jnp.dot(by_row_ref[:, :owners], carries, preferred_element_type=F32)
        weights = (met_ref[...].astype(F32) - stripe_met).astype(BF16)[:, : owners + per]

        def both(n):
            here = terms[pl.ds(n, owners, stride=size), :].astype(BF16)
            return jnp.concatenate([here, every[owner_ref[0] ^ n]], axis=0)

        for n in range(0, size, 2):
            made = jnp.dot(
                weights, jnp.concatenate([both(n), both(n + 1)], axis=1), preferred_element_type=F32
            ).astype(BF16)
            for u in range(2):
                for e in range(entries):
                    bins[(n + u) * blocks : (n + u + 1) * blocks, e * T : (e + 1) * T] = made[
                        e * blocks : (e + 1) * blocks, u * T : (u + 1) * T
                    ]
        fetch.wait()
        whole[...] = jnp.dot(bins[...], library_ref[...].reshape(entries * T, T), preferred_element_type=F32)
        for m, out_ref in enumerate(outs):
            start = lax.rem(q_ref[0] + m, quarters) * held
            for t in range(held):
                out_ref[t] = whole[pl.ds(start + t, size, stride=blocks), :].astype(out_ref.dtype)
        for n in range(size):
            stripes[n * per : (n + 1) * per, :] = every[owner_ref[0] ^ n].astype(F32)
        for b in range(per):
            stripe_ref[b] = stripes[pl.ds(b, size, stride=per), :]

    return pl.pallas_call(
        kernel,
        out_shape=[
            *(jax.ShapeDtypeStruct((held, size, T), BF16 if m else F32) for m in range(quarters)),
            jax.ShapeDtypeStruct((per, size, T), F32),
        ],
        in_specs=[SMEM, SMEM, VMEM, VMEM, VMEM, HBM] + [VMEM] * len(bundles),
        out_specs=[VMEM] * (quarters + 1),
        scratch_shapes=[
            pltpu.VMEM(library.shape, BF16),
            pltpu.VMEM((owners, per, T), BF16),
            pltpu.VMEM((owners * per, T), F32),
            pltpu.VMEM((owners * size, T), F32),
            pltpu.VMEM((size * blocks, entries * T), BF16),
            pltpu.VMEM((size * blocks, T), F32),
            pltpu.SemaphoreType.DMA,
        ],
        compiler_params=params(),
        cost_estimate=pl.CostEstimate(
            flops=2 * 256 * size * T * T, bytes_accessed=8 * 2**20, transcendentals=0
        ),
        name="adjoint_tiles",
    )(quarter, owner, met, by_row, returned, in_hbm(library), *bundles)


def residual_call(phase, stripe, forward):
    per = stripe.shape[0]

    def kernel(phase_ref, stripe_ref, forward_ref, residual_ref):
        for b in range(per):
            where = slice(b * T, (b + 1) * T)
            corrected = (phase_ref[:, where].astype(F32) - stripe_ref[b]).astype(BF16)
            residual_ref[:, where] = (corrected.astype(F32) - forward_ref[:, where]).astype(BF16)

    return pl.pallas_call(
        kernel,
        out_shape=jax.ShapeDtypeStruct(phase.shape, BF16),
        in_specs=[VMEM] * 3,
        out_specs=VMEM,
        compiler_params=params(),
        cost_estimate=pl.CostEstimate(flops=2**19, bytes_accessed=2**21, transcendentals=0),
        name="residual",
    )(phase, stripe, forward)


def image_call(quarter, image, own, others):
    slices = image.shape[0]
    mine = own.shape[0]

    def kernel(q_ref, image_ref, own_ref, *refs):
        others_refs, out_ref = refs[:-1], refs[-1]
        for i in range(mine):
            total = own_ref[i]
            for ref in others_refs:
                total += ref[i].astype(F32)
            pixels = image_ref[:, lanes(q_ref[0] * mine + i)].astype(F32)
            out_ref[:, i * T : (i + 1) * T] = pixels + RELAX * total

    return pl.pallas_call(
        kernel,
        out_shape=jax.ShapeDtypeStruct((slices, mine * T), F32),
        in_specs=[SMEM, VMEM, VMEM] + [VMEM] * len(others),
        out_specs=VMEM,
        compiler_params=params(),
        cost_estimate=pl.CostEstimate(flops=2**18, bytes_accessed=2**20, transcendentals=0),
        name="image_step",
    )(quarter, image, own, *others)


def in_hbm(array):
    return pltpu.with_memory_space_constraint(array, pltpu.HBM)


def exchanged(array, axis):
    return lax.all_to_all(array, axis, split_axis=0, concat_axis=0, tiled=True)


def shards(projections, phase_kernel, image, tile_library, tile_entry, tile_image, tile_slot, tile_count, slot_block):
    projections = projections[0]
    library = tile_library[0, 0]
    image = image.T
    slices = projections.shape[0]
    quarters = lax.axis_size("ray")
    quarter = lax.axis_index("ray").astype(jnp.int32).reshape(1)
    tiles = (tile_entry[0], tile_image[0], tile_slot[0], tile_count)
    carried = slot_block[0]

    owners = lax.axis_size("dom")
    owner = lax.axis_index("dom").astype(jnp.int32).reshape(1)
    blocks = image.shape[1] // T

    def rims(head, tail):
        left = lax.ppermute(tail, "ray", [(i, i + 1) for i in range(quarters - 1)])
        right = lax.ppermute(head, "ray", [(i + 1, i) for i in range(quarters - 1)])
        return left, right

    def swapped(array, m):
        return lax.ppermute(array, "dom", [(i, i ^ m) for i in range(owners)])

    send, head, tail, row = first_call(*tiles, carried, projections, image, library)
    arrived = exchanged(send, "dom")
    rows = [row] + [swapped(row, m) for m in range(1, 8)]
    phase, band, stack = phase_call(projections, *rims(head, tail), phase_kernel, rows)
    forward, back, stack = back_call(carried, arrived, phase, stack)
    returned = exchanged(back, "dom")
    met, by_row = counts_call(*tiles, owner, stack, owners, library.shape[0], blocks)
    stripe = stripe_call(quarter, arrived, *rims(*rim_call(arrived, stack)), band, quarters)
    pair = joined_call([stripe, swapped(stripe, 1)])
    quad = joined_call([pair, swapped(pair, 2)])
    bundle = joined_call([quad, swapped(quad, 4)], stack)
    twin = joined_call([bundle, swapped(bundle, 8)])
    bundles = [twin] + [swapped(twin, m) for m in (16, 32, 48)]
    own, *sent, stripe = adjoint_call(quarter, owner, met, by_row, returned, bundles, library, blocks, quarters)
    others = [
        lax.ppermute(part, "ray", [(i, (i + m) % quarters) for i in range(quarters)])
        for m, part in enumerate(sent, 1)
    ]
    residual = residual_call(phase, stripe, forward)
    image_next = image_call(quarter, image, own, others)
    return residual[None], image_next.T


def solution(mesh):
    return jax.shard_map(
        shards,
        mesh=mesh,
        in_specs=(
            P("dom", None, "ray"),
            P(),
            P("dom", None),
            P("dom", "ray", None, None, None),
            P("dom", "ray", None),
            P("dom", "ray", None),
            P("dom", "ray", None),
            P("dom", "ray"),
            P("dom", "ray", None),
        ),
        out_specs=(P("dom", None, "ray"), P(("dom", "ray"), None)),
        check_vma=False,
    )
```

```python
import jax
import jax.numpy as jnp
from jax import lax
from jax.experimental import pallas as pl
from jax.experimental.pallas import tpu as pltpu
from jax.sharding import PartitionSpec as P

T = 128
SMOOTH = 8
RELAX = 0.25
PER = 16
ROOM = 32
MIB = 2**20
F32, BF16 = jnp.float32, jnp.bfloat16
NT = (((1,), (1,)), ((), ()))
VMEM = pl.BlockSpec(memory_space=pltpu.VMEM)
SMEM = pl.BlockSpec(memory_space=pltpu.SMEM)
HBM = pl.BlockSpec(memory_space=pltpu.HBM)


def params(limit=32):
    return pltpu.CompilerParams(vmem_limit_bytes=limit * MIB)


def middle_network(n):
    pairs = []
    p = 1
    while p < n:
        k = p
        while k >= 1:
            for j in range(k % p, n - k, 2 * k):
                for i in range(min(k, n - j - k)):
                    if (i + j) // (2 * p) == (i + j + k) // (2 * p):
                        pairs.append((i + j, i + j + k))
            k //= 2
        p *= 2
    needed = {n // 2 - 1, n // 2}
    kept = []
    for a, b in reversed(pairs):
        if a in needed or b in needed:
            kept.append((a, b, a in needed, b in needed))
            needed |= {a, b}
    return kept[::-1]


def lanes(block):
    return pl.ds(pl.multiple_of(block * T, T), T)


def first_call(entry, place, slot, count, numbers, projections, image, library):
    slices, columns = projections.shape
    entries, capacity = library.shape[0], entry.shape[1]
    blocks = image.shape[1] // T
    owners = slices
    rows = slices + PER
    parts = 4
    loads = blocks + 6

    def kernel(
        entry_hbm, place_hbm, slot_hbm, count_ref, n_hbm, x_hbm, image_hbm, library_hbm,
        send_ref, head_ref, tail_ref, row_ref, entry_ref, place_ref, slot_ref, n_ref, library_ref, x_ref, spread,
        stacked, product, total, packed, section, sems, load_sems,
    ):
        pairs = [(x_hbm, x_ref), (n_hbm, n_ref), (library_hbm, library_ref)]
        pairs += [
            (image_hbm.at[:, pl.ds(i * T, T)], stacked.at[pl.ds(i * slices, slices)]) for i in range(blocks)
        ]
        pairs += [(entry_hbm, entry_ref), (place_hbm, place_ref), (slot_hbm, slot_ref)]
        fetches = [pltpu.make_async_copy(a, b, load_sems.at[n]) for n, (a, b) in enumerate(pairs)]
        for fetch in fetches:
            fetch.start()
        total[...] = jnp.zeros_like(total)
        row_ref[...] = jnp.zeros_like(row_ref)
        for fetch in fetches[:2]:
            fetch.wait()
        head_ref[...] = x_ref[:, :T]
        tail_ref[...] = x_ref[:, columns - T :]
        row_ref[0:1, :owners] = n_ref[...]
        for b in range(PER):
            spread[pl.ds(b, slices, stride=PER), :] = x_ref[:, b * T : (b + 1) * T].astype(F32)
        section[...] = spread[...].astype(BF16).reshape(slices, PER, T)
        copies = [pltpu.make_async_copy(section, send_ref.at[:, pl.ds(slices, PER), :], sems.at[parts])]
        copies[0].start()
        for fetch in fetches[2:]:
            fetch.wait()
        for e in range(0, entries, 2):
            product[:, e * T : (e + 2) * T] = lax.dot_general(
                stacked[...], library_ref[e : e + 2].reshape(2 * T, T), NT, preferred_element_type=F32
            )

        def add(k):
            live = k < count_ref[0, 0]
            e = jnp.where(live, entry_ref[0, k], 0)
            i = jnp.where(live, place_ref[0, k], 0)
            s = jnp.where(live, slot_ref[0, k], owners)
            total[s] += product[pl.ds(pl.multiple_of(i * slices, slices), slices), lanes(e)]

        def group(g, carry):
            for u in range(8):
                add(g * 8 + u)
            return carry

        lax.fori_loop(0, (count_ref[0, 0] + 7) // 8, group, 0)
        step = owners // parts
        for n in range(parts):
            packed[n * step : (n + 1) * step] = total[n * step : (n + 1) * step].astype(BF16)
            here = pl.ds(n * step, step)
            copies.append(
                pltpu.make_async_copy(packed.at[here], send_ref.at[here, pl.ds(0, slices), :], sems.at[n])
            )
            copies[-1].start()
        for copy in copies:
            copy.wait()

    return pl.pallas_call(
        kernel,
        out_shape=[
            pltpu.HBM((owners, rows, T), BF16),
            jax.ShapeDtypeStruct((slices, T), BF16),
            jax.ShapeDtypeStruct((slices, T), BF16),
            jax.ShapeDtypeStruct((8, T), jnp.int32),
        ],
        in_specs=[HBM] * 3 + [SMEM] + [HBM] * 4,
        out_specs=[HBM] + [VMEM] * 3,
        scratch_shapes=[
            pltpu.SMEM(entry.shape, jnp.int32),
            pltpu.SMEM(place.shape, jnp.int32),
            pltpu.SMEM(slot.shape, jnp.int32),
            pltpu.VMEM(numbers.shape, jnp.int32),
            pltpu.VMEM(library.shape, BF16),
            pltpu.VMEM((slices, columns), BF16),
            pltpu.VMEM((slices * PER, T), F32),
            pltpu.VMEM((blocks * slices, T), BF16),
            pltpu.VMEM((blocks * slices, entries * T), F32),
            pltpu.VMEM((owners + 1, slices, T), F32),
            pltpu.VMEM((owners, slices, T), BF16),
            pltpu.VMEM((slices, PER, T), BF16),
            pltpu.SemaphoreType.DMA((parts + 1,)),
            pltpu.SemaphoreType.DMA((loads,)),
        ],
        compiler_params=params(),
        cost_estimate=pl.CostEstimate(
            flops=2 * capacity * slices * T * T, bytes_accessed=8 * 2**20, transcendentals=0
        ),
        name="forward_tiles",
    )(*map(in_hbm, (entry, place, slot)), count, *map(in_hbm, (numbers, projections, image, library)))


def phase_call(projections, left, right, taps, rows):
    slices, columns = projections.shape
    per = columns // T

    def kernel(x_hbm, l_ref, r_ref, taps_hbm, *refs):
        n = len(rows)
        row_refs, (phase_ref, band_ref, stack_ref, taps_ref, line, wide, sems) = refs[:n], refs[n:]
        for m, ref in enumerate(row_refs):
            stack_ref[m : m + 1, :] = ref[0:1, :]
        fetches = [
            pltpu.make_async_copy(x_hbm, wide.at[:, pl.ds(T, columns)], sems.at[0]),
            pltpu.make_async_copy(taps_hbm, taps_ref, sems.at[1]),
        ]
        for fetch in fetches:
            fetch.start()
        wide[:, :T] = l_ref[...]
        wide[:, T + columns :] = r_ref[...]
        line[...] = jnp.zeros_like(line)
        for fetch in fetches:
            fetch.wait()
        line[0:1, : taps_ref.shape[0]] = taps_ref[...].astype(F32).reshape(1, -1)
        spun = pltpu.roll(jnp.broadcast_to(line[0:1, :], (T, 3 * T)), T // 2, 1, stride=1, stride_axis=0)
        band_ref[...] = spun.astype(BF16)
        for b in range(per):
            phase_ref[:, b * T : (b + 1) * T] = lax.dot_general(
                wide[:, b * T : (b + 3) * T], band_ref[...], NT, preferred_element_type=F32
            ).astype(BF16)

    return pl.pallas_call(
        kernel,
        out_shape=[
            jax.ShapeDtypeStruct((slices, columns), BF16),
            jax.ShapeDtypeStruct((T, 3 * T), BF16),
            jax.ShapeDtypeStruct((8, T), jnp.int32),
        ],
        in_specs=[HBM, VMEM, VMEM, HBM] + [VMEM] * len(rows),
        out_specs=[VMEM] * 3,
        scratch_shapes=[
            pltpu.VMEM(taps.shape, BF16),
            pltpu.VMEM((8, 3 * T), F32),
            pltpu.VMEM((slices, columns + 2 * T), BF16),
            pltpu.SemaphoreType.DMA((2,)),
        ],
        compiler_params=params(),
        cost_estimate=pl.CostEstimate(flops=2**26, bytes_accessed=2**20, transcendentals=0),
        name="phase_filter",
    )(in_hbm(projections), left, right, in_hbm(taps), *rows)


def rim_call(arrived, after):
    angles = arrived.shape[0]
    size = arrived.shape[1] - PER

    def kernel(arrived_ref, _, head_ref, tail_ref, flat):
        flat[...] = arrived_ref[:, size:, :].astype(F32).reshape(angles * PER, T)
        head_ref[...] = flat[pl.ds(0, angles, stride=PER), :].astype(BF16)
        tail_ref[...] = flat[pl.ds(PER - 1, angles, stride=PER), :].astype(BF16)

    return pl.pallas_call(
        kernel,
        out_shape=[jax.ShapeDtypeStruct((angles, T), BF16)] * 2,
        in_specs=[VMEM, VMEM],
        out_specs=[VMEM] * 2,
        scratch_shapes=[pltpu.VMEM((angles * PER, T), F32)],
        compiler_params=params(),
        cost_estimate=pl.CostEstimate(flops=2**17, bytes_accessed=2**18, transcendentals=0),
        name="rim",
    )(arrived, after)


def stripe_of(quarter, quarters, angles, values, rimmed):
    network = middle_network(angles)

    def middle(g, carry):
        v = [values[pl.ds(pl.multiple_of(a * ROOM + g * 8, 8), 8), :] for a in range(angles)]
        for a, b, low, high in network:
            x, y = v[a], v[b]
            if low:
                v[a] = jnp.minimum(x, y)
            if high:
                v[b] = jnp.maximum(x, y)
        rimmed[pl.ds(g * 8 + 1, 8), :] = (v[angles // 2 - 1] + v[angles // 2]) * 0.5
        return carry

    lax.fori_loop(0, 3, middle, 0)
    before, after = rimmed[17:18, :], rimmed[18:19, :]
    rimmed[0:1, :] = jnp.where(quarter == 0, jnp.zeros_like(before), before)
    rimmed[17:18, :] = jnp.where(quarter == quarters - 1, jnp.zeros_like(after), after)
    prev, cur, nxt = rimmed[0:16, :], rimmed[1:17, :], rimmed[2:18, :]
    lane = lax.broadcasted_iota(jnp.int32, (16, T), 1)
    total = cur
    for o in range(1, SMOOTH + 1):
        total += pltpu.roll(jnp.where(lane < o, nxt, cur), T - o, 1)
        total += pltpu.roll(jnp.where(lane >= T - o, prev, cur), o, 1)
    place = quarter * (16 * T) + lax.broadcasted_iota(jnp.int32, (16, T), 0) * T + lane
    last = quarters * 16 * T - 1
    count = jnp.minimum(place + SMOOTH, last) - jnp.maximum(place - SMOOTH, 0) + 1
    return cur - total / count.astype(F32)


def back_call(carried, arrived, phase, stacked):
    owners = arrived.shape[0]
    size, columns = phase.shape
    parts = 4

    def kernel(
        c_ref, arrived_ref, phase_ref, stacked_ref, forward_hbm, send_ref, stack_ref, forward, less, packed, sems
    ):
        forward[...] = jnp.zeros_like(forward)
        for d in range(owners):
            forward[:, lanes(c_ref[0, d])] += arrived_ref[d, :size, :].astype(F32)
        copies = [pltpu.make_async_copy(forward, forward_hbm, sems.at[parts])]
        copies[0].start()
        less[...] = (phase_ref[...].astype(F32) - forward[...]).astype(BF16)
        step = owners // parts
        for n in range(parts):
            for d in range(n * step, (n + 1) * step):
                packed[d] = less[:, lanes(c_ref[0, d])]
            here = pl.ds(n * step, step)
            copies.append(pltpu.make_async_copy(packed.at[here], send_ref.at[here], sems.at[n]))
            copies[-1].start()
        stack_ref[...] = stacked_ref[...]
        for copy in copies:
            copy.wait()

    return pl.pallas_call(
        kernel,
        out_shape=[
            pltpu.HBM((size, columns), F32),
            pltpu.HBM((owners, size, T), BF16),
            jax.ShapeDtypeStruct((8, T), jnp.int32),
        ],
        in_specs=[SMEM] + [VMEM] * 3,
        out_specs=[HBM, HBM, VMEM],
        scratch_shapes=[
            pltpu.VMEM((size, columns), F32),
            pltpu.VMEM((size, columns), BF16),
            pltpu.VMEM((owners, size, T), BF16),
            pltpu.SemaphoreType.DMA((parts + 1,)),
        ],
        compiler_params=params(),
        cost_estimate=pl.CostEstimate(flops=2**24, bytes_accessed=8 * 2**20, transcendentals=0),
        name="slot_sums",
    )(carried, arrived, phase, stacked)


def stripe_call(quarter, arrived, left, right, band, quarters):
    angles = arrived.shape[0]
    size = arrived.shape[1] - PER

    def kernel(
        q_ref, arrived_ref, l_ref, r_ref, band_ref, stripe_ref, flat, wide, values, rimmed
    ):
        def block(n):
            return pl.ds(n * angles, angles)

        flat[...] = arrived_ref[:, size:, :].astype(F32).reshape(angles * PER, T)
        for b in range(PER):
            wide[block(b + 2), :] = flat[pl.ds(b, angles, stride=PER), :].astype(BF16)
        wide[block(0), :] = jnp.zeros((angles, T), BF16)
        wide[block(1), :] = l_ref[...]
        wide[block(PER + 2), :] = r_ref[...]
        wide[block(PER + 3), :] = jnp.zeros((angles, T), BF16)
        values[...] = jnp.zeros_like(values)
        filtered = sum(
            lax.dot_general(
                wide[n * angles : (n + PER + 2) * angles, :],
                band_ref[:, n * T : (n + 1) * T],
                NT,
                preferred_element_type=F32,
            )
            for n in range(3)
        ).astype(BF16)
        for at, b in enumerate([*range(1, PER + 1), 0, PER + 1]):
            values[pl.ds(at, angles, stride=ROOM), :] = filtered[b * angles : (b + 1) * angles].astype(F32)
        stripe_ref[0] = stripe_of(q_ref[0], quarters, angles, values, rimmed).astype(BF16)

    return pl.pallas_call(
        kernel,
        out_shape=jax.ShapeDtypeStruct((1, PER, T), BF16),
        in_specs=[SMEM] + [VMEM] * 4,
        out_specs=VMEM,
        scratch_shapes=[
            pltpu.VMEM((angles * PER, T), F32),
            pltpu.VMEM(((PER + 4) * angles, T), BF16),
            pltpu.VMEM((angles * ROOM, T), F32),
            pltpu.VMEM((32, T), F32),
        ],
        compiler_params=params(),
        cost_estimate=pl.CostEstimate(flops=2**26, bytes_accessed=2**20, transcendentals=0),
        name="stripe",
    )(quarter, arrived, left, right, band)


def joined_call(arrays, stack=None):
    lengths = [array.shape[0] for array in arrays]
    whole = sum(lengths)
    given = list(arrays) + ([] if stack is None else [stack])

    def kernel(*refs):
        out_ref = refs[-1]
        start = 0
        for ref, length in zip(refs, lengths):
            out_ref[start : start + length] = ref[...]
            start += length
        if stack is not None:
            numbers = refs[-2][...].astype(F32)
            out_ref[whole] = jnp.concatenate([numbers, jnp.zeros_like(numbers)], axis=0).astype(BF16)

    return pl.pallas_call(
        kernel,
        out_shape=jax.ShapeDtypeStruct((whole + (stack is not None), PER, T), BF16),
        in_specs=[VMEM] * len(given),
        out_specs=VMEM,
        compiler_params=params(),
        cost_estimate=pl.CostEstimate(flops=2**15, bytes_accessed=2**16, transcendentals=0),
        name="joined",
    )(*given)


def counts_call(entry, place, slot, count, owner, after, owners, entries, blocks):
    capacity = entry.shape[1]

    def kernel(
        entry_hbm, place_hbm, slot_hbm, count_ref, owner_ref, _,
        met_ref, by_row_ref, entry_ref, place_ref, slot_ref, loads,
    ):
        pairs = [(entry_hbm, entry_ref), (place_hbm, place_ref), (slot_hbm, slot_ref)]
        fetches = [pltpu.make_async_copy(a, b, loads.at[n]) for n, (a, b) in enumerate(pairs)]
        for fetch in fetches:
            fetch.start()

        def ones(rows, match):
            return (lax.broadcasted_iota(jnp.int32, (rows, match.shape[1]), 0) == match).astype(F32).astype(BF16)

        for fetch in fetches:
            fetch.wait()
        live = lax.broadcasted_iota(jnp.int32, (1, capacity), 1) < count_ref[0, 0]
        of_bin = ones(entries * blocks, jnp.where(live, entry_ref[...] * blocks + place_ref[...], -1))
        met = lax.dot_general(of_bin, ones(T, slot_ref[...]), NT, preferred_element_type=F32)
        met_ref[...] = met.astype(BF16)
        k = lax.broadcasted_iota(jnp.int32, (T, capacity), 0)
        by_row = (k < owners) & ((owner_ref[0] ^ k) == slot_ref[...])
        by_row = lax.dot_general(of_bin, by_row.astype(F32).astype(BF16), NT, preferred_element_type=F32)
        by_row_ref[...] = by_row.astype(BF16)

    return pl.pallas_call(
        kernel,
        out_shape=[jax.ShapeDtypeStruct((entries * blocks, T), BF16)] * 2,
        in_specs=[HBM] * 3 + [SMEM, SMEM, VMEM],
        out_specs=[VMEM, VMEM],
        scratch_shapes=[
            pltpu.VMEM(entry.shape, jnp.int32),
            pltpu.VMEM(place.shape, jnp.int32),
            pltpu.VMEM(slot.shape, jnp.int32),
            pltpu.SemaphoreType.DMA((3,)),
        ],
        compiler_params=params(),
        cost_estimate=pl.CostEstimate(flops=2**24, bytes_accessed=2**20, transcendentals=0),
        name="tile_counts",
    )(*map(in_hbm, (entry, place, slot)), count, owner, after)


def adjoint_call(quarter, owner, met, by_row, returned, bundles, library, blocks, quarters):
    entries = library.shape[0]
    owners = returned.shape[0]
    per = PER
    size = returned.shape[1]
    near = 8
    each = bundles[0].shape[0] // (near + 1)
    held = blocks // quarters

    def kernel(q_ref, owner_ref, met_ref, by_row_ref, returned_ref, library_hbm, *refs):
        bundle_refs, refs = refs[: len(bundles)], refs[len(bundles) :]
        outs, refs = refs[:quarters], refs[quarters:]
        stripe_ref, library_ref, every, stripes, terms, bins, whole, load = refs
        fetch = pltpu.make_async_copy(library_hbm, library_ref, load)
        fetch.start()
        terms[...] = returned_ref[...].astype(F32).reshape(owners * size, T)
        numbers = []
        for t in range(0, each * (near + 1), near + 1):
            for ref in bundle_refs:
                m = len(numbers)
                every[m * near : (m + 1) * near] = ref[t : t + near]
                numbers.append(ref[t + near].astype(F32)[:near])
        numbers = jnp.concatenate(numbers, axis=0)
        lane = lax.broadcasted_iota(jnp.int32, (owners, T), 1)
        theirs = jnp.sum(jnp.where(lane == owner_ref[0], numbers, 0.0), axis=1, keepdims=True)
        carries = (theirs.astype(jnp.int32) + owners == lane).astype(F32).astype(BF16)
        stripe_met = jnp.dot(by_row_ref[:, :owners], carries, preferred_element_type=F32)
        weights = (met_ref[...].astype(F32) - stripe_met).astype(BF16)[:, : owners + per]

        def both(n):
            here = terms[pl.ds(n, owners, stride=size), :].astype(BF16)
            return jnp.concatenate([here, every[owner_ref[0] ^ n]], axis=0)

        for n in range(0, size, 2):
            made = jnp.dot(
                weights, jnp.concatenate([both(n), both(n + 1)], axis=1), preferred_element_type=F32
            ).astype(BF16)
            for u in range(2):
                for e in range(entries):
                    bins[(n + u) * blocks : (n + u + 1) * blocks, e * T : (e + 1) * T] = made[
                        e * blocks : (e + 1) * blocks, u * T : (u + 1) * T
                    ]
        fetch.wait()
        whole[...] = jnp.dot(bins[...], library_ref[...].reshape(entries * T, T), preferred_element_type=F32)
        for m, out_ref in enumerate(outs):
            start = lax.rem(q_ref[0] + m, quarters) * held
            for t in range(held):
                out_ref[t] = whole[pl.ds(start + t, size, stride=blocks), :].astype(out_ref.dtype)
        for n in range(size):
            stripes[n * per : (n + 1) * per, :] = every[owner_ref[0] ^ n].astype(F32)
        for b in range(per):
            stripe_ref[b] = stripes[pl.ds(b, size, stride=per), :]

    return pl.pallas_call(
        kernel,
        out_shape=[
            *(jax.ShapeDtypeStruct((held, size, T), BF16 if m else F32) for m in range(quarters)),
            jax.ShapeDtypeStruct((per, size, T), F32),
        ],
        in_specs=[SMEM, SMEM, VMEM, VMEM, VMEM, HBM] + [VMEM] * len(bundles),
        out_specs=[VMEM] * (quarters + 1),
        scratch_shapes=[
            pltpu.VMEM(library.shape, BF16),
            pltpu.VMEM((owners, per, T), BF16),
            pltpu.VMEM((owners * per, T), F32),
            pltpu.VMEM((owners * size, T), F32),
            pltpu.VMEM((size * blocks, entries * T), BF16),
            pltpu.VMEM((size * blocks, T), F32),
            pltpu.SemaphoreType.DMA,
        ],
        compiler_params=params(),
        cost_estimate=pl.CostEstimate(
            flops=2 * 256 * size * T * T, bytes_accessed=8 * 2**20, transcendentals=0
        ),
        name="adjoint_tiles",
    )(quarter, owner, met, by_row, returned, in_hbm(library), *bundles)


def residual_call(phase, stripe, forward):
    per = stripe.shape[0]

    def kernel(phase_ref, stripe_ref, forward_ref, residual_ref):
        for b in range(per):
            where = slice(b * T, (b + 1) * T)
            corrected = (phase_ref[:, where].astype(F32) - stripe_ref[b]).astype(BF16)
            residual_ref[:, where] = (corrected.astype(F32) - forward_ref[:, where]).astype(BF16)

    return pl.pallas_call(
        kernel,
        out_shape=jax.ShapeDtypeStruct(phase.shape, BF16),
        in_specs=[VMEM] * 3,
        out_specs=VMEM,
        compiler_params=params(),
        cost_estimate=pl.CostEstimate(flops=2**19, bytes_accessed=2**21, transcendentals=0),
        name="residual",
    )(phase, stripe, forward)


def image_call(quarter, image, own, others):
    slices = image.shape[0]
    mine = own.shape[0]

    def kernel(q_ref, image_ref, own_ref, *refs):
        others_refs, out_ref = refs[:-1], refs[-1]
        for i in range(mine):
            total = own_ref[i]
            for ref in others_refs:
                total += ref[i].astype(F32)
            pixels = image_ref[:, lanes(q_ref[0] * mine + i)].astype(F32)
            out_ref[:, i * T : (i + 1) * T] = pixels + RELAX * total

    return pl.pallas_call(
        kernel,
        out_shape=jax.ShapeDtypeStruct((slices, mine * T), F32),
        in_specs=[SMEM, VMEM, VMEM] + [VMEM] * len(others),
        out_specs=VMEM,
        compiler_params=params(),
        cost_estimate=pl.CostEstimate(flops=2**18, bytes_accessed=2**20, transcendentals=0),
        name="image_step",
    )(quarter, image, own, *others)


def in_hbm(array):
    return pltpu.with_memory_space_constraint(array, pltpu.HBM)


def exchanged(array, axis):
    return lax.all_to_all(array, axis, split_axis=0, concat_axis=0, tiled=True)


def shards(projections, phase_kernel, image, tile_library, tile_entry, tile_image, tile_slot, tile_count, slot_block):
    projections = projections[0]
    library = tile_library[0, 0]
    image = image.T
    slices = projections.shape[0]
    quarters = lax.axis_size("ray")
    quarter = lax.axis_index("ray").astype(jnp.int32).reshape(1)
    tiles = (tile_entry[0], tile_image[0], tile_slot[0], tile_count)
    carried = slot_block[0]

    owners = lax.axis_size("dom")
    owner = lax.axis_index("dom").astype(jnp.int32).reshape(1)
    blocks = image.shape[1] // T

    def rims(head, tail):
        left = lax.ppermute(tail, "ray", [(i, i + 1) for i in range(quarters - 1)])
        right = lax.ppermute(head, "ray", [(i + 1, i) for i in range(quarters - 1)])
        return left, right

    def swapped(array, m):
        return lax.ppermute(array, "dom", [(i, i ^ m) for i in range(owners)])

    send, head, tail, row = first_call(*tiles, carried, projections, image, library)
    arrived = exchanged(send, "dom")
    rows = [row] + [swapped(row, m) for m in range(1, 8)]
    phase, band, stack = phase_call(projections, *rims(head, tail), phase_kernel, rows)
    forward, back, stack = back_call(carried, arrived, phase, stack)
    returned = exchanged(back, "dom")
    met, by_row = counts_call(*tiles, owner, stack, owners, library.shape[0], blocks)
    stripe = stripe_call(quarter, arrived, *rims(*rim_call(arrived, stack)), band, quarters)
    pair = joined_call([stripe, swapped(stripe, 1)])
    bundle = joined_call([pair] + [swapped(pair, m) for m in (2, 4, 6)], stack)
    twin = joined_call([bundle, swapped(bundle, 32)])
    bundles = [twin] + [swapped(twin, m) for m in (8, 16, 24)]
    own, *sent, stripe = adjoint_call(quarter, owner, met, by_row, returned, bundles, library, blocks, quarters)
    others = [
        lax.ppermute(part, "ray", [(i, (i + m) % quarters) for i in range(quarters)])
        for m, part in enumerate(sent, 1)
    ]
    residual = residual_call(phase, stripe, forward)
    image_next = image_call(quarter, image, own, others)
    return residual[None], image_next.T


def solution(mesh):
    return jax.shard_map(
        shards,
        mesh=mesh,
        in_specs=(
            P("dom", None, "ray"),
            P(),
            P("dom", None),
            P("dom", "ray", None, None, None),
            P("dom", "ray", None),
            P("dom", "ray", None),
            P("dom", "ray", None),
            P("dom", "ray"),
            P("dom", "ray", None),
        ),
        out_specs=(P("dom", None, "ray"), P(("dom", "ray"), None)),
        check_vma=False,
    )
```
